128 devices in a mesh: dp: 128 (over x, z, y, core).
Axes of the slice: x: 4, y: 4, z: 4, core: 2. Of those that a mesh axis runs over, the one named last changes fastest.
Arguments:
- text_input: bfloat16 [49152, 768], P('dp'), may hold values from -24 to 24
- caption_lengths: int32 [768, 4], P('dp'), may hold values from 4 to 16, as said below
- image_tokens: bfloat16 [153600, 768], P('dp'), may hold values from -6 to 6
- image_attn: bfloat16 [768, 3072], replicated, may hold values from -0.21875 to 0.21875
- image_mlp: bfloat16 [2, 768, 3072], replicated, may hold values from -0.21875 to 0.21875
- image_vectors: float32 [12, 768], replicated, may hold values from -1.5 to 2.5
- attn_master: float32 [768, 3072], P('dp'), may hold values from -0.21875 to 0.21875
- mlp_master: float32 [2, 768, 3072], P(None, 'dp'), may hold values from -0.21875 to 0.21875
- vector_master: float32 [12, 768], P(None, 'dp'), may hold values from -1.5 to 2.5
- attn_first: float32 [768, 3072], P('dp'), may hold values from -2.3841858e-06 to 2.3841858e-06
- mlp_first: float32 [2, 768, 3072], P(None, 'dp'), may hold values from -2.3841858e-06 to 2.3841858e-06
- vector_first: float32 [12, 768], P(None, 'dp'), may hold values from -9.536743e-06 to 9.536743e-06
- attn_second: float32 [768, 3072], P('dp'), may hold values from 1.4110136e-14 to 5.6440543e-14
- mlp_second: float32 [2, 768, 3072], P(None, 'dp'), may hold values from 1.4110136e-14 to 5.6440543e-14
- vector_second: float32 [12, 768], P(None, 'dp'), may hold values from 1.4110136e-13 to 5.6440546e-13
Outputs:
- input_grad: float32 [49152, 768], P('dp')
- grad_norm: float32 [], replicated
- attn_grad: float32 [768, 3072], P('dp')
- mlp_grad: float32 [2, 768, 3072], P(None, 'dp')
- vector_grad: float32 [12, 768], P(None, 'dp')
- attn_first_new: float32 [768, 3072], P('dp')
- mlp_first_new: float32 [2, 768, 3072], P(None, 'dp')
- vector_first_new: float32 [12, 768], P(None, 'dp')
- attn_second_new: float32 [768, 3072], P('dp')
- mlp_second_new: float32 [2, 768, 3072], P(None, 'dp')
- vector_second_new: float32 [12, 768], P(None, 'dp')
- attn_new: float32 [768, 3072], P('dp')
- mlp_new: float32 [2, 768, 3072], P(None, 'dp')
- vector_new: float32 [12, 768], P(None, 'dp')
The draws below stay inside these ranges and needn't reach their ends.
Inputs may be any that keep to these rules, and one draw needn't show every extreme that they name: `caption_lengths`: 4 caption lengths for each text row of 64 tokens; a row's positions past their sum are padding.
All inputs are finite; a program needn't handle non-finite values.
Results may differ from the reference program's by a relative error of at most 0.023.
Values may be sent and summed in bfloat16 or wider, within the bound.
A program may use at most 192 MiB of HBM per device.

```python
import math
import jax
import jax.numpy as jnp
from jax import lax

D = 768
FF = 3072
ROW_LEN = 64
SLOTS = 4
PATCHES = 50
STEP = 10
ROWS_DEV = 6
PAIRS_DEV = 24
PAIRS = 3072
ROWS = 768
TEXT_TOK = 49152
IMAGE_TOK = 153600
N_DP = 128


def vector_rows(key, gain_start, gain_end):
    gain_key, bias_key = jax.random.split(key)
    ramp = gain_start + (gain_end - gain_start) * jnp.arange(D, dtype=jnp.float32) / (D - 1)
    gains = ramp * jax.random.uniform(gain_key, (2, D), jnp.float32, 0.8, 1.25)
    biases = jax.random.truncated_normal(bias_key, -3.0, 3.0, (10, D), jnp.float32) * 0.05
    return jnp.concatenate([gains[0:1], biases[0:1], gains[1:2], biases[1:10]], 0)


def draw_vector_master(key, part):
    key = jax.random.fold_in(key, 11)
    return vector_rows(key, 0.6, 1.8)


def draw_image_vectors(key, part):
    key = jax.random.fold_in(key, 12)
    return vector_rows(key, 0.6, 1.8)


def draw_caption_lengths(key, part):
    key = jax.random.fold_in(key, 13)
    base_key, high_key, low_key = jax.random.split(key, 3)
    count = ROWS * SLOTS
    drawn_lengths = jax.random.randint(base_key, (count,), 4, 17)
    high_at = jax.random.randint(high_key, (), 0, count)
    low_at = (high_at + 1 + jax.random.randint(low_key, (), 0, count - 1)) % count
    place = jnp.arange(count, dtype=jnp.int32)
    lengths = jnp.where(place == high_at, 16, jnp.where(place == low_at, 4, drawn_lengths))
    return lengths.astype(jnp.int32).reshape(ROWS, SLOTS)


def spiked(result, key, source, target, shards_of, factor):
    owner, partner = [(jnp.arange(result.shape[axis_at]) // (result.shape[axis_at] // shards_of)).reshape([-1 if axis == axis_at else 1 for axis in range(result.ndim)]) for axis_at in (source, target)]
    chosen = jax.random.permutation(key, shards_of)[partner]
    strong = (owner == chosen) | (owner == (partner + shards_of // 2) % shards_of)
    return jnp.where(strong, factor * result, result)


def shard_levels(stream_key, shape, shards, low, top_value):
    factor_of = 1.0
    for dim, blocks in shards:
        steps = jax.random.uniform(jax.random.fold_in(jax.random.fold_in(stream_key, 6), dim), (blocks,), jnp.float32, low / len(shards), top_value / len(shards))
        factor_of = factor_of * jnp.repeat(jnp.exp(steps), shape[dim] // blocks).reshape((-1,) + (1,) * (len(shape) - 1 - dim))
    return factor_of


def scatter_about(own_key, dims, deviation, bound, shards=(), kind=jnp.bfloat16):
    loudness = shard_levels(own_key, dims, shards, -0.22, 0.18) if shards else 1.0
    entries = jax.random.normal(own_key, dims, jnp.float32) * deviation * loudness
    return jnp.minimum(jnp.maximum(entries, -bound), bound).astype(kind)


def gaussian_with(rng, extent, deviation, reach, pieces, heavy, kind=jnp.bfloat16):
    drawn = deviation * jax.random.normal(rng, extent, jnp.float32)
    if pieces:
        drawn = drawn * shard_levels(rng, extent, pieces, -0.22, 0.18)
    return jnp.clip(spiked(drawn, jax.random.fold_in(rng, 3), *heavy), -reach, reach).astype(kind)


def setup_inputs(seed: int = 0) -> dict:
    keys = jax.random.split(jax.random.key(seed), 16)
    text_input = gaussian_with(keys[0], (TEXT_TOK, D), 1.0, 24.0, ((0, 128),), (0, 1, 128, 5.5))
    caption_lengths = draw_caption_lengths(jax.random.fold_in(keys[15], 71), 0)
    image_tokens = scatter_about(keys[2], (IMAGE_TOK, D), 1.0, 6.0, ((0, 128),))
    image_attn = scatter_about(keys[3], (D, 4 * D), D ** -0.5, 0.21875)
    image_mlp = scatter_about(keys[4], (2, D, FF), D ** -0.5, 0.21875)
    image_vectors = draw_image_vectors(jax.random.fold_in(keys[15], 71), 0)
    attn_master = scatter_about(keys[6], (D, 4 * D), D ** -0.5, 0.21875, ((0, 128),), jnp.float32)
    mlp_master = scatter_about(keys[7], (2, D, FF), D ** -0.5, 0.21875, ((1, 128),), jnp.float32)
    vector_master = draw_vector_master(jax.random.fold_in(keys[15], 71), 0)
    attn_first = scatter_about(keys[9], (D, 4 * D), (0.111 * 0.01 * (4*D*D + 2*D*FF) ** -0.5), 2.384185791015625e-06, ((0, 128),), jnp.float32)
    mlp_first = scatter_about(keys[10], (2, D, FF), (0.111 * 0.01 * (4*D*D + 2*D*FF) ** -0.5), 2.384185791015625e-06, ((1, 128),), jnp.float32)
    vector_first = scatter_about(keys[11], (12, D), (0.444 * 0.01 * (4*D*D + 2*D*FF) ** -0.5), 9.5367431640625e-06, ((1, 128),), jnp.float32)
    attn_second = jnp.clip(jnp.exp(math.log(5.644054288603956e-14) - 1.3862944 * jax.random.uniform(keys[12], (D, 4 * D), jnp.float32) ** shard_levels(keys[12], (D, 4 * D), ((0, 128),), -0.2, 0.2)), 1.411013572150989e-14, 5.644054288603956e-14)
    mlp_second = jnp.clip(jnp.exp(math.log(5.644054288603956e-14) - 1.3862944 * jax.random.uniform(keys[13], (2, D, FF), jnp.float32) ** shard_levels(keys[13], (2, D, FF), ((1, 128),), -0.2, 0.2)), 1.411013572150989e-14, 5.644054288603956e-14)
    vector_second = jnp.clip(jnp.exp(math.log(5.644054559654499e-13) - 1.3862944 * jax.random.uniform(keys[14], (12, D), jnp.float32) ** shard_levels(keys[14], (12, D), ((1, 128),), -0.2, 0.2)), 1.4110136399136247e-13, 5.644054559654499e-13)
    return dict(text_input=text_input, caption_lengths=caption_lengths, image_tokens=image_tokens, image_attn=image_attn, image_mlp=image_mlp, image_vectors=image_vectors, attn_master=attn_master, mlp_master=mlp_master, vector_master=vector_master, attn_first=attn_first, mlp_first=mlp_first, vector_first=vector_first, attn_second=attn_second, mlp_second=mlp_second, vector_second=vector_second)


highest = lax.Precision.HIGHEST
logit_scale = 60.0
clip_norm = 0.01
learn_rate = 0.05
vector_rate = 0.3
beta_first = 0.9
beta_second = 0.999
adam_epsilon = 1e-08
weight_decay = 0.1

@jax.custom_vjp
def low(v):
    return lax.optimization_barrier(v.astype(jnp.bfloat16)).astype(jnp.float32)

@jax.custom_vjp
def low_back(v):
    return v

def low_keep(v):
    return (low(v), None)

def low_pass(kept, grad):
    return (grad,)

def back_keep(v):
    return (v, None)

def back_low(kept, grad):
    return (low(grad),)
low.defvjp(low_keep, low_pass)
low_back.defvjp(back_keep, back_low)

def product(left, right):
    return jnp.dot(left, right, precision=highest, preferred_element_type=jnp.float32)

def layer_norm(values, gain_row, bias_row):
    center = lax.optimization_barrier(jnp.mean(values, -1, keepdims=True))
    shifted = values - center
    spread = lax.optimization_barrier(jnp.mean(shifted * shifted, -1, keepdims=True))
    return shifted * lax.rsqrt(spread + 1e-06) * gain_row + bias_row

def unit_rows(values):
    return values * lax.rsqrt(lax.optimization_barrier(jnp.sum(values * values, -1, keepdims=True)) + 1e-06)

def log_sum_exp(values, axis_index):
    maximum = lax.optimization_barrier(jnp.max(values, axis_index, keepdims=True))
    return jnp.log(lax.optimization_barrier(jnp.sum(jnp.exp(values - maximum), axis_index))) + jnp.squeeze(maximum, axis_index)

def caption_slots(lengths, row_len):
    row_ends = jnp.cumsum(lengths, axis=1).astype(jnp.int32)
    position = jnp.arange(row_len, dtype=jnp.int32)
    return lax.optimization_barrier(jnp.sum((position[None, :, None] >= row_ends[:, None, :]).astype(jnp.int32), -1)).astype(jnp.int32)

def pool_matrix(lengths, slot_ids):
    row_count, slot_count = lengths.shape
    row_base = slot_count * jnp.arange(row_count, dtype=jnp.int32)[:, None]
    owner_pair = jnp.where(slot_ids < slot_count, slot_ids + row_base, -1).astype(jnp.int32).reshape(-1)
    target = jnp.arange(row_count * slot_count, dtype=jnp.int32)
    member = (owner_pair[:, None] == target[None, :]).astype(jnp.float32)
    return member / lengths.reshape(-1).astype(jnp.float32)[None, :]

def block(inputs, attn_weight, mlp_weight, vectors, allowed):
    sequences, length, features = inputs.shape
    head_count = features // 64
    tokens_flat = inputs.reshape(sequences * length, features)
    normed = low(layer_norm(tokens_flat, vectors[0], vectors[1]))
    biases = jnp.concatenate([vectors[4], jnp.zeros_like(vectors[4]), vectors[5]])
    triple = low_back(low(product(normed, attn_weight[:, :3 * features]) + biases))
    projected = triple.reshape(sequences, length, 3, head_count, 64)
    scores = low_back(jnp.einsum('nqhd,nkhd->nhqk', projected[:, :, 0], projected[:, :, 1], precision=highest))
    logits = jnp.where(allowed[:, None], scores * 0.125, -1e+30)
    maximum = lax.optimization_barrier(jnp.max(logits, -1, keepdims=True))
    weights = jnp.exp(logits - maximum)
    attn_probs = low(weights / lax.optimization_barrier(jnp.sum(weights, -1, keepdims=True)))
    attended = jnp.einsum('nhqk,nkhd->nqhd', attn_probs, projected[:, :, 2], precision=highest)
    attended = low_back(low(attended.reshape(sequences * length, features)))
    residual = tokens_flat + low_back(product(attended, attn_weight[:, 3 * features:]) + vectors[6])
    normed_two = low(layer_norm(residual, vectors[2], vectors[3]))
    hidden = low_back(product(normed_two, mlp_weight[0]) + vectors[8:].reshape(-1))
    active = low(jax.nn.gelu(hidden))
    branch = jnp.einsum('tf,df->td', active, mlp_weight[1], precision=highest) + vectors[7]
    output = residual + low_back(branch)
    return output.reshape(sequences, length, features)

def adam_update(weight, gradient, first_moment, second_moment, factor, rate, decay_rate):
    clipped = gradient * factor
    first_new = beta_first * first_moment + (1.0 - beta_first) * clipped
    second_new = beta_second * second_moment + (1.0 - beta_second) * clipped * clipped
    ratio = first_new / (1.0 - beta_first ** STEP) / (jnp.sqrt(second_new / (1.0 - beta_second ** STEP)) + adam_epsilon)
    return (first_new, second_new, weight - rate * (ratio + decay_rate * weight))

def reference(text_input, caption_lengths, image_tokens, image_attn, image_mlp, image_vectors, attn_master, mlp_master, vector_master, attn_first, mlp_first, vector_first, attn_second, mlp_second, vector_second):
    group_count = N_DP
    features = D
    image_attn_full = image_attn.astype(jnp.float32)
    image_mlp_full = image_mlp.astype(jnp.float32)
    image_blocks = image_tokens.astype(jnp.float32).reshape(group_count, PAIRS_DEV, PATCHES, features)
    full_mask = jnp.ones((PAIRS_DEV, PATCHES, PATCHES), jnp.bool_)

    def image_group(block_tokens):
        return lax.optimization_barrier(jnp.mean(block(block_tokens, image_attn_full, image_mlp_full, image_vectors, full_mask), 1))
    image_unit = low(unit_rows(lax.map(image_group, image_blocks).reshape(PAIRS, features)))
    length_blocks = caption_lengths.reshape(group_count, ROWS_DEV, SLOTS)

    def total_loss(attn_weight, mlp_weight, vector_weight, text_values):
        attn_low = low(attn_weight)
        mlp_low = low(mlp_weight)
        vector_low = low(vector_weight)

        def text_group(pair_block):
            block_tokens, lengths = pair_block
            slot_ids = caption_slots(lengths, ROW_LEN)
            allowed = slot_ids[:, :, None] == slot_ids[:, None, :]
            output = block(block_tokens, attn_low, mlp_low, vector_low, allowed).reshape(ROWS_DEV * ROW_LEN, features)
            return jnp.einsum('tj,td->jd', pool_matrix(lengths, slot_ids), output, precision=highest)
        text_blocks = text_values.reshape(group_count, ROWS_DEV, ROW_LEN, features)
        pooled = lax.map(jax.checkpoint(text_group), (text_blocks, length_blocks)).reshape(PAIRS, features)
        text_unit = low(unit_rows(pooled))
        similar = low_back(product(image_unit, text_unit.T))
        logits = logit_scale * similar
        row_totals = log_sum_exp(logits, 1)
        col_totals = log_sum_exp(logits, 0)
        diagonal = jnp.diagonal(logits)
        return (jnp.sum(row_totals - diagonal) + jnp.sum(col_totals - diagonal)) / (2.0 * PAIRS)
    loss_value, backward = jax.vjp(total_loss, attn_master, mlp_master, vector_master, text_input.astype(jnp.float32))
    attn_grad, mlp_grad, vector_grad, input_grad = backward(jnp.ones_like(loss_value))
    grad_norm = jnp.sqrt(jnp.sum(attn_grad * attn_grad) + jnp.sum(mlp_grad * mlp_grad) + jnp.sum(vector_grad * vector_grad))
    factor = jnp.minimum(1.0, clip_norm / (grad_norm + 1e-06))
    attn_state = adam_update(attn_master, attn_grad, attn_first, attn_second, factor, learn_rate, weight_decay)
    mlp_state = adam_update(mlp_master, mlp_grad, mlp_first, mlp_second, factor, learn_rate, weight_decay)
    vector_state = adam_update(vector_master, vector_grad, vector_first, vector_second, factor, vector_rate, 0.0)
    return (input_grad, grad_norm, attn_grad, mlp_grad, vector_grad, attn_state[0], mlp_state[0], vector_state[0], attn_state[1], mlp_state[1], vector_state[1], attn_state[2], mlp_state[2], vector_state[2])
```

```python
import jax
import jax.numpy as jnp
from jax import lax
from jax.experimental import pallas as pl
from jax.experimental.pallas import tpu as pltpu
from jax.sharding import PartitionSpec as P

STEP = 10


logit_scale = 60.0
clip_norm = 0.01
learn_rate = 0.05
vector_rate = 0.3
beta_first = 0.9
beta_second = 0.999
adam_epsilon = 1e-08
weight_decay = 0.1
bfloat = jnp.bfloat16
single = jnp.float32


def layer_norm(values, gain_row, bias_row):
    center = jnp.mean(values, -1, keepdims=True)
    shifted = values - center
    spread = jnp.mean(shifted * shifted, -1, keepdims=True)
    return shifted * lax.rsqrt(spread + 1e-06) * gain_row + bias_row


def unit_rows(values):
    return values * lax.rsqrt(jnp.sum(values * values, -1, keepdims=True) + 1e-06)


def log_sum_exp(values, axis_index):
    maximum = jnp.max(values, axis_index, keepdims=True)
    return jnp.log(jnp.sum(jnp.exp(values - maximum), axis_index)) + jnp.squeeze(
        maximum, axis_index
    )


def caption_slots(lengths, row_len):
    row_ends = jnp.cumsum(lengths, axis=1)
    position = jnp.arange(row_len, dtype=jnp.int32)
    return jnp.sum((position[None, :, None] >= row_ends[:, None, :]).astype(jnp.int32), -1)


def pool_matrix(lengths, slot_ids):
    row_count, slot_count = lengths.shape
    row_base = slot_count * jnp.arange(row_count, dtype=jnp.int32)[:, None]
    owner_pair = jnp.where(slot_ids < slot_count, slot_ids + row_base, -1).reshape(-1)
    target = jnp.arange(row_count * slot_count, dtype=jnp.int32)
    member = (owner_pair[:, None] == target[None, :]).astype(single)
    return member / lengths.reshape(-1).astype(single)[None, :]


def attention_logits(queries, key_rows, allowed):
    scores = jnp.einsum("nqhd,nkhd->nhqk", queries, key_rows, preferred_element_type=single)
    return jnp.where(allowed[:, None], scores * 0.125, -1e30)


def block_forward(inputs, attn_weight, mlp_weight, vectors, allowed):
    sequences, length, features = inputs.shape
    head_count = features // 64
    tokens_flat = inputs.reshape(sequences * length, features)
    normed = layer_norm(tokens_flat, vectors[0], vectors[1]).astype(bfloat)
    biases = jnp.concatenate([vectors[4], jnp.zeros_like(vectors[4]), vectors[5]])
    triple = jnp.dot(normed, attn_weight[:, : 3 * features], preferred_element_type=single) + biases
    projected = triple.astype(bfloat).reshape(sequences, length, 3, head_count, 64)
    logits = attention_logits(projected[:, :, 0], projected[:, :, 1], allowed)
    maximum = jnp.max(logits, -1, keepdims=True)
    weights = jnp.exp(logits - maximum)
    totals = jnp.sum(weights, -1, keepdims=True)
    attn_probs = (weights / totals).astype(bfloat)
    log_totals = maximum + jnp.log(totals)
    attended = jnp.einsum(
        "nhqk,nkhd->nqhd", attn_probs, projected[:, :, 2], preferred_element_type=single
    )
    attended = attended.reshape(sequences * length, features).astype(bfloat)
    residual = (
        tokens_flat
        + jnp.dot(attended, attn_weight[:, 3 * features :], preferred_element_type=single)
        + vectors[6]
    )
    normed_two = layer_norm(residual, vectors[2], vectors[3]).astype(bfloat)
    hidden = jnp.dot(normed_two, mlp_weight[0], preferred_element_type=single) + vectors[
        8:
    ].reshape(-1)
    active = jax.nn.gelu(hidden).astype(bfloat)
    output = (
        residual
        + jnp.einsum("tf,df->td", active, mlp_weight[1], preferred_element_type=single)
        + vectors[7]
    )
    saved_state = (
        tokens_flat,
        normed,
        projected,
        log_totals,
        attended,
        residual,
        normed_two,
        hidden,
        active,
    )
    return (output, saved_state)


def block_backward(upstream, saved_state, attn_weight, mlp_weight, vectors, allowed):
    tokens_flat, normed, projected, log_totals, attended, residual, normed_two, hidden, active = (
        saved_state
    )
    features = tokens_flat.shape[1]
    sequences, seq_len, head_count = (projected.shape[0], projected.shape[1], projected.shape[3])
    branch_two = upstream.astype(bfloat)
    down_grad = jnp.einsum("td,tf->df", branch_two, active, preferred_element_type=single)
    down_bias = jnp.sum(branch_two.astype(single), 0)
    active_grad = jnp.dot(branch_two, mlp_weight[1], preferred_element_type=single)
    unused, gelu_back = jax.vjp(jax.nn.gelu, hidden)
    hidden_grad = gelu_back(active_grad)[0].astype(bfloat)
    up_grad = jnp.einsum("td,tf->df", normed_two, hidden_grad, preferred_element_type=single)
    up_bias = jnp.sum(hidden_grad.astype(single), 0)
    normed_grad = jnp.einsum("tf,df->td", hidden_grad, mlp_weight[0], preferred_element_type=single)
    unused, second_back = jax.vjp(layer_norm, residual, vectors[2], vectors[3])
    resid_part, gain_two, shift_two = second_back(normed_grad)
    resid_grad = upstream + resid_part
    branch_one = resid_grad.astype(bfloat)
    out_grad = jnp.einsum("td,te->de", attended, branch_one, preferred_element_type=single)
    out_bias = jnp.sum(branch_one.astype(single), 0)
    attended_grad = jnp.einsum(
        "te,de->td", branch_one, attn_weight[:, 3 * features :], preferred_element_type=single
    )
    attended_grad = attended_grad.astype(bfloat).reshape(sequences, seq_len, head_count, 64)
    queries, key_rows, value_rows = (projected[:, :, 0], projected[:, :, 1], projected[:, :, 2])
    attn_probs = jnp.exp(attention_logits(queries, key_rows, allowed) - log_totals)
    value_grad = jnp.einsum(
        "nhqk,nqhd->nkhd", attn_probs.astype(bfloat), attended_grad, preferred_element_type=single
    )
    prob_grad = jnp.einsum(
        "nqhd,nkhd->nhqk", attended_grad, value_rows, preferred_element_type=single
    )
    score_grad = (
        attn_probs * (prob_grad - jnp.sum(attn_probs * prob_grad, -1, keepdims=True)) * 0.125
    )
    score_grad = score_grad.astype(bfloat)
    query_grad = jnp.einsum("nhqk,nkhd->nqhd", score_grad, key_rows, preferred_element_type=single)
    key_grad = jnp.einsum("nhqk,nqhd->nkhd", score_grad, queries, preferred_element_type=single)
    triple_grad = (
        jnp.stack([query_grad, key_grad, value_grad], 2).astype(bfloat).reshape(-1, 3 * features)
    )
    qkv_grad = jnp.einsum("td,te->de", normed, triple_grad, preferred_element_type=single)
    triple_bias = jnp.sum(triple_grad.astype(single), 0)
    first_grad = jnp.einsum(
        "te,de->td", triple_grad, attn_weight[:, : 3 * features], preferred_element_type=single
    )
    unused, first_back = jax.vjp(layer_norm, tokens_flat, vectors[0], vectors[1])
    input_part, gain_one, shift_one = first_back(first_grad)
    input_grad = resid_grad + input_part
    attn_grad = jnp.concatenate([qkv_grad, out_grad], 1)
    mlp_grad = jnp.stack([up_grad, down_grad])
    vector_rows = jnp.stack(
        [
            gain_one,
            shift_one,
            gain_two,
            shift_two,
            triple_bias[:features],
            triple_bias[2 * features :],
            out_bias,
            down_bias,
        ]
    )
    vector_grad = jnp.concatenate([vector_rows, up_bias.reshape(4, features)], 0)
    return (input_grad, attn_grad, mlp_grad, vector_grad)


def sum_squares(arrays):
    return sum((jnp.sum(member * member) for member in arrays))


def adam_update(weight, gradient, first_moment, second_moment, factor, rate, decay_rate):
    clipped = gradient * factor
    first_new = beta_first * first_moment + (1.0 - beta_first) * clipped
    second_new = beta_second * second_moment + (1.0 - beta_second) * clipped * clipped
    ratio = (
        first_new
        / (1.0 - beta_first**STEP)
        / (jnp.sqrt(second_new / (1.0 - beta_second**STEP)) + adam_epsilon)
    )
    return (first_new, second_new, weight - rate * (ratio + decay_rate * weight))


MESH = pl.DeviceIdType.MESH
LINES = 144
SHARD = 448


def place():
    me = lax.axis_index("dp")
    return (me // 32, lax.rem(me // 8, 4), lax.rem(me // 2, 4), lax.rem(me, 2))


def device(x, z, y, c):
    return ((x * 4 + z) * 4 + y) * 2 + c


def plus(index, step):
    return lax.rem(index + step, 4)


class Wire:
    def __init__(self, send_sems, recv_sems):
        self.send_sems, self.recv_sems, self.copies = (send_sems, recv_sems, [])

    def send(self, source, target, to):
        slot = len(self.copies)
        copy = pltpu.make_async_remote_copy(
            src_ref=source,
            dst_ref=target,
            send_sem=self.send_sems.at[slot],
            recv_sem=self.recv_sems.at[slot],
            device_id=(to,),
            device_id_type=MESH,
        )
        copy.start()
        self.copies.append(copy)
        return copy

    def drain(self):
        for copy in self.copies:
            copy.wait_send()


def greet(peers):
    barrier = pltpu.get_barrier_semaphore()
    for peer in peers:
        pl.semaphore_signal(barrier, inc=1, device_id=(peer,), device_id_type=MESH)
    pl.semaphore_wait(barrier, len(peers))


class Ring:
    def __init__(self, wire, peer, view):
        self.wire, self.peer, self.view = (wire, peer, view)
        self.ahead = wire.send(view(0, None), view(0, None), peer(1))
        self.behind = wire.send(view(0, None), view(0, None), peer(3))

    def forward(self):
        self.ahead.wait_recv()
        self.low = self.wire.send(self.view(3, 0), self.view(3, 0), self.peer(1))
        self.behind.wait_recv()
        self.high = self.wire.send(self.view(1, 1), self.view(1, 1), self.peer(3))

    def finish(self):
        self.low.wait_recv()
        self.high.wait_recv()


def aligned(start, size):
    return pl.ds(pl.multiple_of(start, 128), size)


def halves(start, size, part):
    if part is None:
        return aligned(start, size)
    low = size // 256 * 128
    return aligned(start, low) if part == 0 else aligned(start + low, size - low)


def gather_kernel(
    attn_ref, mlp_ref, vector_ref, weight, turned, line, lines, natural, small, send_sems, recv_sems
):
    x, z, y, c = place()
    peers_x = lambda k: device(plus(x, k), z, y, c)
    peers_z = lambda k: device(x, plus(z, k), y, c)
    peers_y = lambda k: device(x, z, plus(y, k), c)
    sibling = device(x, z, y, 1 - c)
    wire = Wire(send_sems, recv_sems)
    lines[c, y, 0:16] = vector_ref[...]
    for m in range(3):
        for j in range(24):
            columns = slice(j * 128, (j + 1) * 128)
            rows = attn_ref[:, columns] if m == 0 else mlp_ref[m - 1, :, columns]
            line[m, pl.ds(j, 6, stride=24), :] = rows
        lines[c, y, 16 + m * LINES : 16 + (m + 1) * LINES] = line[m].astype(bfloat)
    greet([p(k) for p in (peers_x, peers_z, peers_y) for k in (1, 2, 3)] + [sibling])
    spans = [pl.ds(0, 160), pl.ds(160, 144), pl.ds(304, 144)]
    first = [
        [wire.send(lines.at[c, y, span], lines.at[c, y, span], peers_y(k)) for k in (1, 3, 2)]
        for span in spans
    ]
    swaps = []
    for m in range(3):
        for copy in first[m]:
            copy.wait_recv()
        swaps.append(wire.send(lines.at[c, :, spans[m]], lines.at[c, :, spans[m]], sibling))

    def spread(m):
        swaps[m].wait_recv()
        for s in range(8):
            natural[s * LINES : (s + 1) * LINES] = lines[
                s % 2, s // 2, 16 + m * LINES : 16 + (m + 1) * LINES
            ].astype(single)

    half = c * 1536
    quarter = (c * 4 + y) * 384
    spread(0)
    for j in range(12):
        weight[0, x, z, :, aligned((c * 12 + j) * 128, 128)] = natural[
            pl.ds(c * 12 + j, 48, stride=24), :
        ].astype(bfloat)
    for s in range(8):
        small[s * 6 : (s + 1) * 6] = lines[s % 2, s // 2, 0:16].astype(single)[0:6]
    turned[x, z] = small[...].astype(bfloat)
    attn_x = Ring(wire, peers_x, lambda k, part: weight.at[0, plus(x, k), z, :, halves(half, 1536, part)])
    turn_x = [wire.send(turned.at[x, z], turned.at[x, z], peers_x(k)) for k in (1, 3, 2)]
    spread(1)
    for j in range(12):
        weight[1, x, z, :, aligned((c * 12 + j) * 128, 128)] = natural[
            pl.ds(c * 12 + j, 48, stride=24), :
        ].astype(bfloat)
    up_z = Ring(wire, peers_z, lambda k, part: weight.at[1, x, plus(z, k), :, halves(half, 1536, part)])
    spread(2)
    for j in range(3):
        place_j = (c * 4 + y) * 3 + j
        weight[2, x, z, :, aligned(place_j * 128, 128)] = natural[
            pl.ds(place_j, 48, stride=24), :
        ].astype(bfloat)
    down_x = Ring(wire, peers_x, lambda k, part: weight.at[2, plus(x, k), z, :, halves(quarter, 384, part)])
    attn_x.forward()
    up_z.forward()
    attn_x.finish()
    for copy in turn_x:
        copy.wait_recv()
    attn_z = Ring(wire, peers_z, lambda k, part: weight.at[0, :, plus(z, k), :, halves(half, 1536, part)])
    turn_z = [wire.send(turned.at[:, z], turned.at[:, z], peers_z(k)) for k in (1, 3, 2)]
    up_z.finish()
    up_x = Ring(wire, peers_x, lambda k, part: weight.at[1, plus(x, k), :, :, halves(half, 1536, part)])
    down_x.forward()
    down_x.finish()
    down_z = Ring(wire, peers_z, lambda k, part: weight.at[2, :, plus(z, k), :, halves(quarter, 384, part)])
    across = []

    def cross(view):
        across.append(wire.send(view, view, sibling))

    cross(attn_z.view(0, None))
    cross(up_x.view(0, None))
    attn_z.forward()
    cross(attn_z.view(3, None))
    cross(attn_z.view(1, None))
    up_x.forward()
    cross(up_x.view(3, None))
    cross(up_x.view(1, None))
    down_z.forward()
    down_z.finish()
    down_y = Ring(
        wire, peers_y, lambda k, part: weight.at[2, :, :, :, halves((c * 4 + plus(y, k)) * 384, 384, part)]
    )
    cross(down_y.view(0, None))
    attn_z.finish()
    cross(attn_z.view(2, None))
    up_x.finish()
    cross(up_x.view(2, None))
    down_y.forward()
    cross(down_y.view(3, None))
    cross(down_y.view(1, None))
    down_y.finish()
    cross(down_y.view(2, None))
    for copy in turn_z + across:
        copy.wait_recv()
    wire.drain()


def gather_weights(attn_master, mlp_master, vector_master):
    vector_lines = jnp.pad(vector_master.T, ((0, 10), (0, 116))).astype(bfloat)
    copies = 64
    weight, turned = pl.pallas_call(
        gather_kernel,
        out_shape=(
            jax.ShapeDtypeStruct((3, 4, 4, 48, 3072), bfloat),
            jax.ShapeDtypeStruct((4, 4, 48, 128), bfloat),
        ),
        in_specs=[pl.BlockSpec(memory_space=pltpu.VMEM)] * 3,
        out_specs=[pl.BlockSpec(memory_space=pltpu.VMEM)] * 2,
        scratch_shapes=[
            pltpu.VMEM((3, LINES, 128), single),
            pltpu.VMEM((2, 4, SHARD, 128), bfloat),
            pltpu.VMEM((8 * LINES, 128), single),
            pltpu.VMEM((48, 128), single),
            pltpu.SemaphoreType.DMA((copies,)),
            pltpu.SemaphoreType.DMA((copies,)),
        ],
        compiler_params=pltpu.CompilerParams(
            collective_id=1, has_side_effects=True, vmem_limit_bytes=56 * 2**20
        ),
        name="gather_weights",
    )(attn_master, mlp_master, vector_lines)
    weight = weight.reshape(3, 768, 3072)
    return weight[0], weight[1:], turned.reshape(768, 128)[:, :12].T


def loss_kernel(
    image_ref, pooled_ref, grad_ref, images, own, part, near, far, send_sems, recv_sems
):
    x, z, y, c = place()
    peers_x = lambda k: device(plus(x, k), z, y, c)
    peers_z = lambda k: device(x, plus(z, k), y, c)
    peers_y = lambda k: device(x, z, plus(y, k), c)
    sibling = device(x, z, y, 1 - c)
    wire = Wire(send_sems, recv_sems)
    group = [(k, d) for k in range(4) for d in range(2) if (k, d) != (0, 0)]
    plane = [(i, j) for i in range(4) for j in range(4) if (i, j) != (0, 0)]
    group_peer = lambda k, d: device(x, z, plus(y, k), lax.rem(c + d, 2))
    plane_peer = lambda i, j: device(plus(x, i), plus(z, j), y, c)
    own[c] = image_ref[...]
    greet([group_peer(*g) for g in group] + [plane_peer(*p) for p in plane])
    swap = wire.send(own.at[c], own.at[c], sibling)
    swap.wait_recv()
    lanes = aligned(c * 384, 384)
    images[x, z, y, :, lanes] = own[:, :, lanes].reshape(48, 384).astype(bfloat)
    lane = [aligned((c * 3 + o) * 128, 128) for o in range(3)]

    def view_of(o, axes):
        def view(k, part):
            index = []
            for name, here in (("x", x), ("z", z), ("y", y)):
                if name in axes[:-1]:
                    index.append(slice(None))
                elif name == axes[-1]:
                    index.append(plus(here, k))
                else:
                    index.append(here)
            rows = slice(None) if part is None else (pl.ds(0, 16) if part == 0 else pl.ds(16, 32))
            return images.at[(*index, rows, lane[o])]

        return view

    orders = ("yzx", "zxy", "xyz")
    peers = {"x": peers_x, "z": peers_z, "y": peers_y}
    for step in range(3):
        rings = [
            Ring(wire, peers[orders[o][step]], view_of(o, orders[o][: step + 1])) for o in range(3)
        ]
        for ring in rings:
            ring.forward()
        for ring in rings:
            ring.finish()
    mine = images.at[:, :, :, :, aligned(c * 384, 384)]
    cross = wire.send(mine, mine, sibling)
    pooled = pooled_ref[...]
    scale = lax.rsqrt(jnp.sum(pooled * pooled, -1, keepdims=True) + 1e-06)
    unit = pooled * scale
    cross.wait_recv()
    every = images[...].reshape(3072, 768)
    logits = logit_scale * lax.dot_general(
        unit.astype(bfloat), every, (((1,), (1,)), ((), ())), preferred_element_type=single
    )
    powers = jnp.exp(logits)
    column = jnp.sum(powers, 1, keepdims=True)
    rows = jnp.sum(powers, 0, keepdims=True)
    for k in range(8):
        part[k : k + 1, :] = rows[:, k * 384 : (k + 1) * 384]
    near[y, c] = part[...]
    sent = [wire.send(part, near.at[y, c], group_peer(*g)) for g in group]
    for copy in sent:
        copy.wait_recv()
    total = sum(near[k, d] for k in range(4) for d in range(2))
    far[x, z] = total
    sent = [wire.send(far.at[x, z], far.at[x, z], plane_peer(*p)) for p in plane]
    for copy in sent:
        copy.wait_recv()
    total = sum(far[i, j] for i in range(4) for j in range(4))
    every_row = jnp.concatenate([total[k : k + 1] for k in range(8)], 1)
    caption = lax.broadcasted_iota(jnp.int32, (24, 3072), 0) + lax.axis_index("dp") * 24
    image = lax.broadcasted_iota(jnp.int32, (24, 3072), 1)
    same = (caption == image).astype(single)
    logit_grad = (
        logit_scale * (powers / every_row + powers / column - 2.0 * same) / (2.0 * 3072)
    ).astype(bfloat)
    unit_grad = jnp.dot(logit_grad, every, preferred_element_type=single)
    grad_ref[...] = scale * (
        unit_grad - unit * jnp.sum(unit * unit_grad, -1, keepdims=True)
    )
    wire.drain()


def pair_gradient(image_unit, text_pooled):
    copies = 72
    return pl.pallas_call(
        loss_kernel,
        out_shape=jax.ShapeDtypeStruct((24, 768), single),
        in_specs=[pl.BlockSpec(memory_space=pltpu.VMEM)] * 2,
        out_specs=pl.BlockSpec(memory_space=pltpu.VMEM),
        scratch_shapes=[
            pltpu.VMEM((4, 4, 4, 48, 768), bfloat),
            pltpu.VMEM((2, 24, 768), single),
            pltpu.VMEM((8, 384), single),
            pltpu.VMEM((4, 2, 8, 384), single),
            pltpu.VMEM((4, 4, 8, 384), single),
            pltpu.SemaphoreType.DMA((copies,)),
            pltpu.SemaphoreType.DMA((copies,)),
        ],
        compiler_params=pltpu.CompilerParams(
            collective_id=2, has_side_effects=True, vmem_limit_bytes=56 * 2**20
        ),
        name="pair_gradient",
    )(image_unit, text_pooled)


def scatter_kernel(
    attn_ref,
    mlp_ref,
    vector_ref,
    attn_out,
    mlp_out,
    vector_out,
    square_out,
    held,
    from_z,
    from_x,
    from_y,
    total_z,
    total_x,
    total_y,
    late_x,
    late_z,
    down_x,
    down_z,
    whole,
    last,
    flat,
    third,
    packed,
    pieces,
    landed,
    sums,
    vec_c,
    vec_z,
    vec_x,
    vec_y,
    square,
    near,
    far,
    send_sems,
    recv_sems,
):
    x, z, y, c = place()
    peers_x = lambda k: device(plus(x, k), z, y, c)
    peers_z = lambda k: device(x, plus(z, k), y, c)
    peers_y = lambda k: device(x, z, plus(y, k), c)
    sibling = device(x, z, y, 1 - c)
    group = [(k, d) for k in range(4) for d in range(2) if (k, d) != (0, 0)]
    plane = [(i, j) for i in range(4) for j in range(4) if (i, j) != (0, 0)]
    group_peer = lambda k, d: device(x, z, plus(y, k), lax.rem(c + d, 2))
    plane_peer = lambda i, j: device(plus(x, i), plus(z, j), y, c)
    wire = Wire(send_sems, recv_sems)
    greet([group_peer(*g) for g in group] + [plane_peer(*p) for p in plane])
    grads = [attn_ref, mlp_ref.at[0], mlp_ref.at[1]]
    mine, other = (aligned(c * 1536, 1536), aligned((1 - c) * 1536, 1536))
    vec_c[c] = vector_ref[...]
    swap = [wire.send(grads[m].at[:, :, :, other], held.at[m], sibling) for m in range(3)]
    vec_swap = wire.send(vec_c.at[c], vec_c.at[c], sibling)

    def join(m):
        swap[m].wait_recv()

        @pl.loop(0, 16)
        def _(k):
            i, j = (k // 4, lax.rem(k, 4))
            held[m, i, j] = held[m, i, j] + grads[m][i, j, :, mine]

    turns = (1, 3, 2)
    join(0)
    send_z = [wire.send(held.at[0, :, plus(z, k)], from_z.at[k - 1], peers_z(k)) for k in turns]
    vec_swap.wait_recv()
    vec_z[z] = vec_c[0] + vec_c[1]
    sent_vec_z = [wire.send(vec_z.at[z], vec_z.at[z], peers_z(k)) for k in turns]
    join(1)
    send_x = [wire.send(held.at[1, plus(x, k)], from_x.at[k - 1], peers_x(k)) for k in turns]
    join(2)
    send_y = [
        wire.send(held.at[2, :, :, :, aligned(plus(y, k) * 384, 384)], from_y.at[k - 1], peers_y(k))
        for k in turns
    ]

    def await_all(copies):
        for copy in copies:
            copy.wait_recv()

    await_all(sent_vec_z)
    vec_x[x] = vec_z[0] + vec_z[1] + vec_z[2] + vec_z[3]
    sent_vec_x = [wire.send(vec_x.at[x], vec_x.at[x], peers_x(k)) for k in turns]
    await_all(send_z)

    def add(base, parts):
        return base.astype(single) + sum(part.astype(single) for part in parts)

    for i in range(4):
        total_z[i] = add(held[0, i, z], [from_z[k, i] for k in range(3)]).astype(bfloat)
    late_send_x = [wire.send(total_z.at[plus(x, k)], late_x.at[k - 1], peers_x(k)) for k in turns]
    await_all(send_x)
    for i in range(4):
        total_x[i] = add(held[1, x, i], [from_x[k, i] for k in range(3)]).astype(bfloat)
    late_send_z = [wire.send(total_x.at[plus(z, k)], late_z.at[k - 1], peers_z(k)) for k in turns]
    await_all(send_y)
    quarter = aligned(y * 384, 384)
    for i in range(4):
        for j in range(4):
            total_y[i, j] = add(
                held[2, i, j, :, quarter], [from_y[k, i, j] for k in range(3)]
            ).astype(bfloat)
    down_send_x = [wire.send(total_y.at[plus(x, k)], down_x.at[k - 1], peers_x(k)) for k in turns]
    await_all(sent_vec_x)
    vec_y[y] = vec_x[0] + vec_x[1] + vec_x[2] + vec_x[3]
    sent_vec_y = [wire.send(vec_y.at[y], vec_y.at[y], peers_y(k)) for k in turns]
    await_all(late_send_x)
    whole[0] = add(total_z[x], [late_x[k] for k in range(3)])
    await_all(late_send_z)
    whole[1] = add(total_x[z], [late_z[k] for k in range(3)])
    await_all(down_send_x)
    for j in range(4):
        last[j] = add(total_y[x, j], [down_x[k, j] for k in range(3)]).astype(bfloat)
    down_send_z = [wire.send(last.at[plus(z, k)], down_z.at[k - 1], peers_z(k)) for k in turns]
    for m in range(2):
        for j in range(12):
            flat[m, pl.ds(j, 48, stride=12), :] = whole[m, :, j * 128 : (j + 1) * 128]
    await_all(down_send_z)
    ended = add(last[z], [down_z[k] for k in range(3)])
    for j in range(3):
        third[pl.ds(j, 48, stride=3), :] = ended[:, j * 128 : (j + 1) * 128]
    packed[160:176] = jnp.zeros((16, 128), single)
    for s in range(8):
        packed[0:72] = flat[0, s * 72 : (s + 1) * 72]
        packed[72:144] = flat[1, s * 72 : (s + 1) * 72]
        packed[144:162] = third[s * 18 : (s + 1) * 18]
        pieces[s // 2, s % 2] = packed[...].astype(bfloat)
    landed[y, c] = pieces[y, c]
    piece_sent = [
        wire.send(pieces.at[plus(y, k), lax.rem(c + d, 2)], landed.at[y, c], group_peer(k, d))
        for k, d in group
    ]
    await_all(sent_vec_y)
    vec_total = vec_y[0] + vec_y[1] + vec_y[2] + vec_y[3]
    vector_out[...] = vec_total
    await_all(piece_sent)
    for h in range(2):
        for k in range(4):
            rows = landed[k, h].astype(single)
            packed[...] = rows if k == 0 else packed[...] + rows
            sums[...] = rows[144:168]
            for j in range(3):
                at = ((h * 4 + k) * 3 + j) * 128
                mlp_out[1, :, at : at + 128] = sums[pl.ds(j, 6, stride=3), :]
        for j in range(12):
            at = (h * 12 + j) * 128
            attn_out[:, at : at + 128] = packed[pl.ds(j, 6, stride=12), :]
            mlp_out[0, :, at : at + 128] = packed[pl.ds(72 + j, 6, stride=12), :]
    lanes = lax.broadcasted_iota(jnp.int32, (16, 768), 1)
    start = lax.axis_index("dp") * 6
    owned = jnp.where((lanes >= start) & (lanes < start + 6), vec_total, 0.0)
    squares = sum_squares((attn_out[...], mlp_out[0], mlp_out[1], owned))
    square[...] = jnp.broadcast_to(squares, (8, 128))
    near[y, c] = square[...]
    sent = [wire.send(square, near.at[y, c], group_peer(*g)) for g in group]
    await_all(sent)
    far[x, z] = sum(near[k, d] for k in range(4) for d in range(2))
    sent = [wire.send(far.at[x, z], far.at[x, z], plane_peer(*p)) for p in plane]
    await_all(sent)
    square_out[...] = sum(far[i, j] for i in range(4) for j in range(4))
    wire.drain()


def scatter_gradients(attn_grad, mlp_grad, vector_grad):
    copies = 72
    attn = attn_grad.astype(bfloat).reshape(4, 4, 48, 3072)
    mlp = mlp_grad.astype(bfloat).reshape(2, 4, 4, 48, 3072)
    vector = jnp.pad(vector_grad, ((0, 4), (0, 0)))
    vmem = pl.BlockSpec(memory_space=pltpu.VMEM)
    return pl.pallas_call(
        scatter_kernel,
        out_shape=(
            jax.ShapeDtypeStruct((6, 3072), single),
            jax.ShapeDtypeStruct((2, 6, 3072), single),
            jax.ShapeDtypeStruct((16, 768), single),
            jax.ShapeDtypeStruct((8, 128), single),
        ),
        in_specs=[vmem] * 3,
        out_specs=[vmem] * 4,
        scratch_shapes=[
            pltpu.VMEM((3, 4, 4, 48, 1536), bfloat),
            pltpu.VMEM((3, 4, 48, 1536), bfloat),
            pltpu.VMEM((3, 4, 48, 1536), bfloat),
            pltpu.VMEM((3, 4, 4, 48, 384), bfloat),
            pltpu.VMEM((4, 48, 1536), bfloat),
            pltpu.VMEM((4, 48, 1536), bfloat),
            pltpu.VMEM((4, 4, 48, 384), bfloat),
            pltpu.VMEM((3, 48, 1536), bfloat),
            pltpu.VMEM((3, 48, 1536), bfloat),
            pltpu.VMEM((3, 4, 48, 384), bfloat),
            pltpu.VMEM((3, 48, 384), bfloat),
            pltpu.VMEM((2, 48, 1536), single),
            pltpu.VMEM((4, 48, 384), bfloat),
            pltpu.VMEM((2, 576, 128), single),
            pltpu.VMEM((144, 128), single),
            pltpu.VMEM((176, 128), single),
            pltpu.VMEM((4, 2, 176, 128), bfloat),
            pltpu.VMEM((4, 2, 176, 128), bfloat),
            pltpu.VMEM((24, 128), single),
            pltpu.VMEM((2, 16, 768), single),
            pltpu.VMEM((4, 16, 768), single),
            pltpu.VMEM((4, 16, 768), single),
            pltpu.VMEM((4, 16, 768), single),
            pltpu.VMEM((8, 128), single),
            pltpu.VMEM((4, 2, 8, 128), single),
            pltpu.VMEM((4, 4, 8, 128), single),
            pltpu.SemaphoreType.DMA((copies,)),
            pltpu.SemaphoreType.DMA((copies,)),
        ],
        compiler_params=pltpu.CompilerParams(
            collective_id=3, has_side_effects=True, vmem_limit_bytes=56 * 2**20
        ),
        name="scatter_gradients",
    )(attn, mlp, vector)


def shards(
    text_input,
    caption_lengths,
    image_tokens,
    image_attn,
    image_mlp,
    image_vectors,
    attn_master,
    mlp_master,
    vector_master,
    attn_first,
    mlp_first,
    vector_first,
    attn_second,
    mlp_second,
    vector_second,
):
    attn_weight, mlp_weight, vector_low = gather_weights(attn_master, mlp_master, vector_master)
    vectors = vector_low.astype(single)
    features = text_input.shape[1]
    row_count, slot_count = caption_lengths.shape
    row_len = text_input.shape[0] // row_count
    pair_count = row_count * slot_count
    patches = image_tokens.shape[0] // pair_count
    full_mask = jnp.ones((pair_count, patches, patches), jnp.bool_)
    image_inputs = image_tokens.astype(single).reshape(pair_count, patches, features)
    image_out, unused = block_forward(image_inputs, image_attn, image_mlp, image_vectors, full_mask)
    image_unit = unit_rows(jnp.mean(image_out.reshape(pair_count, patches, features), 1))
    slot_ids = caption_slots(caption_lengths, row_len)
    allowed = slot_ids[:, :, None] == slot_ids[:, None, :]
    text_inputs = text_input.astype(single).reshape(row_count, row_len, features)
    text_out, saved_state = block_forward(text_inputs, attn_weight, mlp_weight, vectors, allowed)
    pooling = pool_matrix(caption_lengths, slot_ids)
    text_pooled = jnp.einsum("tj,td->jd", pooling, text_out, precision=lax.Precision.HIGHEST)
    pooled_grad = pair_gradient(image_unit, text_pooled)
    upstream = jnp.einsum("tj,jd->td", pooling, pooled_grad, precision=lax.Precision.HIGHEST)
    input_grad, attn_grad, mlp_grad, vector_grad = block_backward(
        upstream, saved_state, attn_weight, mlp_weight, vectors, allowed
    )
    attn_sum, mlp_sum, vector_all, square_total = scatter_gradients(
        attn_grad, mlp_grad, vector_grad
    )
    start = lax.axis_index("dp") * 6
    vector_sum = lax.dynamic_slice_in_dim(vector_all[:12], start, 6, 1)
    grad_norm = jnp.sqrt(square_total[0, 0])
    factor = jnp.minimum(1.0, clip_norm / (grad_norm + 1e-06))
    attn_state = adam_update(
        attn_master, attn_sum, attn_first, attn_second, factor, learn_rate, weight_decay
    )
    mlp_state = adam_update(
        mlp_master, mlp_sum, mlp_first, mlp_second, factor, learn_rate, weight_decay
    )
    vector_state = adam_update(
        vector_master, vector_sum, vector_first, vector_second, factor, vector_rate, 0.0
    )
    return (
        input_grad,
        grad_norm,
        attn_sum,
        mlp_sum,
        vector_sum,
        attn_state[0],
        mlp_state[0],
        vector_state[0],
        attn_state[1],
        mlp_state[1],
        vector_state[1],
        attn_state[2],
        mlp_state[2],
        vector_state[2],
    )


def solution(mesh):
    in_specs = (
        P("dp", None),
        P("dp", None),
        P("dp", None),
        P(),
        P(),
        P(),
        P("dp", None),
        P(None, "dp", None),
        P(None, "dp"),
        P("dp", None),
        P(None, "dp", None),
        P(None, "dp"),
        P("dp", None),
        P(None, "dp", None),
        P(None, "dp"),
    )
    out_specs = (
        P("dp", None),
        P(),
        P("dp", None),
        P(None, "dp", None),
        P(None, "dp"),
        P("dp", None),
        P(None, "dp", None),
        P(None, "dp"),
        P("dp", None),
        P(None, "dp", None),
        P(None, "dp"),
        P("dp", None),
        P(None, "dp", None),
        P(None, "dp"),
    )
    return jax.shard_map(shards, mesh=mesh, in_specs=in_specs, out_specs=out_specs, check_vma=False)
```

```python
import jax
import jax.numpy as jnp
from jax import lax
from jax.experimental import pallas as pl
from jax.experimental.pallas import tpu as pltpu
from jax.sharding import PartitionSpec as P

STEP = 10


logit_scale = 60.0
clip_norm = 0.01
learn_rate = 0.05
vector_rate = 0.3
beta_first = 0.9
beta_second = 0.999
adam_epsilon = 1e-08
weight_decay = 0.1
bfloat = jnp.bfloat16
single = jnp.float32


def layer_norm(values, gain_row, bias_row):
    center = jnp.mean(values, -1, keepdims=True)
    shifted = values - center
    spread = jnp.mean(shifted * shifted, -1, keepdims=True)
    return shifted * lax.rsqrt(spread + 1e-06) * gain_row + bias_row


def unit_rows(values):
    return values * lax.rsqrt(jnp.sum(values * values, -1, keepdims=True) + 1e-06)


def sum_squares(arrays):
    return sum((jnp.sum(member * member) for member in arrays))


def adam_update(weight, gradient, first_moment, second_moment, factor, rate, decay_rate):
    clipped = gradient * factor
    first_new = beta_first * first_moment + (1.0 - beta_first) * clipped
    second_new = beta_second * second_moment + (1.0 - beta_second) * clipped * clipped
    ratio = (
        first_new
        / (1.0 - beta_first**STEP)
        / (jnp.sqrt(second_new / (1.0 - beta_second**STEP)) + adam_epsilon)
    )
    return (first_new, second_new, weight - rate * (ratio + decay_rate * weight))


MESH = pl.DeviceIdType.MESH
LINES = 144
SHARD = 448


def place():
    me = lax.axis_index("dp")
    return (me // 32, lax.rem(me // 8, 4), lax.rem(me // 2, 4), lax.rem(me, 2))


def device(x, z, y, c):
    return ((x * 4 + z) * 4 + y) * 2 + c


def plus(index, step):
    return lax.rem(index + step, 4)


class Wire:
    def __init__(self, send_sems, recv_sems):
        self.send_sems, self.recv_sems, self.count, self.open = (send_sems, recv_sems, 0, [])

    def send(self, source, target, to):
        copy = pltpu.make_async_remote_copy(
            src_ref=source,
            dst_ref=target,
            send_sem=self.send_sems.at[self.count],
            recv_sem=self.recv_sems.at[self.count],
            device_id=(to,),
            device_id_type=MESH,
        )
        copy.start()
        self.count += 1
        self.open.append(copy)
        return copy

    def drain(self, keep=()):
        for copy in self.open:
            if not any(copy is other for other in keep):
                copy.wait_send()
        self.open = list(keep)


def greet(peers):
    barrier = pltpu.get_barrier_semaphore()
    for peer in peers:
        pl.semaphore_signal(barrier, inc=1, device_id=(peer,), device_id_type=MESH)
    pl.semaphore_wait(barrier, len(peers))


class Ring:
    def __init__(self, wire, peer, view):
        self.wire, self.peer, self.view = (wire, peer, view)
        self.ahead = wire.send(view(0, None), view(0, None), peer(1))
        self.behind = wire.send(view(0, None), view(0, None), peer(3))

    def forward(self):
        self.ahead.wait_recv()
        self.low = self.wire.send(self.view(3, 0), self.view(3, 0), self.peer(1))
        self.behind.wait_recv()
        self.high = self.wire.send(self.view(1, 1), self.view(1, 1), self.peer(3))

    def finish(self):
        self.low.wait_recv()
        self.high.wait_recv()


def aligned(start, size):
    return pl.ds(pl.multiple_of(start, 128), size)


def halves(start, size, part):
    if part is None:
        return aligned(start, size)
    low = size // 256 * 128
    return aligned(start, low) if part == 0 else aligned(start + low, size - low)


def gather_kernel(
    attn_ref, mlp_ref, vector_ref, weight, turned, line, lines, natural, small, send_sems, recv_sems
):
    x, z, y, c = place()
    peers_x = lambda k: device(plus(x, k), z, y, c)
    peers_z = lambda k: device(x, plus(z, k), y, c)
    peers_y = lambda k: device(x, z, plus(y, k), c)
    sibling = device(x, z, y, 1 - c)
    wire = Wire(send_sems, recv_sems)
    lines[c, y, 0:16] = vector_ref[...]
    for m in range(3):
        for j in range(24):
            columns = slice(j * 128, (j + 1) * 128)
            rows = attn_ref[:, columns] if m == 0 else mlp_ref[m - 1, :, columns]
            line[m, pl.ds(j, 6, stride=24), :] = rows
        lines[c, y, 16 + m * LINES : 16 + (m + 1) * LINES] = line[m].astype(bfloat)
    greet([p(k) for p in (peers_x, peers_z, peers_y) for k in (1, 2, 3)] + [sibling])
    spans = [pl.ds(0, 160), pl.ds(160, 144), pl.ds(304, 144)]
    first = [
        [wire.send(lines.at[c, y, span], lines.at[c, y, span], peers_y(k)) for k in (1, 3, 2)]
        for span in spans
    ]
    swaps = []
    for m in range(3):
        for copy in first[m]:
            copy.wait_recv()
        swaps.append(wire.send(lines.at[c, :, spans[m]], lines.at[c, :, spans[m]], sibling))

    def spread(m):
        swaps[m].wait_recv()
        for s in range(8):
            natural[s * LINES : (s + 1) * LINES] = lines[
                s % 2, s // 2, 16 + m * LINES : 16 + (m + 1) * LINES
            ].astype(single)

    half = c * 1536
    quarter = (c * 4 + y) * 384
    spread(0)
    for j in range(12):
        weight[0, x, z, :, aligned((c * 12 + j) * 128, 128)] = natural[
            pl.ds(c * 12 + j, 48, stride=24), :
        ].astype(bfloat)
    for s in range(8):
        small[s * 6 : (s + 1) * 6] = lines[s % 2, s // 2, 0:16].astype(single)[0:6]
    turned[x, z] = small[...].astype(bfloat)
    attn_x = Ring(wire, peers_x, lambda k, part: weight.at[0, plus(x, k), z, :, halves(half, 1536, part)])
    turn_x = [wire.send(turned.at[x, z], turned.at[x, z], peers_x(k)) for k in (1, 3, 2)]
    spread(1)
    for j in range(12):
        weight[1, x, z, :, aligned((c * 12 + j) * 128, 128)] = natural[
            pl.ds(c * 12 + j, 48, stride=24), :
        ].astype(bfloat)
    up_z = Ring(wire, peers_z, lambda k, part: weight.at[1, x, plus(z, k), :, halves(half, 1536, part)])
    spread(2)
    for j in range(3):
        place_j = (c * 4 + y) * 3 + j
        weight[2, x, z, :, aligned(place_j * 128, 128)] = natural[
            pl.ds(place_j, 48, stride=24), :
        ].astype(bfloat)
    down_x = Ring(wire, peers_x, lambda k, part: weight.at[2, plus(x, k), z, :, halves(quarter, 384, part)])
    attn_x.forward()
    up_z.forward()
    attn_x.finish()
    for copy in turn_x:
        copy.wait_recv()
    attn_z = Ring(wire, peers_z, lambda k, part: weight.at[0, :, plus(z, k), :, halves(half, 1536, part)])
    turn_z = [wire.send(turned.at[:, z], turned.at[:, z], peers_z(k)) for k in (1, 3, 2)]
    up_z.finish()
    up_x = Ring(wire, peers_x, lambda k, part: weight.at[1, plus(x, k), :, :, halves(half, 1536, part)])
    down_x.forward()
    down_x.finish()
    down_z = Ring(wire, peers_z, lambda k, part: weight.at[2, :, plus(z, k), :, halves(quarter, 384, part)])
    across = []

    def cross(view):
        across.append(wire.send(view, view, sibling))

    cross(attn_z.view(0, None))
    cross(up_x.view(0, None))
    attn_z.forward()
    cross(attn_z.view(3, None))
    cross(attn_z.view(1, None))
    up_x.forward()
    cross(up_x.view(3, None))
    cross(up_x.view(1, None))
    down_z.forward()
    down_z.finish()
    down_y = Ring(
        wire, peers_y, lambda k, part: weight.at[2, :, :, :, halves((c * 4 + plus(y, k)) * 384, 384, part)]
    )
    cross(down_y.view(0, None))
    attn_z.finish()
    cross(attn_z.view(2, None))
    up_x.finish()
    cross(up_x.view(2, None))
    down_y.forward()
    cross(down_y.view(3, None))
    cross(down_y.view(1, None))
    down_y.finish()
    cross(down_y.view(2, None))
    for copy in turn_z + across:
        copy.wait_recv()
    wire.drain()


def gather_weights(attn_master, mlp_master, vector_master):
    vector_lines = jnp.pad(vector_master.T, ((0, 10), (0, 116))).astype(bfloat)
    copies = 64
    weight, turned = pl.pallas_call(
        gather_kernel,
        out_shape=(
            jax.ShapeDtypeStruct((3, 4, 4, 48, 3072), bfloat),
            jax.ShapeDtypeStruct((4, 4, 48, 128), bfloat),
        ),
        in_specs=[pl.BlockSpec(memory_space=pltpu.VMEM)] * 3,
        out_specs=[pl.BlockSpec(memory_space=pltpu.VMEM)] * 2,
        scratch_shapes=[
            pltpu.VMEM((3, LINES, 128), single),
            pltpu.VMEM((2, 4, SHARD, 128), bfloat),
            pltpu.VMEM((8 * LINES, 128), single),
            pltpu.VMEM((48, 128), single),
            pltpu.SemaphoreType.DMA((copies,)),
            pltpu.SemaphoreType.DMA((copies,)),
        ],
        compiler_params=pltpu.CompilerParams(
            collective_id=1, has_side_effects=True, vmem_limit_bytes=56 * 2**20
        ),
        name="gather_weights",
    )(attn_master, mlp_master, vector_lines)
    return weight, turned.reshape(768, 128)[:, :12].T.astype(single)


def matmul(left, right):
    return jnp.dot(left, right, preferred_element_type=single)


def matmul_nt(left, right):
    return lax.dot_general(left, right, (((1,), (1,)), ((), ())), preferred_element_type=single)


def matmul_tn(left, right):
    return lax.dot_general(left, right, (((0,), (0,)), ((), ())), preferred_element_type=single)


def normalized(values):
    center = jnp.mean(values, -1, keepdims=True)
    shifted = values - center
    spread = jnp.mean(shifted * shifted, -1, keepdims=True)
    inverse = lax.rsqrt(spread + 1e-06)
    return (shifted * inverse, inverse)


def normalized_back(cotangent, unit, inverse, gain):
    scaled = cotangent * gain
    center = jnp.mean(scaled, -1, keepdims=True)
    along = jnp.mean(scaled * unit, -1, keepdims=True)
    return inverse * (scaled - center - unit * along)


def gelu_parts(hidden):
    squared = hidden * hidden
    angle = jnp.tanh(hidden * (0.7978845608028654 + 0.035677408136300125 * squared))
    return (squared, angle)


def even_lanes(rows):
    return lax.broadcasted_iota(jnp.int32, (rows, 128), 1) < 64


def split_heads(values):
    even = even_lanes(values.shape[0])
    zero = jnp.zeros_like(values)
    return jnp.concatenate([jnp.where(even, values, zero), jnp.where(even, zero, values)], 0)


def join_heads(values):
    rows = values.shape[0] // 2
    return jnp.where(even_lanes(rows), values[:rows], values[rows:])


def pair_probs(queries, key_rows, bias):
    scores = matmul_nt(split_heads(queries * 0.125), key_rows)
    scores = scores + jnp.concatenate([bias, bias], 0)
    weights = jnp.exp(scores - jnp.max(scores, -1, keepdims=True))
    return weights * (1.0 / jnp.sum(weights, -1, keepdims=True))


def attend_images(qkv, attended, bias):
    starts = (0, 96, 192, 288)
    rows = lax.broadcasted_iota(jnp.int32, (16, 128), 0)

    @pl.loop(0, 6)
    def _(p):
        out = []
        for w, start in enumerate(starts):
            window = slice(start, start + 112)
            probs = pair_probs(
                qkv[window, aligned(p * 128, 128)], qkv[window, aligned((6 + p) * 128, 128)], bias[w]
            ).astype(bfloat)
            out.append(join_heads(matmul(probs, qkv[window, aligned((12 + p) * 128, 128)])))
        lanes = aligned(p * 128, 128)
        attended[0:96, lanes] = out[0][0:96].astype(bfloat)
        for w in range(1, 4):
            edge = jnp.where(rows < 4 * w, out[w - 1][96:112], out[w][0:16])
            attended[starts[w] : starts[w] + 16, lanes] = edge.astype(bfloat)
            stop = 112 if w == 3 else 96
            attended[starts[w] + 16 : starts[w] + stop, lanes] = out[w][16:stop].astype(bfloat)


def image_bias(bias):
    for w in range(4):
        first = 96 * w
        query = (lax.broadcasted_iota(jnp.int32, (112, 112), 0) + first) // 50
        key = (lax.broadcasted_iota(jnp.int32, (112, 112), 1) + first) // 50
        bias[w] = jnp.where(query == key, 0.0, -1e30)


def image_chunk(t, tokens, attn, mlp, vec, normed, qkv, attended, residual, total, bias, units, hook):
    start = pl.multiple_of(t * 400, 400)
    inputs = tokens[pl.ds(start, 400), :].astype(single)
    unit, _ = normalized(inputs)
    normed[...] = (unit * vec[0:1] + vec[1:2]).astype(bfloat)
    hook()
    for n, shift in enumerate((4, None, 5)):
        lanes = slice(n * 768, (n + 1) * 768)
        triple = matmul(normed[...], attn[:, lanes])
        if shift is not None:
            triple = triple + vec[shift : shift + 1]
        qkv[:, lanes] = triple.astype(bfloat)
    hook()
    attend_images(qkv, attended, bias)
    hook()
    residual[...] = (
        tokens[pl.ds(start, 400), :].astype(single)
        + matmul(attended[...], attn[:, 2304:3072])
        + vec[6:7]
    )
    unit, _ = normalized(residual[...])
    normed[...] = (unit * vec[2:3] + vec[3:4]).astype(bfloat)
    residual[...] = residual[...] + vec[7:8]
    hook()
    for f in range(4):
        lanes = slice(f * 768, (f + 1) * 768)
        hidden = matmul(normed[...], mlp[0, :, lanes]) + vec[8 + f : 9 + f]
        _, angle = gelu_parts(hidden)
        active = (0.5 * hidden * (1.0 + angle)).astype(bfloat)
        residual[...] = residual[...] + matmul_nt(active, mlp[1, :, lanes])
        hook()
    image = lax.broadcasted_iota(jnp.int32, (8, 400), 0)
    token = lax.broadcasted_iota(jnp.int32, (8, 400), 1)
    member = (token // 50 == image).astype(single)
    pooled = jnp.dot(
        member, residual[...], precision=lax.Precision.HIGHEST, preferred_element_type=single
    ) * (1.0 / 50.0)
    units[pl.ds(pl.multiple_of(t * 8, 8), 8), :] = unit_rows(pooled)


def image_kernel(
    tokens, attn_ref, mlp_ref, vec, units, attn, mlp, normed, qkv, attended, residual, bias, sems
):
    loads = [
        pltpu.make_async_copy(attn_ref, attn, sems.at[0]),
        pltpu.make_async_copy(mlp_ref, mlp, sems.at[1]),
    ]
    for load in loads:
        load.start()
    image_bias(bias)
    for load in loads:
        load.wait()

    @pl.loop(0, 3)
    def _(t):
        image_chunk(t, tokens, attn, mlp, vec, normed, qkv, attended, residual, None, bias, units, lambda: None)


def image_block(tokens, attn, mlp, vectors):
    vmem, anywhere = (pl.BlockSpec(memory_space=pltpu.VMEM), pl.BlockSpec(memory_space=pl.ANY))
    return pl.pallas_call(
        image_kernel,
        out_shape=jax.ShapeDtypeStruct((24, 768), single),
        in_specs=[vmem, anywhere, anywhere, vmem],
        out_specs=vmem,
        scratch_shapes=[
            pltpu.VMEM((768, 3072), bfloat),
            pltpu.VMEM((2, 768, 3072), bfloat),
            pltpu.VMEM((400, 768), bfloat),
            pltpu.VMEM((400, 2304), bfloat),
            pltpu.VMEM((400, 768), bfloat),
            pltpu.VMEM((400, 768), single),
            pltpu.VMEM((4, 112, 112), single),
            pltpu.SemaphoreType.DMA((2,)),
        ],
        compiler_params=pltpu.CompilerParams(vmem_limit_bytes=48 * 2**20),
        name="image_block",
    )(tokens, attn, mlp, vectors)


def slot_codes(index, ends, window):
    later = index >= 64
    position = jnp.where(later, index - 64, index)
    slots = [
        sum((position >= ends[2 * window + r][k]).astype(jnp.int32) for k in range(4)) for r in (0, 1)
    ]
    return jnp.where(later, slots[1] + 8, slots[0])


def text_masks(lengths, bias):
    ends = []
    for r in range(6):
        row, end = ([], 0)
        for k in range(4):
            end = end + lengths[r, k]
            row.append(end)
        ends.append(row)
    codes = []
    for w in range(3):
        query = slot_codes(lax.broadcasted_iota(jnp.int32, (128, 128), 0), ends, w)
        key = slot_codes(lax.broadcasted_iota(jnp.int32, (128, 128), 1), ends, w)
        bias[w] = jnp.where(query == key, 0.0, -1e30)
        code = slot_codes(lax.broadcasted_iota(jnp.int32, (24, 128), 1), ends, w)
        slot = jnp.where(code >= 8, code - 8, code)
        caption = 8 * w + jnp.where(code >= 8, 4, 0) + slot
        codes.append(jnp.where(slot < 4, caption, -1))
    caption = jnp.concatenate(codes, 1)
    return (caption == lax.broadcasted_iota(jnp.int32, (24, 384), 0)).astype(single)


def attend_text(qkv, attended, probs, bias):
    @pl.loop(0, 6)
    def _(p):
        for w in range(3):
            window = slice(w * 128, (w + 1) * 128)
            pair = pair_probs(
                qkv[window, aligned(p * 128, 128)], qkv[window, aligned((6 + p) * 128, 128)], bias[w]
            )
            probs[p, w] = pair
            out = matmul(pair.astype(bfloat), qkv[window, aligned((12 + p) * 128, 128)])
            attended[window, aligned(p * 128, 128)] = join_heads(out).astype(bfloat)


def attend_text_back(qkv, probs, attended_grad, triple_grad):
    @pl.loop(0, 6)
    def _(p):
        for w in range(3):
            window = slice(w * 128, (w + 1) * 128)
            at = [aligned((6 * n + p) * 128, 128) for n in range(3)]
            queries, key_rows, value_rows = (qkv[window, lanes] for lanes in at)
            grads = split_heads(attended_grad[window, at[0]])
            pair = probs[p, w]
            value_grad = matmul_tn(pair.astype(bfloat), grads)
            prob_grad = matmul_nt(grads, value_rows)
            along = jnp.sum(pair * prob_grad, -1, keepdims=True)
            score_grad = (pair * (prob_grad - along) * 0.125).astype(bfloat)
            query_grad = join_heads(matmul(score_grad, key_rows))
            key_grad = matmul_tn(score_grad, split_heads(queries))
            triple_grad[window, at[0]] = query_grad.astype(bfloat)
            triple_grad[window, at[1]] = key_grad.astype(bfloat)
            triple_grad[window, at[2]] = value_grad.astype(bfloat)


def column_sums(values):
    return jnp.sum(values.astype(single), 0, keepdims=True)


def step_kernel(
    lengths,
    tokens_ref,
    weight_ref,
    vec,
    image_ref,
    input_grad,
    attn_out,
    mlp_out,
    vector_out,
    square_out,
    weight,
    tokens,
    bias,
    probs,
    normed,
    qkv,
    attended,
    residual,
    normed_two,
    active,
    slope,
    triple_grad,
    flow,
    part_sum,
    images,
    own,
    row_part,
    row_near,
    row_far,
    held,
    from_z,
    from_x,
    from_y,
    total_z,
    total_x,
    total_y,
    late_x,
    late_z,
    down_x,
    down_z,
    whole,
    last,
    flat,
    third,
    packed,
    pieces,
    landed,
    sums,
    vec_c,
    vec_z,
    vec_x,
    vec_y,
    square,
    near,
    far,
    load_sems,
    send_sems,
    recv_sems,
):
    x, z, y, c = place()
    peers_x = lambda k: device(plus(x, k), z, y, c)
    peers_z = lambda k: device(x, plus(z, k), y, c)
    peers_y = lambda k: device(x, z, plus(y, k), c)
    sibling = device(x, z, y, 1 - c)
    group = [(k, d) for k in range(4) for d in range(2) if (k, d) != (0, 0)]
    plane = [(i, j) for i in range(4) for j in range(4) if (i, j) != (0, 0)]
    group_peer = lambda k, d: device(x, z, plus(y, k), lax.rem(c + d, 2))
    plane_peer = lambda i, j: device(plus(x, i), plus(z, j), y, c)
    wire = Wire(send_sems, recv_sems)
    turns = (1, 3, 2)

    def await_all(copies):
        for copy in copies:
            copy.wait_recv()

    loads = [pltpu.make_async_copy(weight_ref.at[m], weight.at[m], load_sems.at[m]) for m in range(3)]
    load_tokens = pltpu.make_async_copy(tokens_ref, tokens, load_sems.at[3])
    load_tokens.start()
    for load in loads:
        load.start()
    member = text_masks(lengths, bias)
    own[c] = image_ref[...]
    greet([group_peer(*g) for g in group] + [plane_peer(*p) for p in plane])

    swap_units = wire.send(own.at[c], own.at[c], sibling)
    lane = [aligned((c * 3 + o) * 128, 128) for o in range(3)]
    orders = ("yzx", "zxy", "xyz")
    axis_peers = {"x": peers_x, "z": peers_z, "y": peers_y}

    def view_of(o, axes):
        def view(k, part):
            index = []
            for name, here in (("x", x), ("z", z), ("y", y)):
                if name in axes[:-1]:
                    index.append(slice(None))
                elif name == axes[-1]:
                    index.append(plus(here, k))
                else:
                    index.append(here)
            rows = slice(None) if part is None else (pl.ds(0, 16) if part == 0 else pl.ds(16, 32))
            return images.at[(*index, rows, lane[o])]

        return view

    rings = []

    def unit_begin():
        swap_units.wait_recv()
        lanes = aligned(c * 384, 384)
        images[x, z, y, :, lanes] = own[:, :, lanes].reshape(48, 384).astype(bfloat)

    def unit_start(step):
        rings[:] = [
            Ring(wire, axis_peers[orders[o][step]], view_of(o, orders[o][: step + 1])) for o in range(3)
        ]

    def unit_forward():
        for ring in rings:
            ring.forward()

    def unit_finish():
        for ring in rings:
            ring.finish()

    load_tokens.wait()
    unit_one, _ = normalized(tokens[...].astype(single))
    normed[...] = (unit_one * vec[0:1] + vec[1:2]).astype(bfloat)
    unit_begin()
    unit_start(0)
    loads[0].wait()
    attn = lambda first, size: weight[0, :, :, :, first : first + size].reshape(768, size)
    for n, shift in enumerate((4, None, 5)):
        triple = matmul(normed[...], attn(n * 768, 768))
        if shift is not None:
            triple = triple + vec[shift : shift + 1]
        qkv[:, n * 768 : (n + 1) * 768] = triple.astype(bfloat)
        if n == 1:
            unit_forward()
    unit_finish()
    unit_start(1)
    attend_text(qkv, attended, probs, bias)
    unit_forward()
    residual[...] = tokens[...].astype(single) + matmul(attended[...], attn(2304, 768)) + vec[6:7]
    unit_two, _ = normalized(residual[...])
    normed_two[...] = (unit_two * vec[2:3] + vec[3:4]).astype(bfloat)
    unit_finish()
    unit_start(2)
    loads[1].wait()
    loads[2].wait()
    flow[...] = residual[...] + vec[7:8]
    for f in range(4):
        lanes = slice(f * 768, (f + 1) * 768)
        hidden = matmul(normed_two[...], weight[1, :, :, :, lanes].reshape(768, 768)) + vec[8 + f : 9 + f]
        squared, angle = gelu_parts(hidden)
        active[:, lanes] = (0.5 * hidden * (1.0 + angle)).astype(bfloat)
        curve = 0.7978845608028654 + 0.10703222440890037 * squared
        slope[:, lanes] = (
            0.5 * (1.0 + angle) + 0.5 * hidden * (1.0 - angle * angle) * curve
        ).astype(bfloat)
        flow[...] = flow[...] + matmul_nt(
            active[:, lanes], weight[2, :, :, :, lanes].reshape(768, 768)
        )
        if f == 1:
            unit_forward()
    unit_finish()
    mine = images.at[:, :, :, :, aligned(c * 384, 384)]
    cross = wire.send(mine, mine, sibling)
    highest = lax.Precision.HIGHEST
    per_length = 1.0 / jnp.sum(member, -1, keepdims=True)
    pooled = per_length * jnp.dot(member, flow[...], precision=highest, preferred_element_type=single)

    scale = lax.rsqrt(jnp.sum(pooled * pooled, -1, keepdims=True) + 1e-06)
    unit = pooled * scale
    cross.wait_recv()
    every = images[...].reshape(3072, 768)
    logits = logit_scale * matmul_nt(unit.astype(bfloat), every)
    powers = jnp.exp(logits)
    column = jnp.sum(powers, 1, keepdims=True)
    rows = jnp.sum(powers, 0, keepdims=True)
    for k in range(8):
        row_part[k : k + 1, :] = rows[:, k * 384 : (k + 1) * 384]
    row_near[y, c] = row_part[...]
    sent = [wire.send(row_part, row_near.at[y, c], group_peer(*g)) for g in group]
    caption = lax.broadcasted_iota(jnp.int32, (24, 3072), 0) + lax.axis_index("dp") * 24
    same = (caption == lax.broadcasted_iota(jnp.int32, (24, 3072), 1)).astype(single)
    of_column = powers / column - 2.0 * same
    await_all(sent)
    row_far[x, z] = sum(row_near[k, d] for k in range(4) for d in range(2))
    sent = [wire.send(row_far.at[x, z], row_far.at[x, z], plane_peer(*p)) for p in plane]
    await_all(sent)
    total = sum(row_far[i, j] for i in range(4) for j in range(4))
    every_row = jnp.concatenate([total[k : k + 1] for k in range(8)], 1)
    logit_grad = (logit_scale / (2.0 * 3072) * (powers / every_row + of_column)).astype(bfloat)
    unit_grad = matmul(logit_grad, every)
    pooled_grad = scale * (unit_grad - unit * jnp.sum(unit * unit_grad, -1, keepdims=True))
    flow[...] = lax.dot_general(
        member,
        pooled_grad * per_length,
        (((0,), (0,)), ((), ())),
        precision=highest,
        preferred_element_type=single,
    )

    sends = {}

    def block_grad(left, right):
        return matmul_tn(left, right).reshape(4, 4, 48, right.shape[1])

    def other_half(m, make):
        for i in range(2):
            place_i = images.at[:, :, 2 * (m % 2) + i]
            place_i[...] = make((1 - c) * 1536 + i * 768, i).astype(bfloat)
            sends[m, i] = wire.send(
                place_i, held.at[m, :, :, :, i * 768 : (i + 1) * 768], sibling
            )

    def own_half(m, make):
        for i in range(2):
            sends[m, i].wait_recv()
            lanes = slice(i * 768, (i + 1) * 768)
            held[m, :, :, :, lanes] = (
                make(c * 1536 + i * 768, i) + held[m, :, :, :, lanes].astype(single)
            ).astype(bfloat)

    wire.drain()
    branch_two = flow[...].astype(bfloat)
    vec_c[c] = jnp.zeros((16, 768), single)
    vec_c[c, 7:8] = column_sums(branch_two)
    make_two = lambda first, i: block_grad(flow[...].astype(bfloat), active[:, aligned(first, 768)])
    other_half(2, make_two)
    for f in range(4):
        lanes = slice(f * 768, (f + 1) * 768)
        active_grad = matmul(flow[...].astype(bfloat), weight[2, :, :, :, lanes].reshape(768, 768))
        hidden_grad = (active_grad * slope[:, lanes].astype(single)).astype(bfloat)
        slope[:, lanes] = hidden_grad
        vec_c[c, 8 + f : 9 + f] = column_sums(hidden_grad)
    make_one = lambda first, i: block_grad(normed_two[...], slope[:, aligned(first, 768)])
    other_half(1, make_one)
    for f in range(4):
        lanes = slice(f * 768, (f + 1) * 768)
        piece = matmul_nt(slope[:, lanes], weight[1, :, :, :, lanes].reshape(768, 768))
        part_sum[...] = piece if f == 0 else part_sum[...] + piece
    own_half(2, make_two)
    send_y = [
        wire.send(held.at[2, :, :, :, aligned(plus(y, k) * 384, 384)], from_y.at[k - 1], peers_y(k))
        for k in turns
    ]
    unit_two, inverse_two = normalized(residual[...])
    vec_c[c, 2:3] = jnp.sum(part_sum[...] * unit_two, 0, keepdims=True)
    vec_c[c, 3:4] = jnp.sum(part_sum[...], 0, keepdims=True)
    flow[...] = flow[...] + normalized_back(part_sum[...], unit_two, inverse_two, vec[2:3])
    triple_grad[:, 2304:3072] = flow[...].astype(bfloat)
    vec_c[c, 6:7] = column_sums(triple_grad[:, 2304:3072])
    own_half(1, make_one)
    send_x = [wire.send(held.at[1, plus(x, k)], from_x.at[k - 1], peers_x(k)) for k in turns]
    active[:, 0:768] = matmul_nt(triple_grad[:, 2304:3072], attn(2304, 768)).astype(bfloat)
    attend_text_back(qkv, probs, active, triple_grad)
    vec_c[c, 4:5] = column_sums(triple_grad[:, 0:768])
    vec_c[c, 5:6] = column_sums(triple_grad[:, 1536:2304])

    def make_zero(first, i):
        left = normed[...]
        if i == 1:
            left = jnp.where(first >= 2304, attended[...], left)
        return block_grad(left, triple_grad[:, aligned(first, 768)])

    wire.drain()
    other_half(0, make_zero)
    for n in range(3):
        piece = matmul_nt(triple_grad[:, n * 768 : (n + 1) * 768], attn(n * 768, 768))
        part_sum[...] = piece if n == 0 else part_sum[...] + piece
    unit_one, inverse_one = normalized(tokens[...].astype(single))
    vec_c[c, 0:1] = jnp.sum(part_sum[...] * unit_one, 0, keepdims=True)
    vec_c[c, 1:2] = jnp.sum(part_sum[...], 0, keepdims=True)
    vec_swap = wire.send(vec_c.at[c], vec_c.at[c], sibling)
    input_grad[...] = flow[...] + normalized_back(part_sum[...], unit_one, inverse_one, vec[0:1])
    own_half(0, make_zero)
    send_z = [wire.send(held.at[0, :, plus(z, k)], from_z.at[k - 1], peers_z(k)) for k in turns]
    vec_swap.wait_recv()
    vec_z[z] = vec_c[0] + vec_c[1]
    sent_vec_z = [wire.send(vec_z.at[z], vec_z.at[z], peers_z(k)) for k in turns]

    def add(base, parts):
        return base.astype(single) + sum(part.astype(single) for part in parts)

    await_all(send_y)
    quarter = aligned(y * 384, 384)
    for i in range(4):
        for j in range(4):
            total_y[i, j] = add(
                held[2, i, j, :, quarter], [from_y[k, i, j] for k in range(3)]
            ).astype(bfloat)
    down_send_x = [wire.send(total_y.at[plus(x, k)], down_x.at[k - 1], peers_x(k)) for k in turns]
    await_all(send_x)
    for i in range(4):
        total_x[i] = add(held[1, x, i], [from_x[k, i] for k in range(3)]).astype(bfloat)
    late_send_z = [wire.send(total_x.at[plus(z, k)], late_z.at[k - 1], peers_z(k)) for k in turns]
    await_all(sent_vec_z)
    vec_x[x] = vec_z[0] + vec_z[1] + vec_z[2] + vec_z[3]
    sent_vec_x = [wire.send(vec_x.at[x], vec_x.at[x], peers_x(k)) for k in turns]
    await_all(send_z)
    for i in range(4):
        total_z[i] = add(held[0, i, z], [from_z[k, i] for k in range(3)]).astype(bfloat)
    late_send_x = [wire.send(total_z.at[plus(x, k)], late_x.at[k - 1], peers_x(k)) for k in turns]
    await_all(down_send_x)
    for j in range(4):
        last[j] = add(total_y[x, j], [down_x[k, j] for k in range(3)]).astype(bfloat)
    down_send_z = [wire.send(last.at[plus(z, k)], down_z.at[k - 1], peers_z(k)) for k in turns]
    await_all(sent_vec_x)
    vec_y[y] = vec_x[0] + vec_x[1] + vec_x[2] + vec_x[3]
    sent_vec_y = [wire.send(vec_y.at[y], vec_y.at[y], peers_y(k)) for k in turns]
    await_all(late_send_z)
    whole[1] = add(total_x[z], [late_z[k] for k in range(3)])
    await_all(late_send_x)
    whole[0] = add(total_z[x], [late_x[k] for k in range(3)])
    for m in range(2):
        for j in range(12):
            flat[m, pl.ds(j, 48, stride=12), :] = whole[m, :, j * 128 : (j + 1) * 128]
    await_all(down_send_z)
    ended = add(last[z], [down_z[k] for k in range(3)])
    for j in range(3):
        third[pl.ds(j, 48, stride=3), :] = ended[:, j * 128 : (j + 1) * 128]
    packed[160:176] = jnp.zeros((16, 128), single)
    for s in range(8):
        packed[0:72] = flat[0, s * 72 : (s + 1) * 72]
        packed[72:144] = flat[1, s * 72 : (s + 1) * 72]
        packed[144:162] = third[s * 18 : (s + 1) * 18]
        pieces[s // 2, s % 2] = packed[...].astype(bfloat)
    landed[y, c] = pieces[y, c]
    piece_sent = [
        wire.send(pieces.at[plus(y, k), lax.rem(c + d, 2)], landed.at[y, c], group_peer(k, d))
        for k, d in group
    ]
    await_all(sent_vec_y)
    vec_total = vec_y[0] + vec_y[1] + vec_y[2] + vec_y[3]
    vector_out[...] = vec_total
    await_all(piece_sent)
    for h in range(2):
        for k in range(4):
            piece = landed[k, h].astype(single)
            packed[...] = piece if k == 0 else packed[...] + piece
            sums[...] = piece[144:168]
            for j in range(3):
                at = ((h * 4 + k) * 3 + j) * 128
                mlp_out[1, :, at : at + 128] = sums[pl.ds(j, 6, stride=3), :]
        for j in range(12):
            at = (h * 12 + j) * 128
            attn_out[:, at : at + 128] = packed[pl.ds(j, 6, stride=12), :]
            mlp_out[0, :, at : at + 128] = packed[pl.ds(72 + j, 6, stride=12), :]
    lanes = lax.broadcasted_iota(jnp.int32, (16, 768), 1)
    start = lax.axis_index("dp") * 6
    owned = jnp.where((lanes >= start) & (lanes < start + 6), vec_total, 0.0)
    squares = sum_squares((attn_out[...], mlp_out[0], mlp_out[1], owned))
    square[...] = jnp.broadcast_to(squares, (8, 128))
    near[y, c] = square[...]
    sent = [wire.send(square, near.at[y, c], group_peer(*g)) for g in group]
    await_all(sent)
    far[x, z] = sum(near[k, d] for k in range(4) for d in range(2))
    sent = [wire.send(far.at[x, z], far.at[x, z], plane_peer(*p)) for p in plane]
    await_all(sent)
    square_out[...] = sum(far[i, j] for i in range(4) for j in range(4))
    wire.drain()


def text_step(caption_lengths, text_input, weight, vectors, image_unit):
    copies = 144
    vmem = pl.BlockSpec(memory_space=pltpu.VMEM)
    anywhere = pl.BlockSpec(memory_space=pl.ANY)
    return pl.pallas_call(
        step_kernel,
        out_shape=(
            jax.ShapeDtypeStruct((384, 768), single),
            jax.ShapeDtypeStruct((6, 3072), single),
            jax.ShapeDtypeStruct((2, 6, 3072), single),
            jax.ShapeDtypeStruct((16, 768), single),
            jax.ShapeDtypeStruct((8, 128), single),
        ),
        in_specs=[pl.BlockSpec(memory_space=pltpu.SMEM), anywhere, anywhere, vmem, vmem],
        out_specs=[vmem] * 5,
        scratch_shapes=[
            pltpu.VMEM((3, 4, 4, 48, 3072), bfloat),
            pltpu.VMEM((384, 768), bfloat),
            pltpu.VMEM((3, 128, 128), single),
            pltpu.VMEM((6, 3, 256, 128), single),
            pltpu.VMEM((384, 768), bfloat),
            pltpu.VMEM((384, 2304), bfloat),
            pltpu.VMEM((384, 768), bfloat),
            pltpu.VMEM((384, 768), single),
            pltpu.VMEM((384, 768), bfloat),
            pltpu.VMEM((384, 3072), bfloat),
            pltpu.VMEM((384, 3072), bfloat),
            pltpu.VMEM((384, 3072), bfloat),
            pltpu.VMEM((384, 768), single),
            pltpu.VMEM((384, 768), single),
            pltpu.VMEM((4, 4, 4, 48, 768), bfloat),
            pltpu.VMEM((2, 24, 768), single),
            pltpu.VMEM((8, 384), single),
            pltpu.VMEM((4, 2, 8, 384), single),
            pltpu.VMEM((4, 4, 8, 384), single),
            pltpu.VMEM((3, 4, 4, 48, 1536), bfloat),
            pltpu.VMEM((3, 4, 48, 1536), bfloat),
            pltpu.VMEM((3, 4, 48, 1536), bfloat),
            pltpu.VMEM((3, 4, 4, 48, 384), bfloat),
            pltpu.VMEM((4, 48, 1536), bfloat),
            pltpu.VMEM((4, 48, 1536), bfloat),
            pltpu.VMEM((4, 4, 48, 384), bfloat),
            pltpu.VMEM((3, 48, 1536), bfloat),
            pltpu.VMEM((3, 48, 1536), bfloat),
            pltpu.VMEM((3, 4, 48, 384), bfloat),
            pltpu.VMEM((3, 48, 384), bfloat),
            pltpu.VMEM((2, 48, 1536), single),
            pltpu.VMEM((4, 48, 384), bfloat),
            pltpu.VMEM((2, 576, 128), single),
            pltpu.VMEM((144, 128), single),
            pltpu.VMEM((176, 128), single),
            pltpu.VMEM((4, 2, 176, 128), bfloat),
            pltpu.VMEM((4, 2, 176, 128), bfloat),
            pltpu.VMEM((24, 128), single),
            pltpu.VMEM((2, 16, 768), single),
            pltpu.VMEM((4, 16, 768), single),
            pltpu.VMEM((4, 16, 768), single),
            pltpu.VMEM((4, 16, 768), single),
            pltpu.VMEM((8, 128), single),
            pltpu.VMEM((4, 2, 8, 128), single),
            pltpu.VMEM((4, 4, 8, 128), single),
            pltpu.SemaphoreType.DMA((4,)),
            pltpu.SemaphoreType.DMA((copies,)),
            pltpu.SemaphoreType.DMA((copies,)),
        ],
        compiler_params=pltpu.CompilerParams(
            collective_id=2, has_side_effects=True, vmem_limit_bytes=63 * 2**20
        ),
        name="text_step",
    )(caption_lengths, text_input, weight, vectors, image_unit)


def shards(
    text_input,
    caption_lengths,
    image_tokens,
    image_attn,
    image_mlp,
    image_vectors,
    attn_master,
    mlp_master,
    vector_master,
    attn_first,
    mlp_first,
    vector_first,
    attn_second,
    mlp_second,
    vector_second,
):
    weight, vectors = gather_weights(attn_master, mlp_master, vector_master)
    image_unit = image_block(image_tokens, image_attn, image_mlp, image_vectors)
    input_grad, attn_sum, mlp_sum, vector_all, square_total = text_step(
        caption_lengths, text_input, weight, vectors, image_unit
    )
    start = lax.axis_index("dp") * 6
    vector_sum = lax.dynamic_slice_in_dim(vector_all[:12], start, 6, 1)
    grad_norm = jnp.sqrt(square_total[0, 0])
    factor = jnp.minimum(1.0, clip_norm / (grad_norm + 1e-06))
    attn_state = adam_update(
        attn_master, attn_sum, attn_first, attn_second, factor, learn_rate, weight_decay
    )
    mlp_state = adam_update(
        mlp_master, mlp_sum, mlp_first, mlp_second, factor, learn_rate, weight_decay
    )
    vector_state = adam_update(
        vector_master, vector_sum, vector_first, vector_second, factor, vector_rate, 0.0
    )
    return (
        input_grad,
        grad_norm,
        attn_sum,
        mlp_sum,
        vector_sum,
        attn_state[0],
        mlp_state[0],
        vector_state[0],
        attn_state[1],
        mlp_state[1],
        vector_state[1],
        attn_state[2],
        mlp_state[2],
        vector_state[2],
    )


def solution(mesh):
    in_specs = (
        P("dp", None),
        P("dp", None),
        P("dp", None),
        P(),
        P(),
        P(),
        P("dp", None),
        P(None, "dp", None),
        P(None, "dp"),
        P("dp", None),
        P(None, "dp", None),
        P(None, "dp"),
        P("dp", None),
        P(None, "dp", None),
        P(None, "dp"),
    )
    out_specs = (
        P("dp", None),
        P(),
        P("dp", None),
        P(None, "dp", None),
        P(None, "dp"),
        P("dp", None),
        P(None, "dp", None),
        P(None, "dp"),
        P("dp", None),
        P(None, "dp", None),
        P(None, "dp"),
        P("dp", None),
        P(None, "dp", None),
        P(None, "dp"),
    )
    return jax.shard_map(shards, mesh=mesh, in_specs=in_specs, out_specs=out_specs, check_vma=False)
```

```python
import jax
import jax.numpy as jnp
from jax import lax
from jax.experimental import pallas as pl
from jax.experimental.pallas import tpu as pltpu
from jax.sharding import PartitionSpec as P

STEP = 10


logit_scale = 60.0
clip_norm = 0.01
learn_rate = 0.05
vector_rate = 0.3
beta_first = 0.9
beta_second = 0.999
adam_epsilon = 1e-08
weight_decay = 0.1
bfloat = jnp.bfloat16
single = jnp.float32


def unit_rows(values):
    return values * lax.rsqrt(jnp.sum(values * values, -1, keepdims=True) + 1e-06)


def sum_squares(arrays):
    return sum((jnp.sum(member * member) for member in arrays))


def adam_update(weight, gradient, first_moment, second_moment, factor, rate, decay_rate):
    clipped = gradient * factor
    first_new = beta_first * first_moment + (1.0 - beta_first) * clipped
    second_new = beta_second * second_moment + (1.0 - beta_second) * clipped * clipped
    ratio = (
        first_new
        / (1.0 - beta_first**STEP)
        / (jnp.sqrt(second_new / (1.0 - beta_second**STEP)) + adam_epsilon)
    )
    return (first_new, second_new, weight - rate * (ratio + decay_rate * weight))


MESH = pl.DeviceIdType.MESH
LINES = 144
SHARD = 448
TURNS = (1, 3, 2)


def place():
    me = lax.axis_index("dp")
    return (me // 32, lax.rem(me // 8, 4), lax.rem(me // 2, 4), lax.rem(me, 2))


def device(x, z, y, c):
    return ((x * 4 + z) * 4 + y) * 2 + c


def plus(index, step):
    return lax.rem(index + step, 4)


def made(item):
    return item() if callable(item) else item


class Copy:
    def __init__(self, wire, slot, source, target, to):
        self.wire, self.slot, self.parts = (wire, slot, (source, target, to))

    def make(self):
        source, target, to = (made(part) for part in self.parts)
        return pltpu.make_async_remote_copy(
            src_ref=source,
            dst_ref=target,
            send_sem=self.wire.send_sems.at[self.slot],
            recv_sem=self.wire.recv_sems.at[self.slot],
            device_id=(to,),
            device_id_type=MESH,
        )

    def wait_recv(self):
        self.make().wait_recv()

    def wait_send(self):
        self.make().wait_send()


class Wire:
    def __init__(self, send_sems, recv_sems):
        self.send_sems, self.recv_sems, self.count, self.open = (send_sems, recv_sems, 0, [])

    def send(self, source, target, to):
        copy = Copy(self, self.count, source, target, to)
        copy.make().start()
        self.count += 1
        self.open.append(copy)
        return copy

    def drain(self):
        for copy in self.open:
            copy.wait_send()
        self.open = []


def await_all(copies):
    for copy in copies:
        copy.wait_recv()


def greet(peers):
    barrier = pltpu.get_barrier_semaphore()
    for peer in peers:
        pl.semaphore_signal(barrier, inc=1, device_id=(peer,), device_id_type=MESH)
    pl.semaphore_wait(barrier, len(peers))


class Ring:
    def __init__(self, wire, peer, view):
        self.wire, self.peer, self.view = (wire, peer, view)
        self.ahead = self.pass_on(0, None, 1)
        self.behind = self.pass_on(0, None, 3)

    def pass_on(self, k, part, step):
        block = lambda: self.view(k, part)
        return self.wire.send(block, block, lambda: self.peer(step))

    def forward(self):
        self.ahead.wait_recv()
        self.low = self.pass_on(3, 0, 1)
        self.behind.wait_recv()
        self.high = self.pass_on(1, 1, 3)

    def finish(self):
        self.low.wait_recv()
        self.high.wait_recv()


def aligned(start, size):
    return pl.ds(pl.multiple_of(start, 128), size)


def halves(start, size, part):
    if part is None:
        return aligned(start, size)
    low = size // 256 * 128
    return aligned(start, low) if part == 0 else aligned(start + low, size - low)


class Gather:
    def __init__(self, wire, peers, here, weight, turned, lines, natural, small):
        self.wire, self.here, self.weight, self.turned = (wire, here, weight, turned)
        self.lines, self.natural, self.small = (lines, natural, small)
        self.peers_x, self.peers_z, self.peers_y, self.sibling = peers
        x, z, y, c = here
        self.half, self.quarter = (c * 1536, (c * 4 + y) * 384)
        self.across = []

    def span(self, m):
        return (pl.ds(0, 160), pl.ds(160, 144), pl.ds(304, 144))[m]

    def begin(self):
        x, z, y, c = self.here
        self.first = []
        for m in range(3):
            view = lambda m=m: self.lines.at[c, y, self.span(m)]
            self.first.append(
                [self.wire.send(view, view, lambda k=k: self.peers_y(k)) for k in TURNS]
            )

    def swap(self):
        x, z, y, c = self.here
        self.swaps = []
        for m in range(3):
            await_all(self.first[m])
            view = lambda m=m: self.lines.at[c, :, self.span(m)]
            self.swaps.append(self.wire.send(view, view, self.sibling))

    def spread(self, m):
        x, z, y, c = self.here
        self.swaps[m].wait_recv()
        for s in range(8):
            self.natural[s * LINES : (s + 1) * LINES] = self.lines[
                s % 2, s // 2, 16 + m * LINES : 16 + (m + 1) * LINES
            ].astype(single)
        start, count = (c * 12, 12) if m < 2 else ((c * 4 + y) * 3, 3)
        for j in range(count):
            self.weight[m, x, z, :, aligned((start + j) * 128, 128)] = self.natural[
                pl.ds(start + j, 48, stride=24), :
            ].astype(bfloat)

    def spread_all(self):
        x, z, y, c = self.here
        ring = lambda peer, view: Ring(self.wire, peer, view)
        self.spread(2)
        self.down_x = ring(
            self.peers_x,
            lambda k, part: self.weight.at[2, plus(x, k), z, :, halves(self.quarter, 384, part)],
        )
        self.spread(0)
        self.attn_x = ring(
            self.peers_x,
            lambda k, part: self.weight.at[0, plus(x, k), z, :, halves(self.half, 1536, part)],
        )
        self.spread(1)
        self.up_z = ring(
            self.peers_z,
            lambda k, part: self.weight.at[1, x, plus(z, k), :, halves(self.half, 1536, part)],
        )
        for s in range(8):
            self.small[s * 6 : (s + 1) * 6] = self.lines[s % 2, s // 2, 0:16].astype(single)[0:6]
        self.turned[x, z] = self.small[...].astype(bfloat)
        view = lambda: self.turned.at[x, z]
        self.turn_x = [self.wire.send(view, view, lambda k=k: self.peers_x(k)) for k in TURNS]

    def forward_one(self):
        self.down_x.forward()
        self.attn_x.forward()
        self.up_z.forward()

    def second(self):
        x, z, y, c = self.here
        self.down_x.finish()
        self.down_z = Ring(
            self.wire,
            self.peers_z,
            lambda k, part: self.weight.at[2, :, plus(z, k), :, halves(self.quarter, 384, part)],
        )
        self.downs = [self.down_y(0)]
        self.attn_x.finish()
        self.attn_z = Ring(
            self.wire,
            self.peers_z,
            lambda k, part: self.weight.at[0, :, plus(z, k), :, halves(self.half, 1536, part)],
        )
        self.up_z.finish()
        self.up_x = Ring(
            self.wire,
            self.peers_x,
            lambda k, part: self.weight.at[1, plus(x, k), :, :, halves(self.half, 1536, part)],
        )
        await_all(self.turn_x)
        view = lambda: self.turned.at[:, z]
        self.turn_z = [self.wire.send(view, view, lambda k=k: self.peers_z(k)) for k in TURNS]
        self.cross(lambda: self.attn_z.view(0, None))
        self.cross(lambda: self.up_x.view(0, None))

    def down_y(self, j):
        x, z, y, c = self.here
        return Ring(
            self.wire,
            self.peers_y,
            lambda k, part: self.weight.at[
                2, :, plus(z, j), :, halves((c * 4 + plus(y, k)) * 384, 384, part)
            ],
        )

    def cross(self, view):
        self.across.append(self.wire.send(view, view, self.sibling))

    def cross_ring(self, ring, turns):
        for k in turns:
            self.cross(lambda k=k: ring.view(k, None))

    def forward_two(self):
        self.down_z.forward()
        self.downs[0].forward()

    def third(self):
        self.down_z.finish()
        self.downs += [self.down_y(j) for j in (3, 1, 2)]

    def forward_three(self):
        self.attn_z.forward()
        self.cross_ring(self.attn_z, (3, 1))
        self.up_x.forward()
        self.cross_ring(self.up_x, (3, 1))

    def forward_four(self):
        self.downs[0].finish()
        self.cross_ring(self.downs[0], (0, 3, 1, 2))
        for ring in self.downs[1:]:
            ring.forward()
            self.cross_ring(ring, (0, 3, 1))

    def finish(self):
        self.attn_z.finish()
        self.cross_ring(self.attn_z, (2,))
        self.up_x.finish()
        self.cross_ring(self.up_x, (2,))
        for ring in self.downs[1:]:
            ring.finish()
            self.cross_ring(ring, (2,))
        await_all(self.turn_z)

    def end(self):
        await_all(self.across)


def matmul(left, right):
    return jnp.dot(left, right, preferred_element_type=single)


def matmul_nt(left, right):
    return lax.dot_general(left, right, (((1,), (1,)), ((), ())), preferred_element_type=single)


def matmul_tn(left, right):
    return lax.dot_general(left, right, (((0,), (0,)), ((), ())), preferred_element_type=single)


def normalized(values):
    center = jnp.mean(values, -1, keepdims=True)
    shifted = values - center
    spread = jnp.mean(shifted * shifted, -1, keepdims=True)
    inverse = lax.rsqrt(spread + 1e-06)
    return (shifted * inverse, inverse)


def normalized_back(cotangent, unit, inverse, gain):
    scaled = cotangent * gain
    center = jnp.mean(scaled, -1, keepdims=True)
    along = jnp.mean(scaled * unit, -1, keepdims=True)
    return inverse * (scaled - center - unit * along)


def gelu_parts(hidden):
    squared = hidden * hidden
    angle = jnp.tanh(hidden * (0.7978845608028654 + 0.035677408136300125 * squared))
    return (squared, angle)


def even_lanes(rows):
    return lax.broadcasted_iota(jnp.int32, (rows, 128), 1) < 64


def split_heads(values):
    even = even_lanes(values.shape[0])
    zero = jnp.zeros_like(values)
    return jnp.concatenate([jnp.where(even, values, zero), jnp.where(even, zero, values)], 0)


def join_heads(values):
    rows = values.shape[0] // 2
    return jnp.where(even_lanes(rows), values[:rows], values[rows:])


def pair_weights(queries, key_rows, bias):
    scores = matmul_nt(split_heads(queries * 0.125), key_rows)
    scores = scores + jnp.concatenate([bias, bias], 0)
    weights = jnp.exp(scores - jnp.max(scores, -1, keepdims=True))
    return (weights, 1.0 / jnp.sum(weights, -1, keepdims=True))


def attend_images(qkv, attended, bias):
    starts = (0, 96, 192, 288)
    rows = lax.broadcasted_iota(jnp.int32, (16, 128), 0)

    @pl.loop(0, 6, unroll=3)
    def _(p):
        out = []
        for w, start in enumerate(starts):
            window = slice(start, start + 112)
            weights, scale = pair_weights(
                qkv[window, aligned(p * 128, 128)], qkv[window, aligned((6 + p) * 128, 128)], bias[w]
            )
            values = qkv[window, aligned((12 + p) * 128, 128)]
            out.append(join_heads(matmul(weights.astype(bfloat), values) * scale))
        lanes = aligned(p * 128, 128)
        attended[0:96, lanes] = out[0][0:96].astype(bfloat)
        for w in range(1, 4):
            edge = jnp.where(rows < 4 * w, out[w - 1][96:112], out[w][0:16])
            attended[starts[w] : starts[w] + 16, lanes] = edge.astype(bfloat)
            stop = 112 if w == 3 else 96
            attended[starts[w] + 16 : starts[w] + stop, lanes] = out[w][16:stop].astype(bfloat)


def image_bias(bias):
    for w in range(4):
        first = 96 * w
        query = (lax.broadcasted_iota(jnp.int32, (112, 112), 0) + first) // 50
        key = (lax.broadcasted_iota(jnp.int32, (112, 112), 1) + first) // 50
        bias[w] = jnp.where(query == key, 0.0, -1e30)


def image_chunk(t, tokens, weight, vec, normed, qkv, attended, residual, bias, units, hook):
    lanes_t = slice(t * 768, (t + 1) * 768)
    unit, _ = normalized(tokens[:, lanes_t].astype(single))
    normed[...] = (unit * vec[0:1] + vec[1:2]).astype(bfloat)
    hook()
    for n, shift in enumerate((4, None, 5)):
        triple = matmul(normed[...], weight(0, n * 768, 768))
        if shift is not None:
            triple = triple + vec[shift : shift + 1]
        qkv[:, n * 768 : (n + 1) * 768] = triple.astype(bfloat)
    hook()
    attend_images(qkv, attended, bias)
    hook()
    residual[...] = (
        tokens[:, lanes_t].astype(single) + matmul(attended[...], weight(0, 2304, 768)) + vec[6:7]
    )
    unit, _ = normalized(residual[...])
    normed[...] = (unit * vec[2:3] + vec[3:4]).astype(bfloat)
    residual[...] = residual[...] + vec[7:8]
    hook()
    for f in range(4):
        hidden = matmul(normed[...], weight(1, f * 768, 768)) + vec[8 + f : 9 + f]
        _, angle = gelu_parts(hidden)
        active = (0.5 * hidden * (1.0 + angle)).astype(bfloat)
        residual[...] = residual[...] + matmul_nt(active, weight(2, f * 768, 768))
        hook()
    image = lax.broadcasted_iota(jnp.int32, (8, 400), 0)
    token = lax.broadcasted_iota(jnp.int32, (8, 400), 1)
    member = (token // 50 == image).astype(bfloat)
    high = residual[...].astype(bfloat)
    low = (residual[...] - high.astype(single)).astype(bfloat)
    pooled = (matmul(member, high) + matmul(member, low)) * (1.0 / 50.0)
    units[t * 8 : (t + 1) * 8, :] = unit_rows(pooled)


PLAN = {
    (0, 2): "swap",
    (0, 4): "spread_all",
    (0, 5): "forward_one",
    (0, 7): "second",
    (1, 2): "forward_two",
    (1, 4): "third",
    (2, 2): "forward_three",
    (2, 4): "forward_four",
    "after": "finish",
}


def slot_codes(index, ends, window):
    later = index >= 64
    position = jnp.where(later, index - 64, index)
    slots = [
        sum((position >= ends[2 * window + r][k]).astype(jnp.int32) for k in range(4)) for r in (0, 1)
    ]
    return jnp.where(later, slots[1] + 8, slots[0])


def text_masks(lengths, bias):
    ends = []
    for r in range(6):
        row, end = ([], 0)
        for k in range(4):
            end = end + lengths[r, k]
            row.append(end)
        ends.append(row)
    codes = []
    for w in range(3):
        query = slot_codes(lax.broadcasted_iota(jnp.int32, (128, 128), 0), ends, w)
        key = slot_codes(lax.broadcasted_iota(jnp.int32, (128, 128), 1), ends, w)
        bias[w] = jnp.where(query == key, 0.0, -1e30)
        code = slot_codes(lax.broadcasted_iota(jnp.int32, (24, 128), 1), ends, w)
        slot = jnp.where(code >= 8, code - 8, code)
        caption = 8 * w + jnp.where(code >= 8, 4, 0) + slot
        codes.append(jnp.where(slot < 4, caption, -1))
    caption = jnp.concatenate(codes, 1)
    return (caption == lax.broadcasted_iota(jnp.int32, (24, 384), 0)).astype(single)


def attend_text(qkv, attended, probs, bias):
    @pl.loop(0, 6, unroll=3)
    def _(p):
        for w in range(3):
            window = slice(w * 128, (w + 1) * 128)
            weights, scale = pair_weights(
                qkv[window, aligned(p * 128, 128)], qkv[window, aligned((6 + p) * 128, 128)], bias[w]
            )
            pair = weights * scale
            probs[pl.ds(pl.multiple_of((p * 3 + w) * 256, 256), 256)] = pair
            out = matmul(pair.astype(bfloat), qkv[window, aligned((12 + p) * 128, 128)])
            attended[window, aligned(p * 128, 128)] = join_heads(out).astype(bfloat)


def attend_text_back(qkv, probs, attended_grad, triple_grad):
    @pl.loop(0, 6, unroll=3)
    def _(p):
        for w in range(3):
            window = slice(w * 128, (w + 1) * 128)
            at = [aligned((6 * n + p) * 128, 128) for n in range(3)]
            queries, key_rows, value_rows = (qkv[window, lanes] for lanes in at)
            grads = split_heads(attended_grad[window, at[0]])
            pair = probs[pl.ds(pl.multiple_of((p * 3 + w) * 256, 256), 256)]
            value_grad = matmul_tn(pair.astype(bfloat), grads)
            prob_grad = matmul_nt(grads, value_rows)
            along = jnp.sum(pair * prob_grad, -1, keepdims=True)
            score_grad = (pair * (prob_grad - along) * 0.125).astype(bfloat)
            query_grad = join_heads(matmul(score_grad, key_rows))
            key_grad = matmul_tn(score_grad, split_heads(queries))
            triple_grad[window, at[0]] = query_grad.astype(bfloat)
            triple_grad[window, at[1]] = key_grad.astype(bfloat)
            triple_grad[window, at[2]] = value_grad.astype(bfloat)


def column_sums(values):
    return jnp.sum(values.astype(single), 0, keepdims=True)


def step_kernel(
    lengths,
    tokens_ref,
    image_ref,
    image_attn_ref,
    image_mlp_ref,
    image_vec,
    attn_ref,
    mlp_ref,
    vector_ref,
    input_grad,
    attn_out,
    mlp_out,
    vector_out,
    square_out,
    weight,
    store,
    tokens,
    bias,
    image_masks,
    units,
    probs,
    normed,
    qkv,
    attended,
    residual,
    normed_two,
    active,
    slope,
    triple_grad,
    flow,
    part_sum,
    images,
    own,
    lines,
    small,
    turned,
    vec,
    row_part,
    row_near,
    row_far,
    late_x,
    late_z,
    down_x,
    down_z,
    whole,
    last,
    flat,
    third,
    packed,
    pieces,
    landed,
    sums,
    vec_c,
    vec_z,
    vec_x,
    vec_y,
    square,
    near,
    far,
    load_sems,
    send_sems,
    recv_sems,
):
    x, z, y, c = place()
    peers_x = lambda k: device(plus(x, k), z, y, c)
    peers_z = lambda k: device(x, plus(z, k), y, c)
    peers_y = lambda k: device(x, z, plus(y, k), c)
    sibling = device(x, z, y, 1 - c)
    group = [(k, d) for k in range(4) for d in range(2) if (k, d) != (0, 0)]
    plane = [(i, j) for i in range(4) for j in range(4) if (i, j) != (0, 0)]
    group_peer = lambda k, d: device(x, z, plus(y, k), lax.rem(c + d, 2))
    plane_peer = lambda i, j: device(plus(x, i), plus(z, j), y, c)
    wire = Wire(send_sems, recv_sems)
    turns = TURNS

    held = store.at[:, :, :, :, 0:1536]
    from_z = [store.at[0, k, :, :, 1536:3072] for k in range(3)]
    from_x = [store.at[1, k, :, :, 1536:3072] for k in range(3)]
    from_y = [store.at[2, :, :, :, 1536 + 384 * k : 1920 + 384 * k] for k in range(3)]
    total_z, total_x = (store.at[m, 3, :, :, 1536:3072] for m in range(2))
    total_y = store.at[2, :, :, :, 2688:3072]

    loads = [
        pltpu.make_async_copy(source, target, load_sems.at[n])
        for n, (source, target) in enumerate(
            [
                (image_ref.at[0:400], slope.at[:, 0:768]),
                (image_attn_ref, store.at[0]),
                (image_mlp_ref, store.at[1:3]),
                (image_ref.at[400:800], slope.at[:, 768:1536]),
                (image_ref.at[800:1200], slope.at[:, 1536:2304]),
                (tokens_ref, tokens),
            ]
        )
    ]
    for load in loads:
        load.start()
    natural, line = (probs.at[0:1152], [probs.at[1152 + 144 * m : 1296 + 144 * m] for m in range(3)])
    lines[c, y, 0:16] = vector_ref[...]
    for m in range(3):
        for j in range(24):
            columns = slice(j * 128, (j + 1) * 128)
            rows = attn_ref[:, columns] if m == 0 else mlp_ref[m - 1, :, columns]
            line[m][pl.ds(j, 6, stride=24), :] = rows
        lines[c, y, 16 + m * LINES : 16 + (m + 1) * LINES] = line[m][...].astype(bfloat)
    greet([group_peer(*g) for g in group] + [plane_peer(*p) for p in plane])
    gather = Gather(
        wire, (peers_x, peers_z, peers_y, sibling), (x, z, y, c), weight, turned, lines, natural, small
    )
    gather.begin()
    image_bias(image_masks)
    for load in loads:
        load.wait()
    plan = PLAN
    image_weight = lambda m, first, size: store[m, :, :, :, first : first + size].reshape(768, size)

    for t in range(3):
        points = iter(range(99))

        def hook():
            for name in plan.get((t, next(points)), "").split():
                getattr(gather, name)()

        image_chunk(
            t, slope, image_weight, image_vec, normed, qkv, attended, residual, image_masks, units, hook
        )

    for name in plan["after"].split():
        getattr(gather, name)()
    own[c] = units[...]
    swap_units = wire.send(own.at[c], own.at[c], sibling)
    member = text_masks(lengths, bias)
    gather.end()
    vec[...] = turned[...].reshape(768, 128).astype(single).T[0:16]

    lane = [aligned((c * 3 + o) * 128, 128) for o in range(3)]
    orders = ("yzx", "zxy", "xyz")
    axis_peers = {"x": peers_x, "z": peers_z, "y": peers_y}

    def view_of(o, axes):
        def view(k, part):
            index = []
            for name, here in (("x", x), ("z", z), ("y", y)):
                if name in axes[:-1]:
                    index.append(slice(None))
                elif name == axes[-1]:
                    index.append(plus(here, k))
                else:
                    index.append(here)
            rows = slice(None) if part is None else (pl.ds(0, 16) if part == 0 else pl.ds(16, 32))
            return images.at[(*index, rows, lane[o])]

        return view

    rings = []

    def unit_begin():
        swap_units.wait_recv()
        lanes = aligned(c * 384, 384)
        images[x, z, y, :, lanes] = own[:, :, lanes].reshape(48, 384).astype(bfloat)

    def unit_start(step):
        rings[:] = [
            Ring(wire, axis_peers[orders[o][step]], view_of(o, orders[o][: step + 1])) for o in range(3)
        ]

    def unit_forward():
        for ring in rings:
            ring.forward()

    def unit_finish():
        for ring in rings:
            ring.finish()

    normed, qkv, attended, residual, slope = (
        ref.at[0:384] for ref in (normed, qkv, attended, residual, slope)
    )
    unit_one, _ = normalized(tokens[...].astype(single))
    normed[...] = (unit_one * vec[0:1] + vec[1:2]).astype(bfloat)
    unit_begin()
    unit_start(0)
    attn = lambda first, size: weight[0, :, :, :, first : first + size].reshape(768, size)
    for n, shift in enumerate((4, None, 5)):
        triple = matmul(normed[...], attn(n * 768, 768))
        if shift is not None:
            triple = triple + vec[shift : shift + 1]
        qkv[:, n * 768 : (n + 1) * 768] = triple.astype(bfloat)
        if n == 1:
            unit_forward()
    unit_finish()
    unit_start(1)
    attend_text(qkv, attended, probs, bias)
    unit_forward()
    residual[...] = tokens[...].astype(single) + matmul(attended[...], attn(2304, 768)) + vec[6:7]
    unit_two, _ = normalized(residual[...])
    normed_two[...] = (unit_two * vec[2:3] + vec[3:4]).astype(bfloat)
    unit_finish()
    unit_start(2)
    flow[...] = residual[...] + vec[7:8]
    for f in range(4):
        lanes = slice(f * 768, (f + 1) * 768)
        hidden = matmul(normed_two[...], weight[1, :, :, :, lanes].reshape(768, 768)) + vec[8 + f : 9 + f]
        squared, angle = gelu_parts(hidden)
        active[:, lanes] = (0.5 * hidden * (1.0 + angle)).astype(bfloat)
        curve = 0.7978845608028654 + 0.10703222440890037 * squared
        slope[:, lanes] = (
            0.5 * (1.0 + angle) + 0.5 * hidden * (1.0 - angle * angle) * curve
        ).astype(bfloat)
        flow[...] = flow[...] + matmul_nt(
            active[:, lanes], weight[2, :, :, :, lanes].reshape(768, 768)
        )
        if f == 1:
            unit_forward()
    unit_finish()
    mine = images.at[:, :, :, :, aligned(c * 384, 384)]
    cross = wire.send(mine, mine, sibling)
    highest = lax.Precision.HIGHEST
    per_length = 1.0 / jnp.sum(member, -1, keepdims=True)
    pooled = per_length * jnp.dot(member, flow[...], precision=highest, preferred_element_type=single)

    scale = lax.rsqrt(jnp.sum(pooled * pooled, -1, keepdims=True) + 1e-06)
    unit = pooled * scale
    cross.wait_recv()
    every = images[...].reshape(3072, 768)
    logits = logit_scale * matmul_nt(unit.astype(bfloat), every)
    powers = jnp.exp(logits)
    column = jnp.sum(powers, 1, keepdims=True)
    rows = jnp.sum(powers, 0, keepdims=True)
    for k in range(8):
        row_part[k : k + 1, :] = rows[:, k * 384 : (k + 1) * 384]
    row_near[y, c] = row_part[...]
    sent = [wire.send(row_part, row_near.at[y, c], group_peer(*g)) for g in group]
    caption = lax.broadcasted_iota(jnp.int32, (24, 3072), 0) + lax.axis_index("dp") * 24
    same = (caption == lax.broadcasted_iota(jnp.int32, (24, 3072), 1)).astype(single)
    of_column = powers / column - 2.0 * same
    await_all(sent)
    row_far[x, z] = sum(row_near[k, d] for k in range(4) for d in range(2))
    sent = [wire.send(row_far.at[x, z], row_far.at[x, z], plane_peer(*p)) for p in plane]
    await_all(sent)
    total = sum(row_far[i, j] for i in range(4) for j in range(4))
    every_row = jnp.concatenate([total[k : k + 1] for k in range(8)], 1)
    logit_grad = (logit_scale / (2.0 * 3072) * (powers / every_row + of_column)).astype(bfloat)
    unit_grad = matmul(logit_grad, every)
    pooled_grad = scale * (unit_grad - unit * jnp.sum(unit * unit_grad, -1, keepdims=True))
    flow[...] = lax.dot_general(
        member,
        pooled_grad * per_length,
        (((0,), (0,)), ((), ())),
        precision=highest,
        preferred_element_type=single,
    )

    sends = {}

    def block_grad(left, right):
        return matmul_tn(left, right).reshape(4, 4, 48, right.shape[1])

    def other_half(m, make):
        for i in range(2):
            place_i = images.at[:, :, 2 * (m % 2) + i]
            place_i[...] = make((1 - c) * 1536 + i * 768, i).astype(bfloat)
            sends[m, i] = wire.send(
                place_i, held.at[m, :, :, :, i * 768 : (i + 1) * 768], sibling
            )

    def own_half(m, make):
        for i in range(2):
            sends[m, i].wait_recv()
            lanes = slice(i * 768, (i + 1) * 768)
            held[m, :, :, :, lanes] = (
                make(c * 1536 + i * 768, i) + held[m, :, :, :, lanes].astype(single)
            ).astype(bfloat)

    wire.drain()
    branch_two = flow[...].astype(bfloat)
    vec_c[c] = jnp.zeros((16, 768), single)
    vec_c[c, 7:8] = column_sums(branch_two)
    make_two = lambda first, i: block_grad(flow[...].astype(bfloat), active[:, aligned(first, 768)])
    other_half(2, make_two)
    for f in range(4):
        lanes = slice(f * 768, (f + 1) * 768)
        active_grad = matmul(flow[...].astype(bfloat), weight[2, :, :, :, lanes].reshape(768, 768))
        hidden_grad = (active_grad * slope[:, lanes].astype(single)).astype(bfloat)
        slope[:, lanes] = hidden_grad
        vec_c[c, 8 + f : 9 + f] = column_sums(hidden_grad)
    make_one = lambda first, i: block_grad(normed_two[...], slope[:, aligned(first, 768)])
    other_half(1, make_one)
    for f in range(4):
        lanes = slice(f * 768, (f + 1) * 768)
        piece = matmul_nt(slope[:, lanes], weight[1, :, :, :, lanes].reshape(768, 768))
        part_sum[...] = piece if f == 0 else part_sum[...] + piece
    own_half(2, make_two)
    send_y = [
        wire.send(held.at[2, :, :, :, aligned(plus(y, k) * 384, 384)], from_y[k - 1], peers_y(k))
        for k in turns
    ]
    unit_two, inverse_two = normalized(residual[...])
    vec_c[c, 2:3] = jnp.sum(part_sum[...] * unit_two, 0, keepdims=True)
    vec_c[c, 3:4] = jnp.sum(part_sum[...], 0, keepdims=True)
    flow[...] = flow[...] + normalized_back(part_sum[...], unit_two, inverse_two, vec[2:3])
    triple_grad[:, 2304:3072] = flow[...].astype(bfloat)
    vec_c[c, 6:7] = column_sums(triple_grad[:, 2304:3072])
    own_half(1, make_one)
    send_x = [wire.send(held.at[1, plus(x, k)], from_x[k - 1], peers_x(k)) for k in turns]
    active[:, 0:768] = matmul_nt(triple_grad[:, 2304:3072], attn(2304, 768)).astype(bfloat)
    attend_text_back(qkv, probs, active, triple_grad)
    vec_c[c, 4:5] = column_sums(triple_grad[:, 0:768])
    vec_c[c, 5:6] = column_sums(triple_grad[:, 1536:2304])

    def make_zero(first, i):
        left = normed[...]
        if i == 1:
            left = jnp.where(first >= 2304, attended[...], left)
        return block_grad(left, triple_grad[:, aligned(first, 768)])

    wire.drain()
    other_half(0, make_zero)
    for n in range(3):
        piece = matmul_nt(triple_grad[:, n * 768 : (n + 1) * 768], attn(n * 768, 768))
        part_sum[...] = piece if n == 0 else part_sum[...] + piece
    unit_one, inverse_one = normalized(tokens[...].astype(single))
    vec_c[c, 0:1] = jnp.sum(part_sum[...] * unit_one, 0, keepdims=True)
    vec_c[c, 1:2] = jnp.sum(part_sum[...], 0, keepdims=True)
    vec_swap = wire.send(vec_c.at[c], vec_c.at[c], sibling)
    input_grad[...] = flow[...] + normalized_back(part_sum[...], unit_one, inverse_one, vec[0:1])
    own_half(0, make_zero)
    send_z = [wire.send(held.at[0, :, plus(z, k)], from_z[k - 1], peers_z(k)) for k in turns]
    vec_swap.wait_recv()
    vec_z[z] = vec_c[0] + vec_c[1]
    sent_vec_z = [wire.send(vec_z.at[z], vec_z.at[z], peers_z(k)) for k in turns]

    def add(base, parts):
        return base.astype(single) + sum(part.astype(single) for part in parts)

    await_all(send_y)
    quarter = aligned(y * 384, 384)
    for i in range(4):
        for j in range(4):
            total_y[i, j] = add(
                held[2, i, j, :, quarter], [from_y[k][i, j] for k in range(3)]
            ).astype(bfloat)
    down_send_x = [wire.send(total_y.at[plus(x, k)], down_x.at[k - 1], peers_x(k)) for k in turns]
    await_all(send_x)
    for i in range(4):
        total_x[i] = add(held[1, x, i], [from_x[k][i] for k in range(3)]).astype(bfloat)
    late_send_z = [wire.send(total_x.at[plus(z, k)], late_z.at[k - 1], peers_z(k)) for k in turns]
    await_all(sent_vec_z)
    vec_x[x] = vec_z[0] + vec_z[1] + vec_z[2] + vec_z[3]
    sent_vec_x = [wire.send(vec_x.at[x], vec_x.at[x], peers_x(k)) for k in turns]
    await_all(send_z)
    for i in range(4):
        total_z[i] = add(held[0, i, z], [from_z[k][i] for k in range(3)]).astype(bfloat)
    late_send_x = [wire.send(total_z.at[plus(x, k)], late_x.at[k - 1], peers_x(k)) for k in turns]
    await_all(down_send_x)
    for j in range(4):
        last[j] = add(total_y[x, j], [down_x[k, j] for k in range(3)]).astype(bfloat)
    down_send_z = [wire.send(last.at[plus(z, k)], down_z.at[k - 1], peers_z(k)) for k in turns]
    await_all(sent_vec_x)
    vec_y[y] = vec_x[0] + vec_x[1] + vec_x[2] + vec_x[3]
    sent_vec_y = [wire.send(vec_y.at[y], vec_y.at[y], peers_y(k)) for k in turns]
    await_all(late_send_z)
    whole[1] = add(total_x[z], [late_z[k] for k in range(3)])
    await_all(late_send_x)
    whole[0] = add(total_z[x], [late_x[k] for k in range(3)])
    for m in range(2):
        for j in range(12):
            flat[m, pl.ds(j, 48, stride=12), :] = whole[m, :, j * 128 : (j + 1) * 128]
    await_all(down_send_z)
    ended = add(last[z], [down_z[k] for k in range(3)])
    for j in range(3):
        third[pl.ds(j, 48, stride=3), :] = ended[:, j * 128 : (j + 1) * 128]
    packed[160:176] = jnp.zeros((16, 128), single)
    for s in range(8):
        packed[0:72] = flat[0, s * 72 : (s + 1) * 72]
        packed[72:144] = flat[1, s * 72 : (s + 1) * 72]
        packed[144:162] = third[s * 18 : (s + 1) * 18]
        pieces[s // 2, s % 2] = packed[...].astype(bfloat)
    landed[y, c] = pieces[y, c]
    piece_sent = [
        wire.send(pieces.at[plus(y, k), lax.rem(c + d, 2)], landed.at[y, c], group_peer(k, d))
        for k, d in group
    ]
    await_all(sent_vec_y)
    vec_total = vec_y[0] + vec_y[1] + vec_y[2] + vec_y[3]
    vector_out[...] = vec_total
    await_all(piece_sent)
    for h in range(2):
        for k in range(4):
            piece = landed[k, h].astype(single)
            packed[...] = piece if k == 0 else packed[...] + piece
            sums[...] = piece[144:168]
            for j in range(3):
                at = ((h * 4 + k) * 3 + j) * 128
                mlp_out[1, :, at : at + 128] = sums[pl.ds(j, 6, stride=3), :]
        for j in range(12):
            at = (h * 12 + j) * 128
            attn_out[:, at : at + 128] = packed[pl.ds(j, 6, stride=12), :]
            mlp_out[0, :, at : at + 128] = packed[pl.ds(72 + j, 6, stride=12), :]
    lanes = lax.broadcasted_iota(jnp.int32, (16, 768), 1)
    start = lax.axis_index("dp") * 6
    owned = jnp.where((lanes >= start) & (lanes < start + 6), vec_total, 0.0)
    squares = sum_squares((attn_out[...], mlp_out[0], mlp_out[1], owned))
    square[...] = jnp.broadcast_to(squares, (8, 128))
    near[y, c] = square[...]
    sent = [wire.send(square, near.at[y, c], group_peer(*g)) for g in group]
    await_all(sent)
    far[x, z] = sum(near[k, d] for k in range(4) for d in range(2))
    sent = [wire.send(far.at[x, z], far.at[x, z], plane_peer(*p)) for p in plane]
    await_all(sent)
    square_out[...] = sum(far[i, j] for i in range(4) for j in range(4))
    wire.drain()


def train_step(
    lengths, text, images, image_attn, image_mlp, image_vectors, attn_master, mlp_master, vector_master
):
    copies = 256
    vmem = pl.BlockSpec(memory_space=pltpu.VMEM)
    anywhere = pl.BlockSpec(memory_space=pl.ANY)
    vector_lines = jnp.pad(vector_master.T, ((0, 10), (0, 116))).astype(bfloat)
    return pl.pallas_call(
        step_kernel,
        out_shape=(
            jax.ShapeDtypeStruct((384, 768), single),
            jax.ShapeDtypeStruct((6, 3072), single),
            jax.ShapeDtypeStruct((2, 6, 3072), single),
            jax.ShapeDtypeStruct((16, 768), single),
            jax.ShapeDtypeStruct((8, 128), single),
        ),
        in_specs=[pl.BlockSpec(memory_space=pltpu.SMEM)] + [anywhere] * 4 + [vmem] * 4,
        out_specs=[vmem] * 5,
        scratch_shapes=[
            pltpu.VMEM((3, 4, 4, 48, 3072), bfloat),
            pltpu.VMEM((3, 4, 4, 48, 3072), bfloat),
            pltpu.VMEM((384, 768), bfloat),
            pltpu.VMEM((3, 128, 128), single),
            pltpu.VMEM((4, 112, 112), single),
            pltpu.VMEM((24, 768), single),
            pltpu.VMEM((4608, 128), single),
            pltpu.VMEM((400, 768), bfloat),
            pltpu.VMEM((400, 2304), bfloat),
            pltpu.VMEM((400, 768), bfloat),
            pltpu.VMEM((400, 768), single),
            pltpu.VMEM((384, 768), bfloat),
            pltpu.VMEM((384, 3072), bfloat),
            pltpu.VMEM((400, 3072), bfloat),
            pltpu.VMEM((384, 3072), bfloat),
            pltpu.VMEM((384, 768), single),
            pltpu.VMEM((384, 768), single),
            pltpu.VMEM((4, 4, 4, 48, 768), bfloat),
            pltpu.VMEM((2, 24, 768), single),
            pltpu.VMEM((2, 4, SHARD, 128), bfloat),
            pltpu.VMEM((48, 128), single),
            pltpu.VMEM((4, 4, 48, 128), bfloat),
            pltpu.VMEM((16, 768), single),
            pltpu.VMEM((8, 384), single),
            pltpu.VMEM((4, 2, 8, 384), single),
            pltpu.VMEM((4, 4, 8, 384), single),
            pltpu.VMEM((3, 48, 1536), bfloat),
            pltpu.VMEM((3, 48, 1536), bfloat),
            pltpu.VMEM((3, 4, 48, 384), bfloat),
            pltpu.VMEM((3, 48, 384), bfloat),
            pltpu.VMEM((2, 48, 1536), single),
            pltpu.VMEM((4, 48, 384), bfloat),
            pltpu.VMEM((2, 576, 128), single),
            pltpu.VMEM((144, 128), single),
            pltpu.VMEM((176, 128), single),
            pltpu.VMEM((4, 2, 176, 128), bfloat),
            pltpu.VMEM((4, 2, 176, 128), bfloat),
            pltpu.VMEM((24, 128), single),
            pltpu.VMEM((2, 16, 768), single),
            pltpu.VMEM((4, 16, 768), single),
            pltpu.VMEM((4, 16, 768), single),
            pltpu.VMEM((4, 16, 768), single),
            pltpu.VMEM((8, 128), single),
            pltpu.VMEM((4, 2, 8, 128), single),
            pltpu.VMEM((4, 4, 8, 128), single),
            pltpu.SemaphoreType.DMA((6,)),
            pltpu.SemaphoreType.DMA((copies,)),
            pltpu.SemaphoreType.DMA((copies,)),
        ],
        compiler_params=pltpu.CompilerParams(
            collective_id=1, has_side_effects=True, vmem_limit_bytes=63 * 2**20
        ),
        name="train_step",
    )(
        lengths,
        text,
        images,
        image_attn.reshape(4, 4, 48, 3072),
        image_mlp.reshape(2, 4, 4, 48, 3072),
        image_vectors,
        attn_master,
        mlp_master,
        vector_lines,
    )


def shards(
    text_input,
    caption_lengths,
    image_tokens,
    image_attn,
    image_mlp,
    image_vectors,
    attn_master,
    mlp_master,
    vector_master,
    attn_first,
    mlp_first,
    vector_first,
    attn_second,
    mlp_second,
    vector_second,
):
    input_grad, attn_sum, mlp_sum, vector_all, square_total = train_step(
        caption_lengths,
        text_input,
        image_tokens,
        image_attn,
        image_mlp,
        image_vectors,
        attn_master,
        mlp_master,
        vector_master,
    )
    start = lax.axis_index("dp") * 6
    vector_sum = lax.dynamic_slice_in_dim(vector_all[:12], start, 6, 1)
    grad_norm = jnp.sqrt(square_total[0, 0])
    factor = jnp.minimum(1.0, clip_norm / (grad_norm + 1e-06))
    attn_state = adam_update(
        attn_master, attn_sum, attn_first, attn_second, factor, learn_rate, weight_decay
    )
    mlp_state = adam_update(
        mlp_master, mlp_sum, mlp_first, mlp_second, factor, learn_rate, weight_decay
    )
    vector_state = adam_update(
        vector_master, vector_sum, vector_first, vector_second, factor, vector_rate, 0.0
    )
    return (
        input_grad,
        grad_norm,
        attn_sum,
        mlp_sum,
        vector_sum,
        attn_state[0],
        mlp_state[0],
        vector_state[0],
        attn_state[1],
        mlp_state[1],
        vector_state[1],
        attn_state[2],
        mlp_state[2],
        vector_state[2],
    )


def solution(mesh):
    in_specs = (
        P("dp", None),
        P("dp", None),
        P("dp", None),
        P(),
        P(),
        P(),
        P("dp", None),
        P(None, "dp", None),
        P(None, "dp"),
        P("dp", None),
        P(None, "dp", None),
        P(None, "dp"),
        P("dp", None),
        P(None, "dp", None),
        P(None, "dp"),
    )
    out_specs = (
        P("dp", None),
        P(),
        P("dp", None),
        P(None, "dp", None),
        P(None, "dp"),
        P("dp", None),
        P(None, "dp", None),
        P(None, "dp"),
        P("dp", None),
        P(None, "dp", None),
        P(None, "dp"),
        P("dp", None),
        P(None, "dp", None),
        P(None, "dp"),
    )
    return jax.shard_map(shards, mesh=mesh, in_specs=in_specs, out_specs=out_specs, check_vma=False)
```

```python
import jax
import jax.numpy as jnp
from jax import lax
from jax.experimental import pallas as pl
from jax.experimental.pallas import tpu as pltpu
from jax.sharding import PartitionSpec as P

STEP = 10


logit_scale = 60.0
clip_norm = 0.01
learn_rate = 0.05
vector_rate = 0.3
beta_first = 0.9
beta_second = 0.999
adam_epsilon = 1e-08
weight_decay = 0.1
bfloat = jnp.bfloat16
single = jnp.float32


def unit_rows(values):
    return values * lax.rsqrt(jnp.sum(values * values, -1, keepdims=True) + 1e-06)


def sum_squares(arrays):
    return sum((jnp.sum(member * member) for member in arrays))


def adam_update(weight, gradient, first_moment, second_moment, factor, rate, decay_rate):
    clipped = gradient * factor
    first_new = beta_first * first_moment + (1.0 - beta_first) * clipped
    second_new = beta_second * second_moment + (1.0 - beta_second) * clipped * clipped
    ratio = (
        first_new
        / (1.0 - beta_first**STEP)
        / (jnp.sqrt(second_new / (1.0 - beta_second**STEP)) + adam_epsilon)
    )
    return (first_new, second_new, weight - rate * (ratio + decay_rate * weight))


MESH = pl.DeviceIdType.MESH
LINES = 144
SHARD = 448
SUM_COPIES = 80
TURNS = (1, 3, 2)


def place():
    me = lax.axis_index("dp")
    return (me // 32, lax.rem(me // 8, 4), lax.rem(me // 2, 4), lax.rem(me, 2))


def device(x, z, y, c):
    return ((x * 4 + z) * 4 + y) * 2 + c


def plus(index, step):
    return lax.rem(index + step, 4)


def made(item):
    return item() if callable(item) else item


class Copy:
    def __init__(self, wire, slot, source, target, to):
        self.wire, self.slot, self.parts = (wire, slot, (source, target, to))

    def make(self):
        source, target, to = (made(part) for part in self.parts)
        return pltpu.make_async_remote_copy(
            src_ref=source,
            dst_ref=target,
            send_sem=self.wire.send_sems.at[self.slot],
            recv_sem=self.wire.recv_sems.at[self.slot],
            device_id=(to,),
            device_id_type=MESH,
        )

    def wait_recv(self):
        self.make().wait_recv()

    def wait_send(self):
        self.make().wait_send()


class Wire:
    def __init__(self, send_sems, recv_sems):
        self.send_sems, self.recv_sems, self.count, self.open = (send_sems, recv_sems, 0, [])

    def send(self, source, target, to):
        copy = Copy(self, self.count, source, target, to)
        copy.make().start()
        self.count += 1
        self.open.append(copy)
        return copy

    def clear(self, copies):
        for copy in copies:
            copy.wait_send()
        self.open = [copy for copy in self.open if not any(copy is other for other in copies)]

    def drain(self):
        self.clear(self.open)


def await_all(copies):
    for copy in copies:
        copy.wait_recv()


def greet(peers):
    for peer in peers:
        pl.semaphore_signal(
            pltpu.get_barrier_semaphore(), inc=1, device_id=(peer,), device_id_type=MESH
        )


def greeted(peers):
    pl.semaphore_wait(pltpu.get_barrier_semaphore(), len(peers))


class Ring:
    def __init__(self, wire, peer, view):
        self.wire, self.peer, self.view = (wire, peer, view)
        self.ahead = self.pass_on(0, None, 1)
        self.behind = self.pass_on(0, None, 3)

    def pass_on(self, k, part, step):
        block = lambda: self.view(k, part)
        return self.wire.send(block, block, lambda: self.peer(step))

    def forward(self):
        self.ahead.wait_recv()
        self.low = self.pass_on(3, 0, 1)
        self.behind.wait_recv()
        self.high = self.pass_on(1, 1, 3)

    def finish(self):
        self.low.wait_recv()
        self.high.wait_recv()


def aligned(start, size):
    return pl.ds(pl.multiple_of(start, 128), size)


def halves(start, size, part):
    if part is None:
        return aligned(start, size)
    low = size // 256 * 128
    return aligned(start, low) if part == 0 else aligned(start + low, size - low)


class Gather:
    def __init__(self, wire, peers, here, weight, turned, lines, natural, small):
        self.wire, self.here, self.weight, self.turned = (wire, here, weight, turned)
        self.lines, self.natural, self.small = (lines, natural, small)
        self.peers_x, self.peers_z, self.peers_y, self.sibling = peers
        x, z, y, c = here
        self.half, self.quarter = (c * 1536, (c * 4 + y) * 384)
        self.across = ([], [], [])

    def span(self, m):
        return (pl.ds(0, 160), pl.ds(160, 144), pl.ds(304, 144))[m]

    def begin(self):
        x, z, y, c = self.here
        self.first = {}
        for m in (2, 0, 1):
            view = lambda m=m: self.lines.at[c, y, self.span(m)]
            self.first[m] = [self.wire.send(view, view, lambda k=k: self.peers_y(k)) for k in TURNS]

    def swap(self):
        x, z, y, c = self.here
        self.swaps = {}
        for m in (2, 0, 1):
            await_all(self.first[m])
            view = lambda m=m: self.lines.at[c, :, self.span(m)]
            self.swaps[m] = self.wire.send(view, view, self.sibling)

    def spread(self, m):
        x, z, y, c = self.here
        self.swaps[m].wait_recv()
        for s in range(8):
            self.natural[s * LINES : (s + 1) * LINES] = self.lines[
                s % 2, s // 2, 16 + m * LINES : 16 + (m + 1) * LINES
            ].astype(single)
        start, count = (c * 12, 12) if m < 2 else ((c * 4 + y) * 3, 3)
        for j in range(count):
            self.weight[m, x, z, :, aligned((start + j) * 128, 128)] = self.natural[
                pl.ds(start + j, 48, stride=24), :
            ].astype(bfloat)

    def ring(self, peer, view):
        return Ring(self.wire, peer, view)

    def attn_x(self):
        x, z, y, c = self.here
        return self.ring(
            self.peers_x,
            lambda k, part: self.weight.at[0, plus(x, k), z, :, halves(self.half, 1536, part)],
        )

    def attn_z(self, b):
        x, z, y, c = self.here
        return self.ring(
            self.peers_z,
            lambda k, part: self.weight.at[
                0, plus(x, b), plus(z, k), :, halves(self.half, 1536, part)
            ],
        )

    def up_z(self):
        x, z, y, c = self.here
        return self.ring(
            self.peers_z,
            lambda k, part: self.weight.at[1, x, plus(z, k), :, halves(self.half, 1536, part)],
        )

    def up_x(self, b):
        x, z, y, c = self.here
        return self.ring(
            self.peers_x,
            lambda k, part: self.weight.at[
                1, plus(x, k), plus(z, b), :, halves(self.half, 1536, part)
            ],
        )

    def down_x(self):
        x, z, y, c = self.here
        return self.ring(
            self.peers_x,
            lambda k, part: self.weight.at[2, plus(x, k), z, :, halves(self.quarter, 384, part)],
        )

    def down_z(self, b):
        x, z, y, c = self.here
        return self.ring(
            self.peers_z,
            lambda k, part: self.weight.at[
                2, plus(x, b), plus(z, k), :, halves(self.quarter, 384, part)
            ],
        )

    def down_y(self, b):
        x, z, y, c = self.here
        return self.ring(
            self.peers_y,
            lambda k, part: self.weight.at[
                2, plus(x, b), :, :, halves((c * 4 + plus(y, k)) * 384, 384, part)
            ],
        )

    def spread_all(self):
        x, z, y, c = self.here
        self.spread(2)
        self.c1 = self.down_x()
        self.c2 = {0: self.down_z(0)}
        self.spread(0)
        self.a1 = self.attn_x()
        self.spread(1)
        self.b1 = self.up_z()
        for s in range(8):
            self.small[s * 6 : (s + 1) * 6] = self.lines[s % 2, s // 2, 0:16].astype(single)[0:6]
        self.turned[x, z] = self.small[...].astype(bfloat)
        view = lambda: self.turned.at[x, z]
        self.turn_x = [self.wire.send(view, view, lambda k=k: self.peers_x(k)) for k in TURNS]

    def nearest(self):
        self.c1.forward()
        for b in (3, 1):
            self.c2[b] = self.down_z(b)
        self.a1.forward()
        self.b1.forward()
        self.c2[0].forward()
        self.a2 = {0: self.attn_z(0)}
        self.b2 = {0: self.up_x(0)}

    def farthest(self):
        self.c1.finish()
        self.c2[2] = self.down_z(2)
        self.c2[0].finish()
        self.c3 = {0: self.down_y(0)}
        for b in (3, 1):
            self.c2[b].forward()
        for b in (3, 1):
            self.a2[b] = self.attn_z(b)
            self.b2[b] = self.up_x(b)
        x, z, y, c = self.here
        await_all(self.turn_x)
        view = lambda: self.turned.at[:, z]
        self.turn_z = [self.wire.send(view, view, lambda k=k: self.peers_z(k)) for k in TURNS]

    def second_own(self):
        for b in (3, 1):
            self.c2[b].finish()
            self.c3[b] = self.down_y(b)
        self.c2[2].forward()
        self.a1.finish()
        self.a2[2] = self.attn_z(2)
        self.b1.finish()
        self.b2[2] = self.up_x(2)
        self.a2[0].forward()
        self.b2[0].forward()

    def second_near(self):
        self.c3[0].forward()
        self.c2[2].finish()
        self.c3[2] = self.down_y(2)
        for b in (3, 1):
            self.a2[b].forward()
            self.b2[b].forward()
        self.finish_attn(0)
        self.finish_up(0)

    def third_near(self):
        for b in (3, 1):
            self.c3[b].forward()
        self.finish_down(0)
        for b in (3, 1):
            self.finish_attn(b)
            self.finish_up(b)

    def second_far(self):
        self.a2[2].forward()
        self.b2[2].forward()
        self.c3[2].forward()
        for b in (3, 1):
            self.finish_down(b)

    def finish_attn(self, b):
        x, z, y, c = self.here
        self.a2[b].finish()
        self.cross(0, lambda: self.weight.at[0, plus(x, b), :, :, aligned(self.half, 1536)])

    def finish_up(self, b):
        x, z, y, c = self.here
        self.b2[b].finish()
        self.cross(1, lambda: self.weight.at[1, :, plus(z, b), :, aligned(self.half, 1536)])

    def finish_down(self, b):
        x, z, y, c = self.here
        self.c3[b].finish()
        self.cross(2, lambda: self.weight.at[2, plus(x, b), :, :, aligned(self.half, 1536)])

    def cross(self, m, view):
        self.across[m].append(self.wire.send(view, view, self.sibling))

    def end(self, m):
        await_all(self.across[m])


def matmul(left, right):
    return jnp.dot(left, right, preferred_element_type=single)


def matmul_nt(left, right):
    return lax.dot_general(left, right, (((1,), (1,)), ((), ())), preferred_element_type=single)


def matmul_tn(left, right):
    return lax.dot_general(left, right, (((0,), (0,)), ((), ())), preferred_element_type=single)


def normalized(values):
    center = jnp.mean(values, -1, keepdims=True)
    shifted = values - center
    spread = jnp.mean(shifted * shifted, -1, keepdims=True)
    inverse = lax.rsqrt(spread + 1e-06)
    return (shifted * inverse, inverse)


def normalized_back(cotangent, unit, inverse, gain):
    scaled = cotangent * gain
    center = jnp.mean(scaled, -1, keepdims=True)
    along = jnp.mean(scaled * unit, -1, keepdims=True)
    return inverse * (scaled - center - unit * along)


def gelu_parts(hidden):
    squared = hidden * hidden
    angle = jnp.tanh(hidden * (0.7978845608028654 + 0.035677408136300125 * squared))
    return (squared, angle)


def even_lanes(rows):
    return lax.broadcasted_iota(jnp.int32, (rows, 128), 1) < 64


def split_heads(values):
    even = even_lanes(values.shape[0])
    zero = jnp.zeros_like(values)
    return jnp.concatenate([jnp.where(even, values, zero), jnp.where(even, zero, values)], 0)


def join_heads(values):
    rows = values.shape[0] // 2
    return jnp.where(even_lanes(rows), values[:rows], values[rows:])


def pair_weights(queries, key_rows, bias):
    scores = matmul_nt(split_heads(queries * 0.125), key_rows)
    scores = scores + jnp.concatenate([bias, bias], 0)
    weights = jnp.exp(scores - jnp.max(scores, -1, keepdims=True))
    return (weights, 1.0 / jnp.sum(weights, -1, keepdims=True))


def attend_images(qkv, attended, bias):
    starts = (0, 96, 192, 288)
    rows = lax.broadcasted_iota(jnp.int32, (16, 128), 0)

    @pl.loop(0, 6, unroll=3)
    def _(p):
        out = []
        for w, start in enumerate(starts):
            window = slice(start, start + 112)
            weights, scale = pair_weights(
                qkv[window, aligned(p * 128, 128)], qkv[window, aligned((6 + p) * 128, 128)], bias[w]
            )
            values = qkv[window, aligned((12 + p) * 128, 128)]
            out.append(join_heads(matmul(weights.astype(bfloat), values) * scale))
        lanes = aligned(p * 128, 128)
        attended[0:96, lanes] = out[0][0:96].astype(bfloat)
        for w in range(1, 4):
            edge = jnp.where(rows < 4 * w, out[w - 1][96:112], out[w][0:16])
            attended[starts[w] : starts[w] + 16, lanes] = edge.astype(bfloat)
            stop = 112 if w == 3 else 96
            attended[starts[w] + 16 : starts[w] + stop, lanes] = out[w][16:stop].astype(bfloat)


class UnitGather:
    def __init__(self, wire, peers, here, units, own, images, first, count):
        self.wire, self.here, self.units, self.own, self.images = (wire, here, units, own, images)
        self.peers_x, self.peers_z, self.peers_y, self.sibling = peers
        self.first, self.count, self.step = (first, count, 0)

    def swap(self):
        c = self.here[3]
        rows = pl.ds(self.first, self.count)
        self.own[c, rows] = self.units[rows, :]
        self.swapped = self.wire.send(self.own.at[c, rows], self.own.at[c, rows], self.sibling)

    def begin(self):
        x, z, y, c = self.here
        self.swapped.wait_recv()
        lanes = aligned(c * 384, 384)
        for first in range(self.first, self.first + self.count, 8):
            both = [self.own[core, first : first + 8, lanes] for core in range(2)]
            self.images[x, z, y, 2 * first : 2 * first + 16, lanes] = jnp.concatenate(both, 0).astype(
                bfloat
            )
        self.start()

    def start(self):
        x, z, y, c = self.here
        here = {"x": x, "z": z, "y": y}
        peer = {"x": self.peers_x, "z": self.peers_z, "y": self.peers_y}
        rows = pl.ds(2 * self.first, 2 * self.count)
        self.sent = []
        for o, order in enumerate(("yzx", "zxy", "xyz")):
            index = [slice(None) if n in order[: self.step] else here[n] for n in "xzy"]
            view = self.images.at[(*index, rows, aligned((c * 3 + o) * 128, 128))]
            self.sent += [self.wire.send(view, view, peer[order[self.step]](k)) for k in TURNS]
        self.step += 1

    def next(self):
        await_all(self.sent)
        self.start()

    def finish(self):
        await_all(self.sent)
        rows = pl.ds(2 * self.first, 2 * self.count)
        mine = self.images.at[:, :, :, rows, aligned(self.here[3] * 384, 384)]
        self.crossed = self.wire.send(mine, mine, self.sibling)

    def end(self):
        self.crossed.wait_recv()


def image_bias(bias):
    for w in range(4):
        first = 96 * w
        query = (lax.broadcasted_iota(jnp.int32, (112, 112), 0) + first) // 50
        key = (lax.broadcasted_iota(jnp.int32, (112, 112), 1) + first) // 50
        bias[w] = jnp.where(query == key, 0.0, -1e30)


def image_chunk(t, tokens, weight, vec, normed, qkv, attended, residual, bias, units, hook):
    lanes_t = slice(t * 768, (t + 1) * 768)
    unit, _ = normalized(tokens[:, lanes_t].astype(single))
    normed[...] = (unit * vec[0:1] + vec[1:2]).astype(bfloat)
    hook()
    for n, shift in enumerate((4, None, 5)):
        triple = matmul(normed[...], weight(0, n * 768, 768))
        if shift is not None:
            triple = triple + vec[shift : shift + 1]
        qkv[:, n * 768 : (n + 1) * 768] = triple.astype(bfloat)
    hook()
    attend_images(qkv, attended, bias)
    hook()
    residual[...] = (
        tokens[:, lanes_t].astype(single) + matmul(attended[...], weight(0, 2304, 768)) + vec[6:7]
    )
    unit, _ = normalized(residual[...])
    normed[...] = (unit * vec[2:3] + vec[3:4]).astype(bfloat)
    residual[...] = residual[...] + vec[7:8]
    hook()
    for f in range(4):
        hidden = matmul(normed[...], weight(1, f * 768, 768)) + vec[8 + f : 9 + f]
        _, angle = gelu_parts(hidden)
        active = (0.5 * hidden * (1.0 + angle)).astype(bfloat)
        residual[...] = residual[...] + matmul_nt(active, weight(2, f * 768, 768))
        hook()
    image = lax.broadcasted_iota(jnp.int32, (8, 400), 0)
    token = lax.broadcasted_iota(jnp.int32, (8, 400), 1)
    member = (token // 50 == image).astype(bfloat)
    high = residual[...].astype(bfloat)
    low = (residual[...] - high.astype(single)).astype(bfloat)
    pooled = (matmul(member, high) + matmul(member, low)) * (1.0 / 50.0)
    units[t * 8 : (t + 1) * 8, :] = unit_rows(pooled)


PLAN = {
    (0, 2): "swap",
    (0, 4): "spread_all",
    (0, 6): "nearest",
    (1, 0): "farthest",
    (1, 2): "second_own",
    (1, 5): "second_near",
    (2, 2): "third_near",
    (2, 6): "second_far",
}


def slot_codes(index, ends, window):
    later = index >= 64
    position = jnp.where(later, index - 64, index)
    slots = [
        sum((position >= ends[2 * window + r][k]).astype(jnp.int32) for k in range(4)) for r in (0, 1)
    ]
    return jnp.where(later, slots[1] + 8, slots[0])


def text_masks(lengths, bias):
    ends = []
    for r in range(6):
        row, end = ([], 0)
        for k in range(4):
            end = end + lengths[k, r]
            row.append(end)
        ends.append(row)
    codes = []
    for w in range(3):
        query = slot_codes(lax.broadcasted_iota(jnp.int32, (128, 128), 0), ends, w)
        key = slot_codes(lax.broadcasted_iota(jnp.int32, (128, 128), 1), ends, w)
        bias[w] = jnp.where(query == key, 0.0, -1e30)
        code = slot_codes(lax.broadcasted_iota(jnp.int32, (24, 128), 1), ends, w)
        slot = jnp.where(code >= 8, code - 8, code)
        caption = 8 * w + jnp.where(code >= 8, 4, 0) + slot
        codes.append(jnp.where(slot < 4, caption, -1))
    caption = jnp.concatenate(codes, 1)
    return (caption == lax.broadcasted_iota(jnp.int32, (24, 384), 0)).astype(single)


def attend_text(qkv, attended, probs, bias):
    @pl.loop(0, 6, unroll=3)
    def _(p):
        for w in range(3):
            window = slice(w * 128, (w + 1) * 128)
            weights, scale = pair_weights(
                qkv[window, aligned(p * 128, 128)], qkv[window, aligned((6 + p) * 128, 128)], bias[w]
            )
            pair = weights * scale
            probs[pl.ds(pl.multiple_of((p * 3 + w) * 256, 256), 256)] = pair
            out = matmul(pair.astype(bfloat), qkv[window, aligned((12 + p) * 128, 128)])
            attended[window, aligned(p * 128, 128)] = join_heads(out).astype(bfloat)


def attend_text_back(qkv, probs, attended_grad, triple_grad):
    @pl.loop(0, 6, unroll=3)
    def _(p):
        for w in range(3):
            window = slice(w * 128, (w + 1) * 128)
            at = [aligned((6 * n + p) * 128, 128) for n in range(3)]
            queries, key_rows, value_rows = (qkv[window, lanes] for lanes in at)
            grads = split_heads(attended_grad[window, at[0]])
            pair = probs[pl.ds(pl.multiple_of((p * 3 + w) * 256, 256), 256)]
            value_grad = matmul_tn(pair.astype(bfloat), grads)
            prob_grad = matmul_nt(grads, value_rows)
            along = jnp.sum(pair * prob_grad, -1, keepdims=True)
            score_grad = (pair * (prob_grad - along) * 0.125).astype(bfloat)
            query_grad = join_heads(matmul(score_grad, key_rows))
            key_grad = matmul_tn(score_grad, split_heads(queries))
            triple_grad[window, at[0]] = query_grad.astype(bfloat)
            triple_grad[window, at[1]] = key_grad.astype(bfloat)
            triple_grad[window, at[2]] = value_grad.astype(bfloat)


def column_sums(values):
    return jnp.sum(values.astype(single), 0, keepdims=True)


def step_kernel(
    lengths,
    tokens_ref,
    image_ref,
    image_attn_ref,
    image_mlp_ref,
    image_vec,
    attn_ref,
    mlp_ref,
    vector_ref,
    input_grad,
    attn_out,
    mlp_out,
    vector_out,
    square_out,
    weight,
    store,
    tokens,
    bias,
    image_masks,
    units,
    probs,
    normed,
    qkv,
    attended,
    residual,
    normed_two,
    active,
    slope,
    triple_grad,
    flow,
    part_sum,
    images,
    own,
    lines,
    small,
    turned,
    vec,
    row_part,
    row_near,
    row_far,
    late_x,
    late_z,
    down_x,
    down_z,
    whole,
    last,
    flat,
    third,
    packed,
    pieces,
    landed,
    sums,
    vec_c,
    vec_z,
    vec_x,
    vec_y,
    square,
    near,
    far,
    load_sems,
    send_sems,
    recv_sems,
):
    x, z, y, c = place()
    peers_x = lambda k: device(plus(x, k), z, y, c)
    peers_z = lambda k: device(x, plus(z, k), y, c)
    peers_y = lambda k: device(x, z, plus(y, k), c)
    sibling = device(x, z, y, 1 - c)
    group = [(k, d) for k in range(4) for d in range(2) if (k, d) != (0, 0)]
    plane = [(i, j) for i in range(4) for j in range(4) if (i, j) != (0, 0)]
    group_peer = lambda k, d: device(x, z, plus(y, k), lax.rem(c + d, 2))
    plane_peer = lambda i, j: device(plus(x, i), plus(z, j), y, c)
    wire = Wire(send_sems, recv_sems)
    turns = TURNS

    held = store.at[:, :, :, :, 0:1536]
    low, high = (slice(0, 768), slice(768, 1536))
    from_z = [[store.at[m, k, :, :, 1536:2304] for k in range(3)] for m in range(2)]
    from_x = [[store.at[m, k, :, :, 2304:3072] for k in range(3)] for m in range(2)]
    from_y = [store.at[2, :, :, :, 1536 + 384 * k : 1920 + 384 * k] for k in range(3)]
    total_z = [store.at[m, 3, :, :, 1536:2304] for m in range(2)]
    total_x = [store.at[m, 3, :, :, 2304:3072] for m in range(2)]
    total_y = store.at[2, :, :, :, 2688:3072]

    loads = [
        pltpu.make_async_copy(source, target, load_sems.at[n])
        for n, (source, target) in enumerate(
            [
                (image_ref.at[0:400], slope.at[:, 0:768]),
                (image_attn_ref, store.at[0]),
                (image_mlp_ref, store.at[1:3]),
                (image_ref.at[400:800], slope.at[:, 768:1536]),
                (image_ref.at[800:1200], slope.at[:, 1536:2304]),
                (tokens_ref, tokens),
            ]
        )
    ]
    for load in loads:
        load.start()
    others = [group_peer(*g) for g in group] + [plane_peer(*p) for p in plane]
    greet(others)
    natural, line = (probs.at[0:1152], [probs.at[1152 + 144 * m : 1296 + 144 * m] for m in range(3)])
    small[0:16] = jnp.zeros((16, 128), single)
    small[0:6, 0:12] = vector_ref[...]
    lines[c, y, 0:16] = small[0:16].astype(bfloat)
    for m in range(3):
        for j in range(24):
            columns = slice(j * 128, (j + 1) * 128)
            rows = attn_ref[:, columns] if m == 0 else mlp_ref[:, m - 1, columns]
            line[m][pl.ds(j, 6, stride=24), :] = rows
        lines[c, y, 16 + m * LINES : 16 + (m + 1) * LINES] = line[m][...].astype(bfloat)
    greeted(others)
    peers = (peers_x, peers_z, peers_y, sibling)
    unit_gather = UnitGather(wire, peers, (x, z, y, c), units, own, images, 0, 24)
    gather = Gather(
        wire, peers, (x, z, y, c), weight, turned, lines, natural, small
    )
    gather.begin()
    image_bias(image_masks)
    for load in loads:
        load.wait()
    plan = PLAN
    image_weight = lambda m, first, size: store[m, :, :, :, first : first + size].reshape(768, size)

    for t in range(3):
        points = iter(range(99))

        def hook():
            for name in plan.get((t, next(points)), "").split():
                getattr(gather, name)()

        image_chunk(
            t, slope, image_weight, image_vec, normed, qkv, attended, residual, image_masks, units, hook
        )

    unit_gather.swap()
    gather.finish_attn(2)
    gather.finish_up(2)
    member = text_masks(lengths, bias)
    unit_gather.begin()
    await_all(gather.turn_z)
    vec[...] = turned[...].reshape(768, 128).astype(single).T[0:16]

    normed, qkv, attended, residual, slope = (
        ref.at[0:384] for ref in (normed, qkv, attended, residual, slope)
    )
    unit_one, _ = normalized(tokens[...].astype(single))
    normed[...] = (unit_one * vec[0:1] + vec[1:2]).astype(bfloat)
    gather.end(0)
    attn = lambda first, size: weight[0, :, :, :, first : first + size].reshape(768, size)
    for n, shift in enumerate((4, None, 5)):
        triple = matmul(normed[...], attn(n * 768, 768))
        if shift is not None:
            triple = triple + vec[shift : shift + 1]
        qkv[:, n * 768 : (n + 1) * 768] = triple.astype(bfloat)
    unit_gather.next()
    gather.finish_down(2)
    attend_text(qkv, attended, probs, bias)
    residual[...] = tokens[...].astype(single) + matmul(attended[...], attn(2304, 768)) + vec[6:7]
    unit_two, _ = normalized(residual[...])
    normed_two[...] = (unit_two * vec[2:3] + vec[3:4]).astype(bfloat)
    unit_gather.next()
    gather.end(1)
    for f in range(4):
        lanes = slice(f * 768, (f + 1) * 768)
        hidden = matmul(normed_two[...], weight[1, :, :, :, lanes].reshape(768, 768)) + vec[8 + f : 9 + f]
        squared, angle = gelu_parts(hidden)
        active[:, lanes] = (0.5 * hidden * (1.0 + angle)).astype(bfloat)
        curve = 0.7978845608028654 + 0.10703222440890037 * squared
        slope[:, lanes] = (
            0.5 * (1.0 + angle) + 0.5 * hidden * (1.0 - angle * angle) * curve
        ).astype(bfloat)
    gather.end(2)
    unit_gather.finish()
    flow[...] = residual[...] + vec[7:8]
    for f in range(4):
        lanes = slice(f * 768, (f + 1) * 768)
        flow[...] = flow[...] + matmul_nt(
            active[:, lanes], weight[2, :, :, :, lanes].reshape(768, 768)
        )
    highest = lax.Precision.HIGHEST
    per_length = 1.0 / jnp.sum(member, -1, keepdims=True)
    pooled = per_length * jnp.dot(member, flow[...], precision=highest, preferred_element_type=single)

    scale = lax.rsqrt(jnp.sum(pooled * pooled, -1, keepdims=True) + 1e-06)
    unit = pooled * scale
    unit_gather.end()
    every = images[...].reshape(3072, 768)
    logits = logit_scale * matmul_nt(unit.astype(bfloat), every)
    powers = jnp.exp(logits)
    column = jnp.sum(powers, 1, keepdims=True)
    rows = jnp.sum(powers, 0, keepdims=True)
    for k in range(8):
        row_part[k : k + 1, :] = rows[:, k * 384 : (k + 1) * 384]
    row_near[y, c] = row_part[...]
    wire.count = max(wire.count, SUM_COPIES)
    sent = [wire.send(row_part, row_near.at[y, c], group_peer(*g)) for g in group]
    caption = lax.broadcasted_iota(jnp.int32, (24, 3072), 0) + lax.axis_index("dp") * 24
    at = lax.broadcasted_iota(jnp.int32, (24, 3072), 1)
    inside = at % 48
    image = at - inside + inside // 8 % 2 * 24 + inside // 16 * 8 + inside % 8
    same = (caption == image).astype(single)
    of_column = powers / column - 2.0 * same
    await_all(sent)
    row_far[x, z] = sum(row_near[k, d] for k in range(4) for d in range(2))
    sent = [wire.send(row_far.at[x, z], row_far.at[x, z], plane_peer(*p)) for p in plane]
    await_all(sent)
    total = sum(row_far[i, j] for i in range(4) for j in range(4))
    every_row = jnp.concatenate([total[k : k + 1] for k in range(8)], 1)
    logit_grad = (logit_scale / (2.0 * 3072) * (powers / every_row + of_column)).astype(bfloat)
    unit_grad = matmul(logit_grad, every)
    pooled_grad = scale * (unit_grad - unit * jnp.sum(unit * unit_grad, -1, keepdims=True))
    flow[...] = lax.dot_general(
        member,
        pooled_grad * per_length,
        (((0,), (0,)), ((), ())),
        precision=highest,
        preferred_element_type=single,
    )

    sends = {}

    def block_grad(left, right):
        return matmul_tn(left, right).reshape(4, 4, 48, right.shape[1])

    def other_half(m, make):
        for i in range(2):
            place_i = images.at[:, :, 2 * (m % 2) + i]
            place_i[...] = make((1 - c) * 1536 + i * 768, i).astype(bfloat)
            sends[m, i] = wire.send(
                place_i, held.at[m, :, :, :, i * 768 : (i + 1) * 768], sibling
            )

    def own_half(m, make):
        for i in range(2):
            sends[m, i].wait_recv()
            lanes = slice(i * 768, (i + 1) * 768)
            held[m, :, :, :, lanes] = (
                make(c * 1536 + i * 768, i) + held[m, :, :, :, lanes].astype(single)
            ).astype(bfloat)

    wire.drain()
    wire.count = 0

    def add(base, parts):
        return base.astype(single) + sum(part.astype(single) for part in parts)

    def first_sums(m):
        return [
            [wire.send(held.at[m, :, plus(z, k), :, low], from_z[m][k - 1], peers_z(k)) for k in turns],
            [wire.send(held.at[m, plus(x, k), :, :, high], from_x[m][k - 1], peers_x(k)) for k in turns],
        ]

    def second_sums(m, sent):
        await_all(sent[0])
        for i in range(4):
            total_z[m][i] = add(held[m, i, z, :, low], [from_z[m][k][i] for k in range(3)]).astype(bfloat)
        over_x = [
            wire.send(total_z[m].at[plus(x, k)], late_x.at[m, k - 1], peers_x(k)) for k in turns
        ]
        await_all(sent[1])
        for i in range(4):
            total_x[m][i] = add(held[m, x, i, :, high], [from_x[m][k][i] for k in range(3)]).astype(bfloat)
        over_z = [
            wire.send(total_x[m].at[plus(z, k)], late_z.at[m, k - 1], peers_z(k)) for k in turns
        ]
        return (over_x, over_z)

    def whole_sums(m, sent):
        await_all(sent[0])
        whole[m, :, low] = add(total_z[m][x], [late_x[m, k] for k in range(3)])
        await_all(sent[1])
        whole[m, :, high] = add(total_x[m][z], [late_z[m, k] for k in range(3)])
        for j in range(12):
            flat[m, pl.ds(j, 48, stride=12), :] = whole[m, :, j * 128 : (j + 1) * 128]

    branch_two = flow[...].astype(bfloat)
    vec_c[c] = jnp.zeros((16, 768), single)
    vec_c[c, 7:8] = column_sums(branch_two)
    make_two = lambda first, i: block_grad(flow[...].astype(bfloat), active[:, aligned(first, 768)])
    other_half(2, make_two)
    for f in range(4):
        lanes = slice(f * 768, (f + 1) * 768)
        active_grad = matmul(flow[...].astype(bfloat), weight[2, :, :, :, lanes].reshape(768, 768))
        hidden_grad = (active_grad * slope[:, lanes].astype(single)).astype(bfloat)
        slope[:, lanes] = hidden_grad
        vec_c[c, 8 + f : 9 + f] = column_sums(hidden_grad)
    make_one = lambda first, i: block_grad(normed_two[...], slope[:, aligned(first, 768)])
    other_half(1, make_one)
    for f in range(4):
        lanes = slice(f * 768, (f + 1) * 768)
        piece = matmul_nt(slope[:, lanes], weight[1, :, :, :, lanes].reshape(768, 768))
        part_sum[...] = piece if f == 0 else part_sum[...] + piece
    own_half(2, make_two)
    send_y = [
        wire.send(held.at[2, :, :, :, aligned(plus(y, k) * 384, 384)], from_y[k - 1], peers_y(k))
        for k in turns
    ]
    unit_two, inverse_two = normalized(residual[...])
    vec_c[c, 2:3] = jnp.sum(part_sum[...] * unit_two, 0, keepdims=True)
    vec_c[c, 3:4] = jnp.sum(part_sum[...], 0, keepdims=True)
    flow[...] = flow[...] + normalized_back(part_sum[...], unit_two, inverse_two, vec[2:3])
    triple_grad[:, 2304:3072] = flow[...].astype(bfloat)
    vec_c[c, 6:7] = column_sums(triple_grad[:, 2304:3072])
    own_half(1, make_one)
    send_one = first_sums(1)
    active[:, 0:768] = matmul_nt(triple_grad[:, 2304:3072], attn(2304, 768)).astype(bfloat)
    attend_text_back(qkv, probs, active, triple_grad)
    vec_c[c, 4:5] = column_sums(triple_grad[:, 0:768])
    vec_c[c, 5:6] = column_sums(triple_grad[:, 1536:2304])

    def make_zero(first, i):
        left = normed[...]
        if i == 1:
            left = jnp.where(first >= 2304, attended[...], left)
        return block_grad(left, triple_grad[:, aligned(first, 768)])

    wire.clear([sends[2, i] for i in range(2)])
    other_half(0, make_zero)
    for n in range(3):
        piece = matmul_nt(triple_grad[:, n * 768 : (n + 1) * 768], attn(n * 768, 768))
        part_sum[...] = piece if n == 0 else part_sum[...] + piece
    own_half(0, make_zero)
    send_zero = first_sums(0)
    unit_one, inverse_one = normalized(tokens[...].astype(single))
    vec_c[c, 0:1] = jnp.sum(part_sum[...] * unit_one, 0, keepdims=True)
    vec_c[c, 1:2] = jnp.sum(part_sum[...], 0, keepdims=True)
    vec_swap = wire.send(vec_c.at[c], vec_c.at[c], sibling)
    input_grad[...] = flow[...] + normalized_back(part_sum[...], unit_one, inverse_one, vec[0:1])
    second_one = second_sums(1, send_one)
    vec_swap.wait_recv()
    vec_z[z] = vec_c[0] + vec_c[1]
    sent_vec_z = [wire.send(vec_z.at[z], vec_z.at[z], peers_z(k)) for k in turns]

    await_all(send_y)
    quarter = aligned(y * 384, 384)
    for i in range(4):
        for j in range(4):
            total_y[i, j] = add(
                held[2, i, j, :, quarter], [from_y[k][i, j] for k in range(3)]
            ).astype(bfloat)
    down_send_x = [wire.send(total_y.at[plus(x, k)], down_x.at[k - 1], peers_x(k)) for k in turns]
    await_all(sent_vec_z)
    vec_x[x] = vec_z[0] + vec_z[1] + vec_z[2] + vec_z[3]
    sent_vec_x = [wire.send(vec_x.at[x], vec_x.at[x], peers_x(k)) for k in turns]
    second_zero = second_sums(0, send_zero)
    await_all(down_send_x)
    for j in range(4):
        last[j] = add(total_y[x, j], [down_x[k, j] for k in range(3)]).astype(bfloat)
    down_send_z = [wire.send(last.at[plus(z, k)], down_z.at[k - 1], peers_z(k)) for k in turns]
    await_all(sent_vec_x)
    vec_y[y] = vec_x[0] + vec_x[1] + vec_x[2] + vec_x[3]
    sent_vec_y = [wire.send(vec_y.at[y], vec_y.at[y], peers_y(k)) for k in turns]
    whole_sums(1, second_one)
    whole_sums(0, second_zero)
    await_all(down_send_z)
    ended = add(last[z], [down_z[k] for k in range(3)])
    for j in range(3):
        third[pl.ds(j, 48, stride=3), :] = ended[:, j * 128 : (j + 1) * 128]
    packed[160:176] = jnp.zeros((16, 128), single)
    for s in range(8):
        packed[0:72] = flat[0, s * 72 : (s + 1) * 72]
        packed[72:144] = flat[1, s * 72 : (s + 1) * 72]
        packed[144:162] = third[s * 18 : (s + 1) * 18]
        pieces[s // 2, s % 2] = packed[...].astype(bfloat)
    landed[y, c] = pieces[y, c]
    piece_sent = [
        wire.send(pieces.at[plus(y, k), lax.rem(c + d, 2)], landed.at[y, c], group_peer(k, d))
        for k, d in group
    ]
    await_all(sent_vec_y)
    vec_total = vec_y[0] + vec_y[1] + vec_y[2] + vec_y[3]
    vector_out[...] = vec_total
    await_all(piece_sent)
    for h in range(2):
        for k in range(4):
            piece = landed[k, h].astype(single)
            packed[...] = piece if k == 0 else packed[...] + piece
            sums[...] = piece[144:168]
            for j in range(3):
                at = ((h * 4 + k) * 3 + j) * 128
                mlp_out[:, 1, at : at + 128] = sums[pl.ds(j, 6, stride=3), :]
        for j in range(12):
            at = (h * 12 + j) * 128
            attn_out[:, at : at + 128] = packed[pl.ds(j, 6, stride=12), :]
            mlp_out[:, 0, at : at + 128] = packed[pl.ds(72 + j, 6, stride=12), :]
    lanes = lax.broadcasted_iota(jnp.int32, (16, 768), 1)
    start = lax.axis_index("dp") * 6
    owned = jnp.where((lanes >= start) & (lanes < start + 6), vec_total, 0.0)
    squares = sum_squares((attn_out[...], mlp_out[...], owned))
    square[...] = jnp.broadcast_to(squares, (8, 128))
    near[y, c] = square[...]
    sent = [wire.send(square, near.at[y, c], group_peer(*g)) for g in group]
    await_all(sent)
    far[x, z] = sum(near[k, d] for k in range(4) for d in range(2))
    sent = [wire.send(far.at[x, z], far.at[x, z], plane_peer(*p)) for p in plane]
    await_all(sent)
    square_out[...] = sum(far[i, j] for i in range(4) for j in range(4))
    wire.drain()


def train_step(
    lengths, text, images, image_attn, image_mlp, image_vectors, attn_master, mlp_master, vector_master
):
    copies = 176
    vmem = pl.BlockSpec(memory_space=pltpu.VMEM)
    anywhere = pl.BlockSpec(memory_space=pl.ANY)
    return pl.pallas_call(
        step_kernel,
        out_shape=(
            jax.ShapeDtypeStruct((384, 768), single),
            jax.ShapeDtypeStruct((6, 3072), single),
            jax.ShapeDtypeStruct((6, 2, 3072), single),
            jax.ShapeDtypeStruct((16, 768), single),
            jax.ShapeDtypeStruct((8, 128), single),
        ),
        in_specs=[pl.BlockSpec(memory_space=pltpu.SMEM)] + [anywhere] * 4 + [vmem] * 4,
        out_specs=[vmem] * 5,
        scratch_shapes=[
            pltpu.VMEM((3, 4, 4, 48, 3072), bfloat),
            pltpu.VMEM((3, 4, 4, 48, 3072), bfloat),
            pltpu.VMEM((384, 768), bfloat),
            pltpu.VMEM((3, 128, 128), single),
            pltpu.VMEM((4, 112, 112), single),
            pltpu.VMEM((24, 768), single),
            pltpu.VMEM((4608, 128), single),
            pltpu.VMEM((400, 768), bfloat),
            pltpu.VMEM((400, 2304), bfloat),
            pltpu.VMEM((400, 768), bfloat),
            pltpu.VMEM((400, 768), single),
            pltpu.VMEM((384, 768), bfloat),
            pltpu.VMEM((384, 3072), bfloat),
            pltpu.VMEM((400, 3072), bfloat),
            pltpu.VMEM((384, 3072), bfloat),
            pltpu.VMEM((384, 768), single),
            pltpu.VMEM((384, 768), single),
            pltpu.VMEM((4, 4, 4, 48, 768), bfloat),
            pltpu.VMEM((2, 24, 768), single),
            pltpu.VMEM((2, 4, SHARD, 128), bfloat),
            pltpu.VMEM((48, 128), single),
            pltpu.VMEM((4, 4, 48, 128), bfloat),
            pltpu.VMEM((16, 768), single),
            pltpu.VMEM((8, 384), single),
            pltpu.VMEM((4, 2, 8, 384), single),
            pltpu.VMEM((4, 4, 8, 384), single),
            pltpu.VMEM((2, 3, 48, 768), bfloat),
            pltpu.VMEM((2, 3, 48, 768), bfloat),
            pltpu.VMEM((3, 4, 48, 384), bfloat),
            pltpu.VMEM((3, 48, 384), bfloat),
            pltpu.VMEM((2, 48, 1536), single),
            pltpu.VMEM((4, 48, 384), bfloat),
            pltpu.VMEM((2, 576, 128), single),
            pltpu.VMEM((144, 128), single),
            pltpu.VMEM((176, 128), single),
            pltpu.VMEM((4, 2, 176, 128), bfloat),
            pltpu.VMEM((4, 2, 176, 128), bfloat),
            pltpu.VMEM((24, 128), single),
            pltpu.VMEM((2, 16, 768), single),
            pltpu.VMEM((4, 16, 768), single),
            pltpu.VMEM((4, 16, 768), single),
            pltpu.VMEM((4, 16, 768), single),
            pltpu.VMEM((8, 128), single),
            pltpu.VMEM((4, 2, 8, 128), single),
            pltpu.VMEM((4, 4, 8, 128), single),
            pltpu.SemaphoreType.DMA((6,)),
            pltpu.SemaphoreType.DMA((copies,)),
            pltpu.SemaphoreType.DMA((copies,)),
        ],
        compiler_params=pltpu.CompilerParams(
            collective_id=1, has_side_effects=True, vmem_limit_bytes=63 * 2**20
        ),
        name="train_step",
    )(
        lengths,
        text,
        images,
        image_attn.reshape(4, 4, 48, 3072),
        image_mlp.reshape(2, 4, 4, 48, 3072),
        image_vectors,
        attn_master,
        mlp_master,
        vector_master,
    )


def close_kernel(*refs):
    given, out = (refs[:14], refs[14:])
    attn_sum, mlp_sum, vector_all, square, input_grad = given[:5]
    states = given[5:]
    out[0][...] = input_grad[...]
    grad_norm = jnp.sqrt(square[0:1, 0:1])
    out[1][...] = grad_norm
    factor = jnp.minimum(1.0, clip_norm / (grad_norm + 1e-06))
    start = lax.axis_index("dp") * 6
    vector_sum = pltpu.roll(vector_all[...], lax.rem(768 - start, 768), 1)[:, :128].T[:6, :12]
    sums = (attn_sum[...], mlp_sum[...], vector_sum)
    rates = ((learn_rate, weight_decay), (learn_rate, weight_decay), (vector_rate, 0.0))
    for n in range(3):
        out[2 + n][...] = sums[n]
        clip = factor.reshape(1, 1, 1) if n == 1 else factor
        new = adam_update(
            states[n][...], sums[n], states[3 + n][...], states[6 + n][...], clip, *rates[n]
        )
        for k in range(3):
            out[5 + 3 * k + n][...] = new[k]


def close(*given):
    vmem = pl.BlockSpec(memory_space=pltpu.VMEM)
    kinds = [(6, 3072), (6, 2, 3072), (6, 12)]
    shapes = [(384, 768), (1, 1)] + kinds * 4
    return pl.pallas_call(
        close_kernel,
        out_shape=[jax.ShapeDtypeStruct(shape, single) for shape in shapes],
        in_specs=[vmem] * 14,
        out_specs=[vmem] * 14,
        compiler_params=pltpu.CompilerParams(vmem_limit_bytes=32 * 2**20),
        name="close_step",
    )(*given)


def shards(
    text_input,
    caption_lengths,
    image_tokens,
    image_attn,
    image_mlp,
    image_vectors,
    attn_master,
    mlp_master,
    vector_master,
    attn_first,
    mlp_first,
    vector_first,
    attn_second,
    mlp_second,
    vector_second,
):
    mlp_master, mlp_first, mlp_second = (
        jnp.swapaxes(values, 0, 1) for values in (mlp_master, mlp_first, mlp_second)
    )
    vector_master, vector_first, vector_second = (
        values.T for values in (vector_master, vector_first, vector_second)
    )
    input_grad, attn_sum, mlp_sum, vector_all, square_total = train_step(
        caption_lengths.T,
        text_input,
        image_tokens,
        image_attn,
        image_mlp,
        image_vectors,
        attn_master,
        mlp_master,
        vector_master,
    )
    out = close(
        attn_sum,
        mlp_sum,
        vector_all,
        square_total,
        input_grad,
        attn_master,
        mlp_master,
        vector_master,
        attn_first,
        mlp_first,
        vector_first,
        attn_second,
        mlp_second,
        vector_second,
    )
    turned = [jnp.swapaxes(value, 0, 1) if n % 3 else value for n, value in enumerate(out[2:])]
    return (out[0], out[1].reshape(()), *turned)


def solution(mesh):
    in_specs = (
        P("dp", None),
        P("dp", None),
        P("dp", None),
        P(),
        P(),
        P(),
        P("dp", None),
        P(None, "dp", None),
        P(None, "dp"),
        P("dp", None),
        P(None, "dp", None),
        P(None, "dp"),
        P("dp", None),
        P(None, "dp", None),
        P(None, "dp"),
    )
    out_specs = (
        P("dp", None),
        P(),
        P("dp", None),
        P(None, "dp", None),
        P(None, "dp"),
        P("dp", None),
        P(None, "dp", None),
        P(None, "dp"),
        P("dp", None),
        P(None, "dp", None),
        P(None, "dp"),
        P("dp", None),
        P(None, "dp", None),
        P(None, "dp"),
    )
    return jax.shard_map(shards, mesh=mesh, in_specs=in_specs, out_specs=out_specs, check_vma=False)
```

```python
import jax
import jax.numpy as jnp
from jax import lax
from jax.experimental import pallas as pl
from jax.experimental.pallas import tpu as pltpu
from jax.sharding import PartitionSpec as P

STEP = 10


logit_scale = 60.0
clip_norm = 0.01
learn_rate = 0.05
vector_rate = 0.3
beta_first = 0.9
beta_second = 0.999
adam_epsilon = 1e-08
weight_decay = 0.1
bfloat = jnp.bfloat16
single = jnp.float32


def unit_rows(values):
    return values * lax.rsqrt(jnp.sum(values * values, -1, keepdims=True) + 1e-06)


def sum_squares(arrays):
    return sum((jnp.sum(member * member) for member in arrays))


def adam_update(weight, gradient, first_moment, second_moment, factor, rate, decay_rate):
    clipped = gradient * factor
    first_new = beta_first * first_moment + (1.0 - beta_first) * clipped
    second_new = beta_second * second_moment + (1.0 - beta_second) * clipped * clipped
    ratio = (
        first_new
        / (1.0 - beta_first**STEP)
        / (jnp.sqrt(second_new / (1.0 - beta_second**STEP)) + adam_epsilon)
    )
    return (first_new, second_new, weight - rate * (ratio + decay_rate * weight))


MESH = pl.DeviceIdType.MESH
LINES = 144
SHARD = 448
SUM_COPIES = 80
TURNS = (1, 3, 2)


def place():
    me = lax.axis_index("dp")
    return (me // 32, lax.rem(me // 8, 4), lax.rem(me // 2, 4), lax.rem(me, 2))


def device(x, z, y, c):
    return ((x * 4 + z) * 4 + y) * 2 + c


def plus(index, step):
    return lax.rem(index + step, 4)


def made(item):
    return item() if callable(item) else item


class Copy:
    def __init__(self, wire, slot, source, target, to):
        self.wire, self.slot, self.parts = (wire, slot, (source, target, to))

    def make(self):
        source, target, to = (made(part) for part in self.parts)
        return pltpu.make_async_remote_copy(
            src_ref=source,
            dst_ref=target,
            send_sem=self.wire.send_sems.at[self.slot],
            recv_sem=self.wire.recv_sems.at[self.slot],
            device_id=(to,),
            device_id_type=MESH,
        )

    def wait_recv(self):
        self.make().wait_recv()

    def wait_send(self):
        self.make().wait_send()


class Wire:
    def __init__(self, send_sems, recv_sems):
        self.send_sems, self.recv_sems, self.count, self.open = (send_sems, recv_sems, 0, [])

    def send(self, source, target, to):
        copy = Copy(self, self.count, source, target, to)
        copy.make().start()
        self.count += 1
        self.open.append(copy)
        return copy

    def clear(self, copies):
        for copy in copies:
            copy.wait_send()
        self.open = [copy for copy in self.open if not any(copy is other for other in copies)]

    def drain(self):
        self.clear(self.open)


def await_all(copies):
    for copy in copies:
        copy.wait_recv()


def greet(peers):
    for peer in peers:
        pl.semaphore_signal(
            pltpu.get_barrier_semaphore(), inc=1, device_id=(peer,), device_id_type=MESH
        )


def greeted(peers):
    pl.semaphore_wait(pltpu.get_barrier_semaphore(), len(peers))


class Ring:
    def __init__(self, wire, peer, view):
        self.wire, self.peer, self.view = (wire, peer, view)
        self.ahead = self.pass_on(0, None, 1)
        self.behind = self.pass_on(0, None, 3)

    def pass_on(self, k, part, step):
        block = lambda: self.view(k, part)
        return self.wire.send(block, block, lambda: self.peer(step))

    def forward(self):
        self.ahead.wait_recv()
        self.low = self.pass_on(3, 0, 1)
        self.behind.wait_recv()
        self.high = self.pass_on(1, 1, 3)

    def finish(self):
        self.low.wait_recv()
        self.high.wait_recv()


def aligned(start, size):
    return pl.ds(pl.multiple_of(start, 128), size)


def halves(start, size, part):
    if part is None:
        return aligned(start, size)
    low = size // 256 * 128
    return aligned(start, low) if part == 0 else aligned(start + low, size - low)


class Gather:
    def __init__(self, wire, peers, here, weight, turned, lines, natural, small):
        self.wire, self.here, self.weight, self.turned = (wire, here, weight, turned)
        self.lines, self.natural, self.small = (lines, natural, small)
        self.peers_x, self.peers_z, self.peers_y, self.sibling = peers
        x, z, y, c = here
        self.half, self.quarter = (c * 1536, (c * 4 + y) * 384)
        self.across = ([], [], [])

    def span(self, m):
        return (pl.ds(0, 160), pl.ds(160, 144), pl.ds(304, 144))[m]

    def begin(self):
        x, z, y, c = self.here
        self.first = {}
        for m in (2, 0, 1):
            view = lambda m=m: self.lines.at[c, y, self.span(m)]
            self.first[m] = [self.wire.send(view, view, lambda k=k: self.peers_y(k)) for k in TURNS]

    def swap(self):
        x, z, y, c = self.here
        self.swaps = {}
        for m in (2, 0, 1):
            await_all(self.first[m])
            view = lambda m=m: self.lines.at[c, :, self.span(m)]
            self.swaps[m] = self.wire.send(view, view, self.sibling)

    def spread(self, m):
        x, z, y, c = self.here
        self.swaps[m].wait_recv()
        for s in range(8):
            self.natural[s * LINES : (s + 1) * LINES] = self.lines[
                s % 2, s // 2, 16 + m * LINES : 16 + (m + 1) * LINES
            ].astype(single)
        start, count = (c * 12, 12) if m < 2 else ((c * 4 + y) * 3, 3)
        for j in range(count):
            self.weight[m, x, z, :, aligned((start + j) * 128, 128)] = self.natural[
                pl.ds(start + j, 48, stride=24), :
            ].astype(bfloat)

    def ring(self, peer, view):
        return Ring(self.wire, peer, view)

    def attn_x(self):
        x, z, y, c = self.here
        return self.ring(
            self.peers_x,
            lambda k, part: self.weight.at[0, plus(x, k), z, :, halves(self.half, 1536, part)],
        )

    def attn_z(self, b):
        x, z, y, c = self.here
        return self.ring(
            self.peers_z,
            lambda k, part: self.weight.at[
                0, plus(x, b), plus(z, k), :, halves(self.half, 1536, part)
            ],
        )

    def up_z(self):
        x, z, y, c = self.here
        return self.ring(
            self.peers_z,
            lambda k, part: self.weight.at[1, x, plus(z, k), :, halves(self.half, 1536, part)],
        )

    def up_x(self, b):
        x, z, y, c = self.here
        return self.ring(
            self.peers_x,
            lambda k, part: self.weight.at[
                1, plus(x, k), plus(z, b), :, halves(self.half, 1536, part)
            ],
        )

    def down_x(self):
        x, z, y, c = self.here
        return self.ring(
            self.peers_x,
            lambda k, part: self.weight.at[2, plus(x, k), z, :, halves(self.quarter, 384, part)],
        )

    def down_z(self, b):
        x, z, y, c = self.here
        return self.ring(
            self.peers_z,
            lambda k, part: self.weight.at[
                2, plus(x, b), plus(z, k), :, halves(self.quarter, 384, part)
            ],
        )

    def down_y(self, b):
        x, z, y, c = self.here
        return self.ring(
            self.peers_y,
            lambda k, part: self.weight.at[
                2, plus(x, b), :, :, halves((c * 4 + plus(y, k)) * 384, 384, part)
            ],
        )

    def spread_all(self):
        x, z, y, c = self.here
        self.spread(2)
        self.c1 = self.down_x()
        self.c2 = {0: self.down_z(0)}
        self.spread(0)
        self.a1 = self.attn_x()
        self.spread(1)
        self.b1 = self.up_z()
        for s in range(8):
            self.small[s * 6 : (s + 1) * 6] = self.lines[s % 2, s // 2, 0:16].astype(single)[0:6]
        self.turned[x, z] = self.small[...].astype(bfloat)
        view = lambda: self.turned.at[x, z]
        self.turn_x = [self.wire.send(view, view, lambda k=k: self.peers_x(k)) for k in TURNS]

    def nearest(self):
        self.c1.forward()
        for b in (3, 1):
            self.c2[b] = self.down_z(b)
        self.a1.forward()
        self.b1.forward()
        self.c2[0].forward()
        self.a2 = {0: self.attn_z(0)}
        self.b2 = {0: self.up_x(0)}

    def farthest(self):
        self.c1.finish()
        self.c2[2] = self.down_z(2)
        self.c2[0].finish()
        self.c3 = {0: self.down_y(0)}
        for b in (3, 1):
            self.c2[b].forward()
        for b in (3, 1):
            self.a2[b] = self.attn_z(b)
            self.b2[b] = self.up_x(b)
        x, z, y, c = self.here
        await_all(self.turn_x)
        view = lambda: self.turned.at[:, z]
        self.turn_z = [self.wire.send(view, view, lambda k=k: self.peers_z(k)) for k in TURNS]

    def second_own(self):
        for b in (3, 1):
            self.c2[b].finish()
            self.c3[b] = self.down_y(b)
        self.c2[2].forward()
        self.a1.finish()
        self.a2[2] = self.attn_z(2)
        self.b1.finish()
        self.b2[2] = self.up_x(2)
        self.a2[0].forward()
        self.b2[0].forward()

    def second_near(self):
        self.c3[0].forward()
        self.c2[2].finish()
        self.c3[2] = self.down_y(2)
        for b in (3, 1):
            self.a2[b].forward()
            self.b2[b].forward()
        self.finish_attn(0)
        self.finish_up(0)

    def third_near(self):
        for b in (3, 1):
            self.c3[b].forward()
        self.finish_down(0)
        for b in (3, 1):
            self.finish_attn(b)
            self.finish_up(b)

    def second_far(self):
        self.a2[2].forward()
        self.b2[2].forward()
        self.c3[2].forward()
        for b in (3, 1):
            self.finish_down(b)

    def finish_attn(self, b):
        x, z, y, c = self.here
        self.a2[b].finish()
        self.cross(0, lambda: self.weight.at[0, plus(x, b), :, :, aligned(self.half, 1536)])

    def finish_up(self, b):
        x, z, y, c = self.here
        self.b2[b].finish()
        self.cross(1, lambda: self.weight.at[1, :, plus(z, b), :, aligned(self.half, 1536)])

    def finish_down(self, b):
        x, z, y, c = self.here
        self.c3[b].finish()
        self.cross(2, lambda: self.weight.at[2, plus(x, b), :, :, aligned(self.half, 1536)])

    def cross(self, m, view):
        self.across[m].append(self.wire.send(view, view, self.sibling))

    def end(self, m):
        await_all(self.across[m])


def matmul(left, right):
    return jnp.dot(left, right, preferred_element_type=single)


def matmul_nt(left, right):
    return lax.dot_general(left, right, (((1,), (1,)), ((), ())), preferred_element_type=single)


def matmul_tn(left, right):
    return lax.dot_general(left, right, (((0,), (0,)), ((), ())), preferred_element_type=single)


def normalized(values):
    center = jnp.mean(values, -1, keepdims=True)
    shifted = values - center
    spread = jnp.mean(shifted * shifted, -1, keepdims=True)
    inverse = lax.rsqrt(spread + 1e-06)
    return (shifted * inverse, inverse)


def normalized_back(cotangent, unit, inverse, gain):
    scaled = cotangent * gain
    center = jnp.mean(scaled, -1, keepdims=True)
    along = jnp.mean(scaled * unit, -1, keepdims=True)
    return inverse * (scaled - center - unit * along)


def gelu_parts(hidden):
    squared = hidden * hidden
    angle = jnp.tanh(hidden * (0.7978845608028654 + 0.035677408136300125 * squared))
    return (squared, angle)


def even_lanes(rows):
    return lax.broadcasted_iota(jnp.int32, (rows, 128), 1) < 64


def split_heads(values):
    even = even_lanes(values.shape[0])
    zero = jnp.zeros_like(values)
    return jnp.concatenate([jnp.where(even, values, zero), jnp.where(even, zero, values)], 0)


def join_heads(values):
    rows = values.shape[0] // 2
    return jnp.where(even_lanes(rows), values[:rows], values[rows:])


def pair_weights(queries, key_rows, bias):
    scores = matmul_nt(split_heads(queries * 0.125), key_rows)
    scores = scores + jnp.concatenate([bias, bias], 0)
    weights = jnp.exp(scores - jnp.max(scores, -1, keepdims=True))
    return (weights, 1.0 / jnp.sum(weights, -1, keepdims=True))


def attend_images(qkv, attended, bias):
    starts = (0, 96, 192, 288)
    rows = lax.broadcasted_iota(jnp.int32, (16, 128), 0)

    @pl.loop(0, 6, unroll=3)
    def _(p):
        out = []
        for w, start in enumerate(starts):
            window = slice(start, start + 112)
            weights, scale = pair_weights(
                qkv[window, aligned(p * 128, 128)], qkv[window, aligned((6 + p) * 128, 128)], bias[w]
            )
            values = qkv[window, aligned((12 + p) * 128, 128)]
            out.append(join_heads(matmul(weights.astype(bfloat), values) * scale))
        lanes = aligned(p * 128, 128)
        attended[0:96, lanes] = out[0][0:96].astype(bfloat)
        for w in range(1, 4):
            edge = jnp.where(rows < 4 * w, out[w - 1][96:112], out[w][0:16])
            attended[starts[w] : starts[w] + 16, lanes] = edge.astype(bfloat)
            stop = 112 if w == 3 else 96
            attended[starts[w] + 16 : starts[w] + stop, lanes] = out[w][16:stop].astype(bfloat)


class UnitGather:
    def __init__(self, wire, peers, here, units, own, images, first, count):
        self.wire, self.here, self.units, self.own, self.images = (wire, here, units, own, images)
        self.peers_x, self.peers_z, self.peers_y, self.sibling = peers
        self.first, self.count, self.step = (first, count, 0)

    def swap(self):
        c = self.here[3]
        rows = pl.ds(self.first, self.count)
        self.own[c, rows] = self.units[rows, :]
        self.swapped = self.wire.send(self.own.at[c, rows], self.own.at[c, rows], self.sibling)

    def begin(self):
        x, z, y, c = self.here
        self.swapped.wait_recv()
        lanes = aligned(c * 384, 384)
        for first in range(self.first, self.first + self.count, 8):
            both = [self.own[core, first : first + 8, lanes] for core in range(2)]
            self.images[x, z, y, 2 * first : 2 * first + 16, lanes] = jnp.concatenate(both, 0).astype(
                bfloat
            )
        self.start()

    def start(self):
        x, z, y, c = self.here
        here = {"x": x, "z": z, "y": y}
        peer = {"x": self.peers_x, "z": self.peers_z, "y": self.peers_y}
        rows = pl.ds(2 * self.first, 2 * self.count)
        self.sent = []
        for o, order in enumerate(("yzx", "zxy", "xyz")):
            index = [slice(None) if n in order[: self.step] else here[n] for n in "xzy"]
            view = self.images.at[(*index, rows, aligned((c * 3 + o) * 128, 128))]
            self.sent += [self.wire.send(view, view, peer[order[self.step]](k)) for k in TURNS]
        self.step += 1

    def next(self):
        await_all(self.sent)
        self.start()

    def finish(self):
        await_all(self.sent)
        rows = pl.ds(2 * self.first, 2 * self.count)
        mine = self.images.at[:, :, :, rows, aligned(self.here[3] * 384, 384)]
        self.crossed = self.wire.send(mine, mine, self.sibling)

    def end(self):
        self.crossed.wait_recv()


def image_bias(bias):
    for w in range(4):
        first = 96 * w
        query = (lax.broadcasted_iota(jnp.int32, (112, 112), 0) + first) // 50
        key = (lax.broadcasted_iota(jnp.int32, (112, 112), 1) + first) // 50
        bias[w] = jnp.where(query == key, 0.0, -1e30)


def image_chunk(t, tokens, weight, vec, normed, qkv, attended, residual, bias, units, hook):
    lanes_t = slice(t * 768, (t + 1) * 768)
    unit, _ = normalized(tokens[:, lanes_t].astype(single))
    normed[...] = (unit * vec[0:1] + vec[1:2]).astype(bfloat)
    hook()
    for n, shift in enumerate((4, None, 5)):
        triple = matmul(normed[...], weight(0, n * 768, 768))
        if shift is not None:
            triple = triple + vec[shift : shift + 1]
        qkv[:, n * 768 : (n + 1) * 768] = triple.astype(bfloat)
    hook()
    attend_images(qkv, attended, bias)
    hook()
    residual[...] = (
        tokens[:, lanes_t].astype(single) + matmul(attended[...], weight(0, 2304, 768)) + vec[6:7]
    )
    unit, _ = normalized(residual[...])
    normed[...] = (unit * vec[2:3] + vec[3:4]).astype(bfloat)
    residual[...] = residual[...] + vec[7:8]
    hook()
    for f in range(4):
        hidden = matmul(normed[...], weight(1, f * 768, 768)) + vec[8 + f : 9 + f]
        _, angle = gelu_parts(hidden)
        active = (0.5 * hidden * (1.0 + angle)).astype(bfloat)
        residual[...] = residual[...] + matmul_nt(active, weight(2, f * 768, 768))
        hook()
    image = lax.broadcasted_iota(jnp.int32, (8, 400), 0)
    token = lax.broadcasted_iota(jnp.int32, (8, 400), 1)
    member = (token // 50 == image).astype(bfloat)
    high = residual[...].astype(bfloat)
    low = (residual[...] - high.astype(single)).astype(bfloat)
    pooled = (matmul(member, high) + matmul(member, low)) * (1.0 / 50.0)
    units[t * 8 : (t + 1) * 8, :] = unit_rows(pooled)


PLAN = {
    (0, 2): "swap",
    (0, 4): "spread_all",
    (0, 6): "nearest",
    (1, 0): "farthest",
    (1, 2): "second_own",
    (1, 5): "second_near",
    (2, 2): "third_near",
    (2, 6): "second_far",
}


def slot_codes(index, ends, window):
    later = index >= 64
    position = jnp.where(later, index - 64, index)
    slots = [
        sum((position >= ends[2 * window + r][k]).astype(jnp.int32) for k in range(4)) for r in (0, 1)
    ]
    return jnp.where(later, slots[1] + 8, slots[0])


def text_masks(lengths, bias):
    ends = []
    for r in range(6):
        row, end = ([], 0)
        for k in range(4):
            end = end + lengths[k, r]
            row.append(end)
        ends.append(row)
    codes = []
    for w in range(3):
        query = slot_codes(lax.broadcasted_iota(jnp.int32, (128, 128), 0), ends, w)
        key = slot_codes(lax.broadcasted_iota(jnp.int32, (128, 128), 1), ends, w)
        bias[w] = jnp.where(query == key, 0.0, -1e30)
        code = slot_codes(lax.broadcasted_iota(jnp.int32, (24, 128), 1), ends, w)
        slot = jnp.where(code >= 8, code - 8, code)
        caption = 8 * w + jnp.where(code >= 8, 4, 0) + slot
        codes.append(jnp.where(slot < 4, caption, -1))
    caption = jnp.concatenate(codes, 1)
    return (caption == lax.broadcasted_iota(jnp.int32, (24, 384), 0)).astype(single)


def attend_text(qkv, attended, probs, bias):
    @pl.loop(0, 6, unroll=3)
    def _(p):
        for w in range(3):
            window = slice(w * 128, (w + 1) * 128)
            weights, scale = pair_weights(
                qkv[window, aligned(p * 128, 128)], qkv[window, aligned((6 + p) * 128, 128)], bias[w]
            )
            pair = weights * scale
            probs[pl.ds(pl.multiple_of((p * 3 + w) * 256, 256), 256)] = pair
            out = matmul(pair.astype(bfloat), qkv[window, aligned((12 + p) * 128, 128)])
            attended[window, aligned(p * 128, 128)] = join_heads(out).astype(bfloat)


def attend_text_back(qkv, probs, attended_grad, triple_grad):
    @pl.loop(0, 6, unroll=3)
    def _(p):
        for w in range(3):
            window = slice(w * 128, (w + 1) * 128)
            at = [aligned((6 * n + p) * 128, 128) for n in range(3)]
            queries, key_rows, value_rows = (qkv[window, lanes] for lanes in at)
            grads = split_heads(attended_grad[window, at[0]])
            pair = probs[pl.ds(pl.multiple_of((p * 3 + w) * 256, 256), 256)]
            value_grad = matmul_tn(pair.astype(bfloat), grads)
            prob_grad = matmul_nt(grads, value_rows)
            along = jnp.sum(pair * prob_grad, -1, keepdims=True)
            score_grad = (pair * (prob_grad - along) * 0.125).astype(bfloat)
            query_grad = join_heads(matmul(score_grad, key_rows))
            key_grad = matmul_tn(score_grad, split_heads(queries))
            triple_grad[window, at[0]] = query_grad.astype(bfloat)
            triple_grad[window, at[1]] = key_grad.astype(bfloat)
            triple_grad[window, at[2]] = value_grad.astype(bfloat)


def column_sums(values):
    return jnp.sum(values.astype(single), 0, keepdims=True)


def step_kernel(
    lengths,
    tokens_ref,
    image_ref,
    image_attn_ref,
    image_mlp_ref,
    image_vec,
    attn_ref,
    mlp_ref,
    vector_ref,
    input_grad,
    attn_out,
    mlp_out,
    vector_out,
    square_out,
    weight,
    store,
    tokens,
    bias,
    image_masks,
    units,
    probs,
    normed,
    qkv,
    attended,
    residual,
    normed_two,
    active,
    slope,
    triple_grad,
    flow,
    part_sum,
    images,
    own,
    lines,
    small,
    turned,
    vec,
    row_part,
    row_near,
    row_far,
    late_x,
    late_z,
    down_x,
    down_z,
    whole,
    last,
    flat,
    third,
    packed,
    pieces,
    landed,
    sums,
    vec_c,
    vec_z,
    vec_x,
    vec_y,
    square,
    near,
    far,
    load_sems,
    send_sems,
    recv_sems,
):
    x, z, y, c = place()
    peers_x = lambda k: device(plus(x, k), z, y, c)
    peers_z = lambda k: device(x, plus(z, k), y, c)
    peers_y = lambda k: device(x, z, plus(y, k), c)
    sibling = device(x, z, y, 1 - c)
    group = [(k, d) for k in range(4) for d in range(2) if (k, d) != (0, 0)]
    plane = [(i, j) for i in range(4) for j in range(4) if (i, j) != (0, 0)]
    group_peer = lambda k, d: device(x, z, plus(y, k), lax.rem(c + d, 2))
    plane_peer = lambda i, j: device(plus(x, i), plus(z, j), y, c)
    wire = Wire(send_sems, recv_sems)
    turns = TURNS

    held = store.at[:, :, :, :, 0:1536]
    low, high = (slice(0, 768), slice(768, 1536))
    from_z = [[store.at[m, k, :, :, 1536:2304] for k in range(3)] for m in range(2)]
    from_x = [[store.at[m, k, :, :, 2304:3072] for k in range(3)] for m in range(2)]
    from_y = [store.at[2, :, :, :, 1536 + 384 * k : 1920 + 384 * k] for k in range(3)]
    total_z = [store.at[m, 3, :, :, 1536:2304] for m in range(2)]
    total_x = [store.at[m, 3, :, :, 2304:3072] for m in range(2)]
    total_y = store.at[2, :, :, :, 2688:3072]

    loads = [
        pltpu.make_async_copy(source, target, load_sems.at[n])
        for n, (source, target) in enumerate(
            [
                (image_ref.at[0:400], slope.at[:, 0:768]),
                (image_attn_ref, store.at[0]),
                (image_mlp_ref, store.at[1:3]),
                (image_ref.at[400:800], slope.at[:, 768:1536]),
                (image_ref.at[800:1200], slope.at[:, 1536:2304]),
                (tokens_ref, tokens),
            ]
        )
    ]
    for load in loads:
        load.start()
    others = [group_peer(*g) for g in group] + [plane_peer(*p) for p in plane]
    greet(others)
    natural, line = (probs.at[0:1152], [probs.at[1152 + 144 * m : 1296 + 144 * m] for m in range(3)])
    small[0:16] = jnp.zeros((16, 128), single)
    small[0:6, 0:12] = vector_ref[...]
    lines[c, y, 0:16] = small[0:16].astype(bfloat)
    for m in range(3):
        for j in range(24):
            columns = slice(j * 128, (j + 1) * 128)
            rows = attn_ref[:, columns] if m == 0 else mlp_ref[:, m - 1, columns]
            line[m][pl.ds(j, 6, stride=24), :] = rows
        lines[c, y, 16 + m * LINES : 16 + (m + 1) * LINES] = line[m][...].astype(bfloat)
    greeted(others)
    peers = (peers_x, peers_z, peers_y, sibling)
    unit_gather = UnitGather(wire, peers, (x, z, y, c), units, own, images, 0, 24)
    gather = Gather(
        wire, peers, (x, z, y, c), weight, turned, lines, natural, small
    )
    gather.begin()
    image_bias(image_masks)
    for load in loads:
        load.wait()
    plan = PLAN
    image_weight = lambda m, first, size: store[m, :, :, :, first : first + size].reshape(768, size)

    for t in range(3):
        points = iter(range(99))

        def hook():
            for name in plan.get((t, next(points)), "").split():
                getattr(gather, name)()

        image_chunk(
            t, slope, image_weight, image_vec, normed, qkv, attended, residual, image_masks, units, hook
        )

    unit_gather.swap()
    gather.finish_attn(2)
    gather.finish_up(2)
    member = text_masks(lengths, bias)
    unit_gather.begin()
    await_all(gather.turn_z)
    vec[...] = turned[...].reshape(768, 128).astype(single).T[0:16]

    normed, qkv, attended, residual, slope = (
        ref.at[0:384] for ref in (normed, qkv, attended, residual, slope)
    )
    unit_one, _ = normalized(tokens[...].astype(single))
    normed[...] = (unit_one * vec[0:1] + vec[1:2]).astype(bfloat)
    gather.end(0)
    attn = lambda first, size: weight[0, :, :, :, first : first + size].reshape(768, size)
    for n, shift in enumerate((4, None, 5)):
        triple = matmul(normed[...], attn(n * 768, 768))
        if shift is not None:
            triple = triple + vec[shift : shift + 1]
        qkv[:, n * 768 : (n + 1) * 768] = triple.astype(bfloat)
    unit_gather.next()
    gather.finish_down(2)
    attend_text(qkv, attended, probs, bias)
    residual[...] = tokens[...].astype(single) + matmul(attended[...], attn(2304, 768)) + vec[6:7]
    unit_two, _ = normalized(residual[...])
    normed_two[...] = (unit_two * vec[2:3] + vec[3:4]).astype(bfloat)
    unit_gather.next()
    gather.end(1)
    for f in range(4):
        lanes = slice(f * 768, (f + 1) * 768)
        hidden = matmul(normed_two[...], weight[1, :, :, :, lanes].reshape(768, 768)) + vec[8 + f : 9 + f]
        squared, angle = gelu_parts(hidden)
        active[:, lanes] = (0.5 * hidden * (1.0 + angle)).astype(bfloat)
        curve = 0.7978845608028654 + 0.10703222440890037 * squared
        slope[:, lanes] = (
            0.5 * (1.0 + angle) + 0.5 * hidden * (1.0 - angle * angle) * curve
        ).astype(bfloat)
    gather.end(2)
    flow[...] = residual[...] + vec[7:8]
    for f in range(4):
        lanes = slice(f * 768, (f + 1) * 768)
        flow[...] = flow[...] + matmul_nt(
            active[:, lanes], weight[2, :, :, :, lanes].reshape(768, 768)
        )
    unit_gather.finish()
    highest = lax.Precision.HIGHEST
    per_length = 1.0 / jnp.sum(member, -1, keepdims=True)
    pooled = per_length * jnp.dot(member, flow[...], precision=highest, preferred_element_type=single)

    scale = lax.rsqrt(jnp.sum(pooled * pooled, -1, keepdims=True) + 1e-06)
    unit = pooled * scale
    unit_gather.end()
    every = images[...].reshape(3072, 768)
    logits = logit_scale * matmul_nt(unit.astype(bfloat), every)
    powers = jnp.exp(logits)
    column = jnp.sum(powers, 1, keepdims=True)
    rows = jnp.sum(powers, 0, keepdims=True)
    for k in range(8):
        row_part[k : k + 1, :] = rows[:, k * 384 : (k + 1) * 384]
    row_near[y, c] = row_part[...]
    wire.count = max(wire.count, SUM_COPIES)
    sent = [wire.send(row_part, row_near.at[y, c], group_peer(*g)) for g in group]
    caption = lax.broadcasted_iota(jnp.int32, (24, 3072), 0) + lax.axis_index("dp") * 24
    at = lax.broadcasted_iota(jnp.int32, (24, 3072), 1)
    inside = at % 48
    image = at - inside + inside // 8 % 2 * 24 + inside // 16 * 8 + inside % 8
    same = (caption == image).astype(single)
    of_column = powers / column - 2.0 * same
    await_all(sent)
    row_far[x, z] = sum(row_near[k, d] for k in range(4) for d in range(2))
    sent = [wire.send(row_far.at[x, z], row_far.at[x, z], plane_peer(*p)) for p in plane]
    await_all(sent)
    total = sum(row_far[i, j] for i in range(4) for j in range(4))
    every_row = jnp.concatenate([total[k : k + 1] for k in range(8)], 1)
    logit_grad = (logit_scale / (2.0 * 3072) * (powers / every_row + of_column)).astype(bfloat)
    unit_grad = matmul(logit_grad, every)
    pooled_grad = scale * (unit_grad - unit * jnp.sum(unit * unit_grad, -1, keepdims=True))
    flow[...] = lax.dot_general(
        member,
        pooled_grad * per_length,
        (((0,), (0,)), ((), ())),
        precision=highest,
        preferred_element_type=single,
    )

    sends = {}

    def block_grad(left, right):
        return matmul_tn(left, right).reshape(4, 4, 48, right.shape[1])

    def other_half(m, make):
        for i in range(2):
            place_i = images.at[:, :, 2 * (m % 2) + i]
            place_i[...] = make((1 - c) * 1536 + i * 768, i).astype(bfloat)
            sends[m, i] = wire.send(
                place_i, held.at[m, :, :, :, i * 768 : (i + 1) * 768], sibling
            )

    def own_half(m, make):
        for i in range(2):
            sends[m, i].wait_recv()
            lanes = slice(i * 768, (i + 1) * 768)
            held[m, :, :, :, lanes] = (
                make(c * 1536 + i * 768, i) + held[m, :, :, :, lanes].astype(single)
            ).astype(bfloat)

    wire.drain()
    wire.count = 0

    def add(base, parts):
        return base.astype(single) + sum(part.astype(single) for part in parts)

    def first_sums(m):
        return [
            [wire.send(held.at[m, :, plus(z, k), :, low], from_z[m][k - 1], peers_z(k)) for k in turns],
            [wire.send(held.at[m, plus(x, k), :, :, high], from_x[m][k - 1], peers_x(k)) for k in turns],
        ]

    def second_sums(m, sent):
        await_all(sent[0])
        for i in range(4):
            total_z[m][i] = add(held[m, i, z, :, low], [from_z[m][k][i] for k in range(3)]).astype(bfloat)
        over_x = [
            wire.send(total_z[m].at[plus(x, k)], late_x.at[m, k - 1], peers_x(k)) for k in turns
        ]
        await_all(sent[1])
        for i in range(4):
            total_x[m][i] = add(held[m, x, i, :, high], [from_x[m][k][i] for k in range(3)]).astype(bfloat)
        over_z = [
            wire.send(total_x[m].at[plus(z, k)], late_z.at[m, k - 1], peers_z(k)) for k in turns
        ]
        return (over_x, over_z)

    def whole_sums(m, sent):
        await_all(sent[0])
        whole[m, :, low] = add(total_z[m][x], [late_x[m, k] for k in range(3)])
        await_all(sent[1])
        whole[m, :, high] = add(total_x[m][z], [late_z[m, k] for k in range(3)])
        for j in range(12):
            flat[m, pl.ds(j, 48, stride=12), :] = whole[m, :, j * 128 : (j + 1) * 128]

    branch_two = triple_grad.at[:, 2304:3072]
    branch_two[...] = flow[...].astype(bfloat)
    vec_c[c] = jnp.zeros((16, 768), single)
    vec_c[c, 7:8] = column_sums(branch_two[...])
    make_two = lambda first, i: block_grad(branch_two[...], active[:, aligned(first, 768)])
    other_half(2, make_two)
    for f in range(4):
        lanes = slice(f * 768, (f + 1) * 768)
        active_grad = matmul(branch_two[...], weight[2, :, :, :, lanes].reshape(768, 768))
        hidden_grad = (active_grad * slope[:, lanes].astype(single)).astype(bfloat)
        slope[:, lanes] = hidden_grad
        vec_c[c, 8 + f : 9 + f] = column_sums(hidden_grad)
    make_one = lambda first, i: block_grad(normed_two[...], slope[:, aligned(first, 768)])
    other_half(1, make_one)
    for f in range(4):
        lanes = slice(f * 768, (f + 1) * 768)
        piece = matmul_nt(slope[:, lanes], weight[1, :, :, :, lanes].reshape(768, 768))
        part_sum[...] = piece if f == 0 else part_sum[...] + piece
    own_half(2, make_two)
    send_y = [
        wire.send(held.at[2, :, :, :, aligned(plus(y, k) * 384, 384)], from_y[k - 1], peers_y(k))
        for k in turns
    ]
    unit_two, inverse_two = normalized(residual[...])
    vec_c[c, 2:3] = jnp.sum(part_sum[...] * unit_two, 0, keepdims=True)
    vec_c[c, 3:4] = jnp.sum(part_sum[...], 0, keepdims=True)
    flow[...] = flow[...] + normalized_back(part_sum[...], unit_two, inverse_two, vec[2:3])
    triple_grad[:, 2304:3072] = flow[...].astype(bfloat)
    vec_c[c, 6:7] = column_sums(triple_grad[:, 2304:3072])
    own_half(1, make_one)
    send_one = first_sums(1)
    active[:, 0:768] = matmul_nt(triple_grad[:, 2304:3072], attn(2304, 768)).astype(bfloat)
    attend_text_back(qkv, probs, active, triple_grad)
    vec_c[c, 4:5] = column_sums(triple_grad[:, 0:768])
    vec_c[c, 5:6] = column_sums(triple_grad[:, 1536:2304])

    def make_zero(first, i):
        left = normed[...]
        if i == 1:
            left = jnp.where(first >= 2304, attended[...], left)
        return block_grad(left, triple_grad[:, aligned(first, 768)])

    wire.clear([sends[2, i] for i in range(2)])
    other_half(0, make_zero)
    for n in range(3):
        piece = matmul_nt(triple_grad[:, n * 768 : (n + 1) * 768], attn(n * 768, 768))
        part_sum[...] = piece if n == 0 else part_sum[...] + piece
    own_half(0, make_zero)
    send_zero = first_sums(0)
    unit_one, inverse_one = normalized(tokens[...].astype(single))
    vec_c[c, 0:1] = jnp.sum(part_sum[...] * unit_one, 0, keepdims=True)
    vec_c[c, 1:2] = jnp.sum(part_sum[...], 0, keepdims=True)
    vec_swap = wire.send(vec_c.at[c], vec_c.at[c], sibling)
    input_grad[...] = flow[...] + normalized_back(part_sum[...], unit_one, inverse_one, vec[0:1])
    second_one = second_sums(1, send_one)
    vec_swap.wait_recv()
    vec_z[z] = vec_c[0] + vec_c[1]
    sent_vec_z = [wire.send(vec_z.at[z], vec_z.at[z], peers_z(k)) for k in turns]

    await_all(send_y)
    quarter = aligned(y * 384, 384)
    for i in range(4):
        for j in range(4):
            total_y[i, j] = add(
                held[2, i, j, :, quarter], [from_y[k][i, j] for k in range(3)]
            ).astype(bfloat)
    down_send_x = [wire.send(total_y.at[plus(x, k)], down_x.at[k - 1], peers_x(k)) for k in turns]
    await_all(sent_vec_z)
    vec_x[x] = vec_z[0] + vec_z[1] + vec_z[2] + vec_z[3]
    sent_vec_x = [wire.send(vec_x.at[x], vec_x.at[x], peers_x(k)) for k in turns]
    whole_sums(1, second_one)
    await_all(down_send_x)
    for j in range(4):
        last[j] = add(total_y[x, j], [down_x[k, j] for k in range(3)]).astype(bfloat)
    down_send_z = [wire.send(last.at[plus(z, k)], down_z.at[k - 1], peers_z(k)) for k in turns]
    await_all(sent_vec_x)
    vec_y[y] = vec_x[0] + vec_x[1] + vec_x[2] + vec_x[3]
    sent_vec_y = [wire.send(vec_y.at[y], vec_y.at[y], peers_y(k)) for k in turns]
    second_zero = second_sums(0, send_zero)
    await_all(down_send_z)
    ended = add(last[z], [down_z[k] for k in range(3)])
    for j in range(3):
        third[pl.ds(j, 48, stride=3), :] = ended[:, j * 128 : (j + 1) * 128]
    whole_sums(0, second_zero)
    packed[160:176] = jnp.zeros((16, 128), single)
    for s in range(8):
        packed[0:72] = flat[0, s * 72 : (s + 1) * 72]
        packed[72:144] = flat[1, s * 72 : (s + 1) * 72]
        packed[144:162] = third[s * 18 : (s + 1) * 18]
        pieces[s // 2, s % 2] = packed[...].astype(bfloat)
    landed[y, c] = pieces[y, c]
    piece_sent = [
        wire.send(pieces.at[plus(y, k), lax.rem(c + d, 2)], landed.at[y, c], group_peer(k, d))
        for k, d in group
    ]
    await_all(sent_vec_y)
    vec_total = vec_y[0] + vec_y[1] + vec_y[2] + vec_y[3]
    vector_out[...] = vec_total
    await_all(piece_sent)
    for h in range(2):
        for k in range(4):
            piece = landed[k, h].astype(single)
            packed[...] = piece if k == 0 else packed[...] + piece
            sums[...] = piece[144:168]
            for j in range(3):
                at = ((h * 4 + k) * 3 + j) * 128
                mlp_out[:, 1, at : at + 128] = sums[pl.ds(j, 6, stride=3), :]
        for j in range(12):
            at = (h * 12 + j) * 128
            attn_out[:, at : at + 128] = packed[pl.ds(j, 6, stride=12), :]
            mlp_out[:, 0, at : at + 128] = packed[pl.ds(72 + j, 6, stride=12), :]
    lanes = lax.broadcasted_iota(jnp.int32, (16, 768), 1)
    start = lax.axis_index("dp") * 6
    owned = jnp.where((lanes >= start) & (lanes < start + 6), vec_total, 0.0)
    squares = sum_squares((attn_out[...], mlp_out[...], owned))
    square[...] = jnp.broadcast_to(squares, (8, 128))
    near[y, c] = square[...]
    sent = [wire.send(square, near.at[y, c], group_peer(*g)) for g in group]
    await_all(sent)
    far[x, z] = sum(near[k, d] for k in range(4) for d in range(2))
    sent = [wire.send(far.at[x, z], far.at[x, z], plane_peer(*p)) for p in plane]
    await_all(sent)
    square_out[...] = sum(far[i, j] for i in range(4) for j in range(4))
    wire.drain()


def train_step(
    lengths, text, images, image_attn, image_mlp, image_vectors, attn_master, mlp_master, vector_master
):
    copies = 160
    vmem = pl.BlockSpec(memory_space=pltpu.VMEM)
    anywhere = pl.BlockSpec(memory_space=pl.ANY)
    return pl.pallas_call(
        step_kernel,
        out_shape=(
            jax.ShapeDtypeStruct((384, 768), single),
            jax.ShapeDtypeStruct((6, 3072), single),
            jax.ShapeDtypeStruct((6, 2, 3072), single),
            jax.ShapeDtypeStruct((16, 768), single),
            jax.ShapeDtypeStruct((8, 128), single),
        ),
        in_specs=[pl.BlockSpec(memory_space=pltpu.SMEM)] + [anywhere] * 4 + [vmem] * 4,
        out_specs=[vmem] * 5,
        scratch_shapes=[
            pltpu.VMEM((3, 4, 4, 48, 3072), bfloat),
            pltpu.VMEM((3, 4, 4, 48, 3072), bfloat),
            pltpu.VMEM((384, 768), bfloat),
            pltpu.VMEM((3, 128, 128), single),
            pltpu.VMEM((4, 112, 112), single),
            pltpu.VMEM((24, 768), single),
            pltpu.VMEM((4608, 128), single),
            pltpu.VMEM((400, 768), bfloat),
            pltpu.VMEM((400, 2304), bfloat),
            pltpu.VMEM((400, 768), bfloat),
            pltpu.VMEM((400, 768), single),
            pltpu.VMEM((384, 768), bfloat),
            pltpu.VMEM((384, 3072), bfloat),
            pltpu.VMEM((400, 3072), bfloat),
            pltpu.VMEM((384, 3072), bfloat),
            pltpu.VMEM((384, 768), single),
            pltpu.VMEM((384, 768), single),
            pltpu.VMEM((4, 4, 4, 48, 768), bfloat),
            pltpu.VMEM((2, 24, 768), single),
            pltpu.VMEM((2, 4, SHARD, 128), bfloat),
            pltpu.VMEM((48, 128), single),
            pltpu.VMEM((4, 4, 48, 128), bfloat),
            pltpu.VMEM((16, 768), single),
            pltpu.VMEM((8, 384), single),
            pltpu.VMEM((4, 2, 8, 384), single),
            pltpu.VMEM((4, 4, 8, 384), single),
            pltpu.VMEM((2, 3, 48, 768), bfloat),
            pltpu.VMEM((2, 3, 48, 768), bfloat),
            pltpu.VMEM((3, 4, 48, 384), bfloat),
            pltpu.VMEM((3, 48, 384), bfloat),
            pltpu.VMEM((2, 48, 1536), single),
            pltpu.VMEM((4, 48, 384), bfloat),
            pltpu.VMEM((2, 576, 128), single),
            pltpu.VMEM((144, 128), single),
            pltpu.VMEM((176, 128), single),
            pltpu.VMEM((4, 2, 176, 128), bfloat),
            pltpu.VMEM((4, 2, 176, 128), bfloat),
            pltpu.VMEM((24, 128), single),
            pltpu.VMEM((2, 16, 768), single),
            pltpu.VMEM((4, 16, 768), single),
            pltpu.VMEM((4, 16, 768), single),
            pltpu.VMEM((4, 16, 768), single),
            pltpu.VMEM((8, 128), single),
            pltpu.VMEM((4, 2, 8, 128), single),
            pltpu.VMEM((4, 4, 8, 128), single),
            pltpu.SemaphoreType.DMA((6,)),
            pltpu.SemaphoreType.DMA((copies,)),
            pltpu.SemaphoreType.DMA((copies,)),
        ],
        compiler_params=pltpu.CompilerParams(
            collective_id=1, has_side_effects=True, vmem_limit_bytes=63 * 2**20
        ),
        name="train_step",
    )(
        lengths,
        text,
        images,
        image_attn.reshape(4, 4, 48, 3072),
        image_mlp.reshape(2, 4, 4, 48, 3072),
        image_vectors,
        attn_master,
        mlp_master,
        vector_master,
    )


def close_kernel(*refs):
    given, out = (refs[:14], refs[14:])
    attn_sum, mlp_sum, vector_all, square, input_grad = given[:5]
    states = given[5:]
    out[0][...] = input_grad[...]
    grad_norm = jnp.sqrt(square[0:1, 0:1])
    out[1][...] = grad_norm
    factor = jnp.minimum(1.0, clip_norm / (grad_norm + 1e-06))
    start = lax.axis_index("dp") * 6
    vector_sum = pltpu.roll(vector_all[...], lax.rem(768 - start, 768), 1)[:, :128].T[:6, :12]
    sums = (attn_sum[...], mlp_sum[...], vector_sum)
    rates = ((learn_rate, weight_decay), (learn_rate, weight_decay), (vector_rate, 0.0))
    for n in range(3):
        out[2 + n][...] = sums[n]
        clip = factor.reshape(1, 1, 1) if n == 1 else factor
        new = adam_update(
            states[n][...], sums[n], states[3 + n][...], states[6 + n][...], clip, *rates[n]
        )
        for k in range(3):
            out[5 + 3 * k + n][...] = new[k]


def close(*given):
    vmem = pl.BlockSpec(memory_space=pltpu.VMEM)
    kinds = [(6, 3072), (6, 2, 3072), (6, 12)]
    shapes = [(384, 768), (1, 1)] + kinds * 4
    return pl.pallas_call(
        close_kernel,
        out_shape=[jax.ShapeDtypeStruct(shape, single) for shape in shapes],
        in_specs=[vmem] * 14,
        out_specs=[vmem] * 14,
        compiler_params=pltpu.CompilerParams(vmem_limit_bytes=63 * 2**20),
        name="close_step",
    )(*given)


def shards(
    text_input,
    caption_lengths,
    image_tokens,
    image_attn,
    image_mlp,
    image_vectors,
    attn_master,
    mlp_master,
    vector_master,
    attn_first,
    mlp_first,
    vector_first,
    attn_second,
    mlp_second,
    vector_second,
):
    mlp_master, mlp_first, mlp_second = (
        jnp.swapaxes(values, 0, 1) for values in (mlp_master, mlp_first, mlp_second)
    )
    vector_master, vector_first, vector_second = (
        values.T for values in (vector_master, vector_first, vector_second)
    )
    input_grad, attn_sum, mlp_sum, vector_all, square_total = train_step(
        caption_lengths.T,
        text_input,
        image_tokens,
        image_attn,
        image_mlp,
        image_vectors,
        attn_master,
        mlp_master,
        vector_master,
    )
    out = close(
        attn_sum,
        mlp_sum,
        vector_all,
        square_total,
        input_grad,
        attn_master,
        mlp_master,
        vector_master,
        attn_first,
        mlp_first,
        vector_first,
        attn_second,
        mlp_second,
        vector_second,
    )
    turned = [jnp.swapaxes(value, 0, 1) if n % 3 else value for n, value in enumerate(out[2:])]
    return (out[0], out[1].reshape(()), *turned)


def solution(mesh):
    in_specs = (
        P("dp", None),
        P("dp", None),
        P("dp", None),
        P(),
        P(),
        P(),
        P("dp", None),
        P(None, "dp", None),
        P(None, "dp"),
        P("dp", None),
        P(None, "dp", None),
        P(None, "dp"),
        P("dp", None),
        P(None, "dp", None),
        P(None, "dp"),
    )
    out_specs = (
        P("dp", None),
        P(),
        P("dp", None),
        P(None, "dp", None),
        P(None, "dp"),
        P("dp", None),
        P(None, "dp", None),
        P(None, "dp"),
        P("dp", None),
        P(None, "dp", None),
        P(None, "dp"),
        P("dp", None),
        P(None, "dp", None),
        P(None, "dp"),
    )
    return jax.shard_map(shards, mesh=mesh, in_specs=in_specs, out_specs=out_specs, check_vma=False)
```

```python
import jax
import jax.numpy as jnp
from jax import lax
from jax.experimental import pallas as pl
from jax.experimental.pallas import tpu as pltpu
from jax.sharding import PartitionSpec as P

STEP = 10


logit_scale = 60.0
clip_norm = 0.01
learn_rate = 0.05
vector_rate = 0.3
beta_first = 0.9
beta_second = 0.999
adam_epsilon = 1e-08
weight_decay = 0.1
bfloat = jnp.bfloat16
single = jnp.float32


def unit_rows(values):
    return values * lax.rsqrt(jnp.sum(values * values, -1, keepdims=True) + 1e-06)


def sum_squares(arrays):
    return sum((jnp.sum(member * member) for member in arrays))


def adam_update(weight, gradient, first_moment, second_moment, factor, rate, decay_rate):
    clipped = gradient * factor
    first_new = beta_first * first_moment + (1.0 - beta_first) * clipped
    second_new = beta_second * second_moment + (1.0 - beta_second) * clipped * clipped
    ratio = (
        first_new
        / (1.0 - beta_first**STEP)
        / (jnp.sqrt(second_new / (1.0 - beta_second**STEP)) + adam_epsilon)
    )
    return (first_new, second_new, weight - rate * (ratio + decay_rate * weight))


MESH = pl.DeviceIdType.MESH
LINES = 144
SHARD = 448
SUM_COPIES = 80
TURNS = (1, 3, 2)


def place():
    me = lax.axis_index("dp")
    return (me // 32, lax.rem(me // 8, 4), lax.rem(me // 2, 4), lax.rem(me, 2))


def device(x, z, y, c):
    return ((x * 4 + z) * 4 + y) * 2 + c


def plus(index, step):
    return lax.rem(index + step, 4)


def made(item):
    return item() if callable(item) else item


class Copy:
    def __init__(self, wire, slot, source, target, to):
        self.wire, self.slot, self.parts = (wire, slot, (source, target, to))

    def make(self):
        source, target, to = (made(part) for part in self.parts)
        return pltpu.make_async_remote_copy(
            src_ref=source,
            dst_ref=target,
            send_sem=self.wire.send_sems.at[self.slot],
            recv_sem=self.wire.recv_sems.at[self.slot],
            device_id=(to,),
            device_id_type=MESH,
        )

    def wait_recv(self):
        self.make().wait_recv()

    def wait_send(self):
        self.make().wait_send()


class Wire:
    def __init__(self, send_sems, recv_sems):
        self.send_sems, self.recv_sems, self.count, self.open = (send_sems, recv_sems, 0, [])

    def send(self, source, target, to):
        copy = Copy(self, self.count, source, target, to)
        copy.make().start()
        self.count += 1
        self.open.append(copy)
        return copy

    def clear(self, copies):
        for copy in copies:
            copy.wait_send()
        self.open = [copy for copy in self.open if not any(copy is other for other in copies)]

    def drain(self):
        self.clear(self.open)


def await_all(copies):
    for copy in copies:
        copy.wait_recv()


def greet(peers):
    for peer in peers:
        pl.semaphore_signal(
            pltpu.get_barrier_semaphore(), inc=1, device_id=(peer,), device_id_type=MESH
        )


def greeted(peers):
    pl.semaphore_wait(pltpu.get_barrier_semaphore(), len(peers))


class Ring:
    def __init__(self, wire, peer, view):
        self.wire, self.peer, self.view = (wire, peer, view)
        self.ahead = self.pass_on(0, None, 1)
        self.behind = self.pass_on(0, None, 3)

    def pass_on(self, k, part, step):
        block = lambda: self.view(k, part)
        return self.wire.send(block, block, lambda: self.peer(step))

    def forward(self):
        self.ahead.wait_recv()
        self.low = self.pass_on(3, 0, 1)
        self.behind.wait_recv()
        self.high = self.pass_on(1, 1, 3)

    def finish(self):
        self.low.wait_recv()
        self.high.wait_recv()


def aligned(start, size):
    return pl.ds(pl.multiple_of(start, 128), size)


def halves(start, size, part):
    if part is None:
        return aligned(start, size)
    low = size // 256 * 128
    return aligned(start, low) if part == 0 else aligned(start + low, size - low)


class Gather:
    def __init__(self, wire, peers, here, weight, turned, lines, natural, small):
        self.wire, self.here, self.weight, self.turned = (wire, here, weight, turned)
        self.lines, self.natural, self.small = (lines, natural, small)
        self.peers_x, self.peers_z, self.peers_y, self.sibling = peers
        x, z, y, c = here
        self.half, self.quarter = (c * 1536, (c * 4 + y) * 384)
        self.across = ([], [], [])

    def span(self, m):
        return (pl.ds(0, 160), pl.ds(160, 144), pl.ds(304, 144))[m]

    def begin(self):
        x, z, y, c = self.here
        self.first = {}
        for m in (2, 0, 1):
            view = lambda m=m: self.lines.at[c, y, self.span(m)]
            self.first[m] = [self.wire.send(view, view, lambda k=k: self.peers_y(k)) for k in TURNS]

    def swap(self):
        x, z, y, c = self.here
        self.swaps = {}
        for m in (2, 0, 1):
            await_all(self.first[m])
            view = lambda m=m: self.lines.at[c, :, self.span(m)]
            self.swaps[m] = self.wire.send(view, view, self.sibling)

    def spread(self, m):
        x, z, y, c = self.here
        self.swaps[m].wait_recv()
        for s in range(8):
            self.natural[s * LINES : (s + 1) * LINES] = self.lines[
                s % 2, s // 2, 16 + m * LINES : 16 + (m + 1) * LINES
            ].astype(single)
        start, count = (c * 12, 12) if m < 2 else ((c * 4 + y) * 3, 3)
        for j in range(count):
            self.weight[m, x, z, :, aligned((start + j) * 128, 128)] = self.natural[
                pl.ds(start + j, 48, stride=24), :
            ].astype(bfloat)

    def ring(self, peer, view):
        return Ring(self.wire, peer, view)

    def attn_x(self):
        x, z, y, c = self.here
        return self.ring(
            self.peers_x,
            lambda k, part: self.weight.at[0, plus(x, k), z, :, halves(self.half, 1536, part)],
        )

    def attn_z(self, b):
        x, z, y, c = self.here
        return self.ring(
            self.peers_z,
            lambda k, part: self.weight.at[
                0, plus(x, b), plus(z, k), :, halves(self.half, 1536, part)
            ],
        )

    def up_z(self):
        x, z, y, c = self.here
        return self.ring(
            self.peers_z,
            lambda k, part: self.weight.at[1, x, plus(z, k), :, halves(self.half, 1536, part)],
        )

    def up_x(self, b):
        x, z, y, c = self.here
        return self.ring(
            self.peers_x,
            lambda k, part: self.weight.at[
                1, plus(x, k), plus(z, b), :, halves(self.half, 1536, part)
            ],
        )

    def down_x(self):
        x, z, y, c = self.here
        return self.ring(
            self.peers_x,
            lambda k, part: self.weight.at[2, plus(x, k), z, :, halves(self.quarter, 384, part)],
        )

    def down_z(self, b):
        x, z, y, c = self.here
        return self.ring(
            self.peers_z,
            lambda k, part: self.weight.at[
                2, plus(x, b), plus(z, k), :, halves(self.quarter, 384, part)
            ],
        )

    def down_y(self, b):
        x, z, y, c = self.here
        return self.ring(
            self.peers_y,
            lambda k, part: self.weight.at[
                2, plus(x, b), :, :, halves((c * 4 + plus(y, k)) * 384, 384, part)
            ],
        )

    def spread_all(self):
        x, z, y, c = self.here
        self.spread(2)
        self.c1 = self.down_x()
        self.c2 = {0: self.down_z(0)}
        self.spread(0)
        self.a1 = self.attn_x()
        self.spread(1)
        self.b1 = self.up_z()
        for s in range(8):
            self.small[s * 6 : (s + 1) * 6] = self.lines[s % 2, s // 2, 0:16].astype(single)[0:6]
        self.turned[x, z] = self.small[...].astype(bfloat)
        view = lambda: self.turned.at[x, z]
        self.turn_x = [self.wire.send(view, view, lambda k=k: self.peers_x(k)) for k in TURNS]

    def near_down(self):
        self.c1.forward()
        for b in (3, 1):
            self.c2[b] = self.down_z(b)
        self.a2 = {0: self.attn_z(0)}
        self.b2 = {0: self.up_x(0)}

    def near_others(self):
        self.a1.forward()
        self.b1.forward()
        self.c2[0].forward()

    def far_down(self):
        self.c1.finish()
        self.c2[2] = self.down_z(2)
        self.c2[0].finish()
        self.c3 = {0: self.down_y(0)}

    def second_start(self):
        for b in (3, 1):
            self.c2[b].forward()
        for b in (3, 1):
            self.a2[b] = self.attn_z(b)
            self.b2[b] = self.up_x(b)
        x, z, y, c = self.here
        await_all(self.turn_x)
        view = lambda: self.turned.at[:, z]
        self.turn_z = [self.wire.send(view, view, lambda k=k: self.peers_z(k)) for k in TURNS]

    def far_others(self):
        self.a1.finish()
        self.a2[2] = self.attn_z(2)
        self.b1.finish()
        self.b2[2] = self.up_x(2)
        self.a2[0].forward()
        self.b2[0].forward()

    def down_near(self):
        for b in (3, 1):
            self.c2[b].finish()
            self.c3[b] = self.down_y(b)
        self.c2[2].forward()

    def down_far(self):
        self.c3[0].forward()
        self.c2[2].finish()
        self.c3[2] = self.down_y(2)

    def second_near(self):
        for b in (3, 1):
            self.a2[b].forward()
            self.b2[b].forward()

    def own_end(self):
        self.finish_attn(0)
        self.finish_up(0)

    def third_near(self):
        for b in (3, 1):
            self.c3[b].forward()
        self.finish_down(0)

    def second_far(self):
        self.a2[2].forward()
        self.b2[2].forward()

    def near_end(self):
        for b in (3, 1):
            self.finish_attn(b)
            self.finish_up(b)

    def third_far(self):
        self.c3[2].forward()

    def down_end(self):
        for b in (3, 1):
            self.finish_down(b)

    def finish_attn(self, b):
        x, z, y, c = self.here
        self.a2[b].finish()
        self.cross(0, lambda: self.weight.at[0, plus(x, b), :, :, aligned(self.half, 1536)])

    def finish_up(self, b):
        x, z, y, c = self.here
        self.b2[b].finish()
        self.cross(1, lambda: self.weight.at[1, :, plus(z, b), :, aligned(self.half, 1536)])

    def finish_down(self, b):
        x, z, y, c = self.here
        self.c3[b].finish()
        self.cross(2, lambda: self.weight.at[2, plus(x, b), :, :, aligned(self.half, 1536)])

    def cross(self, m, view):
        self.across[m].append(self.wire.send(view, view, self.sibling))

    def end(self, m):
        await_all(self.across[m])


def matmul(left, right):
    return jnp.dot(left, right, preferred_element_type=single)


def matmul_nt(left, right):
    return lax.dot_general(left, right, (((1,), (1,)), ((), ())), preferred_element_type=single)


def matmul_tn(left, right):
    return lax.dot_general(left, right, (((0,), (0,)), ((), ())), preferred_element_type=single)


def normalized(values):
    center = jnp.mean(values, -1, keepdims=True)
    shifted = values - center
    spread = jnp.mean(shifted * shifted, -1, keepdims=True)
    inverse = lax.rsqrt(spread + 1e-06)
    return (shifted * inverse, inverse)


def normalized_back(cotangent, unit, inverse, gain):
    scaled = cotangent * gain
    center = jnp.mean(scaled, -1, keepdims=True)
    along = jnp.mean(scaled * unit, -1, keepdims=True)
    return inverse * (scaled - center - unit * along)


def gelu_parts(hidden):
    squared = hidden * hidden
    angle = jnp.tanh(hidden * (0.7978845608028654 + 0.035677408136300125 * squared))
    return (squared, angle)


def even_lanes(rows):
    return lax.broadcasted_iota(jnp.int32, (rows, 128), 1) < 64


def split_heads(values):
    even = even_lanes(values.shape[0])
    zero = jnp.zeros_like(values)
    return jnp.concatenate([jnp.where(even, values, zero), jnp.where(even, zero, values)], 0)


def join_heads(values):
    rows = values.shape[0] // 2
    return jnp.where(even_lanes(rows), values[:rows], values[rows:])


def pair_weights(queries, key_rows, bias):
    scores = matmul_nt(split_heads(queries * 0.125), key_rows)
    scores = scores + jnp.concatenate([bias, bias], 0)
    weights = jnp.exp(scores - jnp.max(scores, -1, keepdims=True))
    return (weights, 1.0 / jnp.sum(weights, -1, keepdims=True))


def attend_images(qkv, attended, bias):
    starts = (0, 96, 192, 288)
    rows = lax.broadcasted_iota(jnp.int32, (16, 128), 0)

    @pl.loop(0, 6, unroll=3)
    def _(p):
        out = []
        for w, start in enumerate(starts):
            window = slice(start, start + 112)
            weights, scale = pair_weights(
                qkv[window, aligned(p * 128, 128)], qkv[window, aligned((6 + p) * 128, 128)], bias[w]
            )
            values = qkv[window, aligned((12 + p) * 128, 128)]
            out.append(join_heads(matmul(weights.astype(bfloat), values) * scale))
        lanes = aligned(p * 128, 128)
        attended[0:96, lanes] = out[0][0:96].astype(bfloat)
        for w in range(1, 4):
            edge = jnp.where(rows < 4 * w, out[w - 1][96:112], out[w][0:16])
            attended[starts[w] : starts[w] + 16, lanes] = edge.astype(bfloat)
            stop = 112 if w == 3 else 96
            attended[starts[w] + 16 : starts[w] + stop, lanes] = out[w][16:stop].astype(bfloat)


class UnitGather:
    def __init__(self, wire, peers, here, units, own, images, first, count):
        self.wire, self.here, self.units, self.own, self.images = (wire, here, units, own, images)
        self.peers_x, self.peers_z, self.peers_y, self.sibling = peers
        self.first, self.count, self.step = (first, count, 0)

    def swap(self):
        c = self.here[3]
        rows = pl.ds(self.first, self.count)
        self.own[c, rows] = self.units[rows, :]
        self.swapped = self.wire.send(self.own.at[c, rows], self.own.at[c, rows], self.sibling)

    def begin(self):
        x, z, y, c = self.here
        self.swapped.wait_recv()
        lanes = aligned(c * 384, 384)
        for first in range(self.first, self.first + self.count, 8):
            both = [self.own[core, first : first + 8, lanes] for core in range(2)]
            self.images[x, z, y, 2 * first : 2 * first + 16, lanes] = jnp.concatenate(both, 0).astype(
                bfloat
            )
        self.start()

    def start(self):
        x, z, y, c = self.here
        here = {"x": x, "z": z, "y": y}
        peer = {"x": self.peers_x, "z": self.peers_z, "y": self.peers_y}
        rows = pl.ds(2 * self.first, 2 * self.count)
        self.sent = []
        for o, order in enumerate(("yzx", "zxy", "xyz")):
            index = [slice(None) if n in order[: self.step] else here[n] for n in "xzy"]
            view = self.images.at[(*index, rows, aligned((c * 3 + o) * 128, 128))]
            self.sent += [self.wire.send(view, view, peer[order[self.step]](k)) for k in TURNS]
        self.step += 1

    def next(self):
        await_all(self.sent)
        self.start()

    def finish(self):
        await_all(self.sent)
        rows = pl.ds(2 * self.first, 2 * self.count)
        mine = self.images.at[:, :, :, rows, aligned(self.here[3] * 384, 384)]
        self.crossed = self.wire.send(mine, mine, self.sibling)

    def end(self):
        self.crossed.wait_recv()


def image_bias(bias):
    for w in range(4):
        first = 96 * w
        query = (lax.broadcasted_iota(jnp.int32, (112, 112), 0) + first) // 50
        key = (lax.broadcasted_iota(jnp.int32, (112, 112), 1) + first) // 50
        bias[w] = jnp.where(query == key, 0.0, -1e30)


def image_chunk(t, tokens, weight, vec, normed, qkv, attended, residual, bias, units, hook):
    lanes_t = slice(t * 768, (t + 1) * 768)
    unit, _ = normalized(tokens[:, lanes_t].astype(single))
    normed[...] = (unit * vec[0:1] + vec[1:2]).astype(bfloat)
    hook()
    for n, shift in enumerate((4, None, 5)):
        triple = matmul(normed[...], weight(0, n * 768, 768))
        if shift is not None:
            triple = triple + vec[shift : shift + 1]
        qkv[:, n * 768 : (n + 1) * 768] = triple.astype(bfloat)
    hook()
    attend_images(qkv, attended, bias)
    hook()
    residual[...] = (
        tokens[:, lanes_t].astype(single) + matmul(attended[...], weight(0, 2304, 768)) + vec[6:7]
    )
    unit, _ = normalized(residual[...])
    normed[...] = (unit * vec[2:3] + vec[3:4]).astype(bfloat)
    residual[...] = residual[...] + vec[7:8]
    hook()
    for f in range(4):
        hidden = matmul(normed[...], weight(1, f * 768, 768)) + vec[8 + f : 9 + f]
        _, angle = gelu_parts(hidden)
        active = (0.5 * hidden * (1.0 + angle)).astype(bfloat)
        residual[...] = residual[...] + matmul_nt(active, weight(2, f * 768, 768))
        hook()
    image = lax.broadcasted_iota(jnp.int32, (8, 400), 0)
    token = lax.broadcasted_iota(jnp.int32, (8, 400), 1)
    member = (token // 50 == image).astype(bfloat)
    high = residual[...].astype(bfloat)
    low = (residual[...] - high.astype(single)).astype(bfloat)
    pooled = (matmul(member, high) + matmul(member, low)) * (1.0 / 50.0)
    units[t * 8 : (t + 1) * 8, :] = unit_rows(pooled)


PLAN = {
    (0, 2): "swap",
    (0, 4): "spread_all",
    (0, 6): "near_down",
    (0, 7): "near_others",
    (1, 1): "far_down",
    (1, 2): "second_start",
    (1, 3): "far_others",
    (1, 4): "down_near",
    (1, 6): "down_far",
    (2, 0): "second_near",
    (2, 1): "own_end",
    (2, 2): "third_near",
    (2, 4): "second_far",
    (2, 5): "near_end",
    (2, 6): "third_far",
    (2, 7): "down_end",
}


def slot_codes(index, ends, window):
    later = index >= 64
    position = jnp.where(later, index - 64, index)
    slots = [
        sum((position >= ends[2 * window + r][k]).astype(jnp.int32) for k in range(4)) for r in (0, 1)
    ]
    return jnp.where(later, slots[1] + 8, slots[0])


def text_masks(lengths, bias):
    ends = []
    for r in range(6):
        row, end = ([], 0)
        for k in range(4):
            end = end + lengths[k, r]
            row.append(end)
        ends.append(row)
    codes = []
    for w in range(3):
        query = slot_codes(lax.broadcasted_iota(jnp.int32, (128, 128), 0), ends, w)
        key = slot_codes(lax.broadcasted_iota(jnp.int32, (128, 128), 1), ends, w)
        bias[w] = jnp.where(query == key, 0.0, -1e30)
        code = slot_codes(lax.broadcasted_iota(jnp.int32, (24, 128), 1), ends, w)
        slot = jnp.where(code >= 8, code - 8, code)
        caption = 8 * w + jnp.where(code >= 8, 4, 0) + slot
        codes.append(jnp.where(slot < 4, caption, -1))
    caption = jnp.concatenate(codes, 1)
    return (caption == lax.broadcasted_iota(jnp.int32, (24, 384), 0)).astype(single)


def attend_text(qkv, attended, probs, bias):
    @pl.loop(0, 6, unroll=3)
    def _(p):
        for w in range(3):
            window = slice(w * 128, (w + 1) * 128)
            weights, scale = pair_weights(
                qkv[window, aligned(p * 128, 128)], qkv[window, aligned((6 + p) * 128, 128)], bias[w]
            )
            pair = weights * scale
            probs[pl.ds(pl.multiple_of((p * 3 + w) * 256, 256), 256)] = pair
            out = matmul(pair.astype(bfloat), qkv[window, aligned((12 + p) * 128, 128)])
            attended[window, aligned(p * 128, 128)] = join_heads(out).astype(bfloat)


def attend_text_back(qkv, probs, attended_grad, triple_grad):
    @pl.loop(0, 6, unroll=3)
    def _(p):
        for w in range(3):
            window = slice(w * 128, (w + 1) * 128)
            at = [aligned((6 * n + p) * 128, 128) for n in range(3)]
            queries, key_rows, value_rows = (qkv[window, lanes] for lanes in at)
            grads = split_heads(attended_grad[window, at[0]])
            pair = probs[pl.ds(pl.multiple_of((p * 3 + w) * 256, 256), 256)]
            value_grad = matmul_tn(pair.astype(bfloat), grads)
            prob_grad = matmul_nt(grads, value_rows)
            along = jnp.sum(pair * prob_grad, -1, keepdims=True)
            score_grad = (pair * (prob_grad - along) * 0.125).astype(bfloat)
            query_grad = join_heads(matmul(score_grad, key_rows))
            key_grad = matmul_tn(score_grad, split_heads(queries))
            triple_grad[window, at[0]] = query_grad.astype(bfloat)
            triple_grad[window, at[1]] = key_grad.astype(bfloat)
            triple_grad[window, at[2]] = value_grad.astype(bfloat)


def column_sums(values):
    return jnp.sum(values.astype(single), 0, keepdims=True)


def step_kernel(
    lengths,
    tokens_ref,
    image_ref,
    image_attn_ref,
    image_mlp_ref,
    image_vec,
    attn_ref,
    mlp_ref,
    vector_ref,
    input_grad,
    attn_out,
    mlp_out,
    vector_out,
    square_out,
    weight,
    store,
    tokens,
    bias,
    image_masks,
    units,
    probs,
    normed,
    qkv,
    attended,
    residual,
    normed_two,
    active,
    slope,
    triple_grad,
    flow,
    part_sum,
    images,
    own,
    lines,
    small,
    turned,
    vec,
    row_part,
    row_near,
    row_far,
    late_x,
    late_z,
    down_x,
    down_z,
    whole,
    last,
    flat,
    third,
    packed,
    pieces,
    landed,
    sums,
    vec_c,
    vec_z,
    vec_x,
    vec_y,
    square,
    near,
    far,
    load_sems,
    send_sems,
    recv_sems,
):
    x, z, y, c = place()
    peers_x = lambda k: device(plus(x, k), z, y, c)
    peers_z = lambda k: device(x, plus(z, k), y, c)
    peers_y = lambda k: device(x, z, plus(y, k), c)
    sibling = device(x, z, y, 1 - c)
    group = [(k, d) for k in range(4) for d in range(2) if (k, d) != (0, 0)]
    plane = [(i, j) for i in range(4) for j in range(4) if (i, j) != (0, 0)]
    group_peer = lambda k, d: device(x, z, plus(y, k), lax.rem(c + d, 2))
    plane_peer = lambda i, j: device(plus(x, i), plus(z, j), y, c)
    wire = Wire(send_sems, recv_sems)
    turns = TURNS

    held = store.at[:, :, :, :, 0:1536]
    low, high = (slice(0, 768), slice(768, 1536))
    from_z = [[store.at[m, k, :, :, 1536:2304] for k in range(3)] for m in range(2)]
    from_x = [[store.at[m, k, :, :, 2304:3072] for k in range(3)] for m in range(2)]
    from_y = [store.at[2, :, :, :, 1536 + 384 * k : 1920 + 384 * k] for k in range(3)]
    total_z = [store.at[m, 3, :, :, 1536:2304] for m in range(2)]
    total_x = [store.at[m, 3, :, :, 2304:3072] for m in range(2)]
    total_y = store.at[2, :, :, :, 2688:3072]

    loads = [
        pltpu.make_async_copy(source, target, load_sems.at[n])
        for n, (source, target) in enumerate(
            [
                (image_ref.at[0:400], slope.at[:, 0:768]),
                (image_attn_ref, store.at[0]),
                (image_mlp_ref, store.at[1:3]),
                (image_ref.at[400:800], slope.at[:, 768:1536]),
                (image_ref.at[800:1200], slope.at[:, 1536:2304]),
                (tokens_ref, tokens),
            ]
        )
    ]
    for load in loads:
        load.start()
    others = [group_peer(*g) for g in group] + [plane_peer(*p) for p in plane]
    greet(others)
    natural, line = (probs.at[0:1152], [probs.at[1152 + 144 * m : 1296 + 144 * m] for m in range(3)])
    small[0:16] = jnp.zeros((16, 128), single)
    small[0:6, 0:12] = vector_ref[...]
    lines[c, y, 0:16] = small[0:16].astype(bfloat)
    for m in range(3):
        for j in range(24):
            columns = slice(j * 128, (j + 1) * 128)
            rows = attn_ref[:, columns] if m == 0 else mlp_ref[:, m - 1, columns]
            line[m][pl.ds(j, 6, stride=24), :] = rows
        lines[c, y, 16 + m * LINES : 16 + (m + 1) * LINES] = line[m][...].astype(bfloat)
    greeted(others)
    peers = (peers_x, peers_z, peers_y, sibling)
    unit_gather = UnitGather(wire, peers, (x, z, y, c), units, own, images, 0, 24)
    gather = Gather(
        wire, peers, (x, z, y, c), weight, turned, lines, natural, small
    )
    gather.begin()
    image_bias(image_masks)
    for load in loads:
        load.wait()
    plan = PLAN
    image_weight = lambda m, first, size: store[m, :, :, :, first : first + size].reshape(768, size)

    for t in range(3):
        points = iter(range(99))

        def hook():
            for name in plan.get((t, next(points)), "").split():
                getattr(gather, name)()

        image_chunk(
            t, slope, image_weight, image_vec, normed, qkv, attended, residual, image_masks, units, hook
        )

    unit_gather.swap()
    gather.finish_attn(2)
    gather.finish_up(2)
    member = text_masks(lengths, bias)
    unit_gather.begin()
    await_all(gather.turn_z)
    vec[...] = turned[...].reshape(768, 128).astype(single).T[0:16]

    normed, qkv, attended, residual, slope = (
        ref.at[0:384] for ref in (normed, qkv, attended, residual, slope)
    )
    unit_one, _ = normalized(tokens[...].astype(single))
    normed[...] = (unit_one * vec[0:1] + vec[1:2]).astype(bfloat)
    gather.end(0)
    attn = lambda first, size: weight[0, :, :, :, first : first + size].reshape(768, size)
    for n, shift in enumerate((4, None, 5)):
        triple = matmul(normed[...], attn(n * 768, 768))
        if shift is not None:
            triple = triple + vec[shift : shift + 1]
        qkv[:, n * 768 : (n + 1) * 768] = triple.astype(bfloat)
    unit_gather.next()
    gather.finish_down(2)
    attend_text(qkv, attended, probs, bias)
    residual[...] = tokens[...].astype(single) + matmul(attended[...], attn(2304, 768)) + vec[6:7]
    unit_two, _ = normalized(residual[...])
    normed_two[...] = (unit_two * vec[2:3] + vec[3:4]).astype(bfloat)
    unit_gather.next()
    gather.end(1)
    for f in range(4):
        lanes = slice(f * 768, (f + 1) * 768)
        hidden = matmul(normed_two[...], weight[1, :, :, :, lanes].reshape(768, 768)) + vec[8 + f : 9 + f]
        squared, angle = gelu_parts(hidden)
        active[:, lanes] = (0.5 * hidden * (1.0 + angle)).astype(bfloat)
        curve = 0.7978845608028654 + 0.10703222440890037 * squared
        slope[:, lanes] = (
            0.5 * (1.0 + angle) + 0.5 * hidden * (1.0 - angle * angle) * curve
        ).astype(bfloat)
    gather.end(2)
    flow[...] = residual[...] + vec[7:8]
    for f in range(4):
        lanes = slice(f * 768, (f + 1) * 768)
        flow[...] = flow[...] + matmul_nt(
            active[:, lanes], weight[2, :, :, :, lanes].reshape(768, 768)
        )
    unit_gather.finish()
    highest = lax.Precision.HIGHEST
    per_length = 1.0 / jnp.sum(member, -1, keepdims=True)
    pooled = per_length * jnp.dot(member, flow[...], precision=highest, preferred_element_type=single)

    scale = lax.rsqrt(jnp.sum(pooled * pooled, -1, keepdims=True) + 1e-06)
    unit = pooled * scale
    unit_gather.end()
    every = images[...].reshape(3072, 768)
    logits = logit_scale * matmul_nt(unit.astype(bfloat), every)
    powers = jnp.exp(logits)
    column = jnp.sum(powers, 1, keepdims=True)
    rows = jnp.sum(powers, 0, keepdims=True)
    for k in range(8):
        row_part[k : k + 1, :] = rows[:, k * 384 : (k + 1) * 384]
    row_near[y, c] = row_part[...]
    wire.count = max(wire.count, SUM_COPIES)
    sent = [wire.send(row_part, row_near.at[y, c], group_peer(*g)) for g in group]
    caption = lax.broadcasted_iota(jnp.int32, (24, 3072), 0) + lax.axis_index("dp") * 24
    at = lax.broadcasted_iota(jnp.int32, (24, 3072), 1)
    inside = at % 48
    image = at - inside + inside // 8 % 2 * 24 + inside // 16 * 8 + inside % 8
    same = (caption == image).astype(single)
    of_column = powers / column - 2.0 * same
    await_all(sent)
    row_far[x, z] = sum(row_near[k, d] for k in range(4) for d in range(2))
    sent = [wire.send(row_far.at[x, z], row_far.at[x, z], plane_peer(*p)) for p in plane]
    await_all(sent)
    total = sum(row_far[i, j] for i in range(4) for j in range(4))
    every_row = jnp.concatenate([total[k : k + 1] for k in range(8)], 1)
    logit_grad = (logit_scale / (2.0 * 3072) * (powers / every_row + of_column)).astype(bfloat)
    unit_grad = matmul(logit_grad, every)
    pooled_grad = scale * (unit_grad - unit * jnp.sum(unit * unit_grad, -1, keepdims=True))
    flow[...] = lax.dot_general(
        member,
        pooled_grad * per_length,
        (((0,), (0,)), ((), ())),
        precision=highest,
        preferred_element_type=single,
    )

    sends = {}

    def block_grad(left, right):
        return matmul_tn(left, right).reshape(4, 4, 48, right.shape[1])

    def other_half(m, make):
        for i in range(2):
            place_i = images.at[:, :, 2 * (m % 2) + i]
            place_i[...] = make((1 - c) * 1536 + i * 768, i).astype(bfloat)
            sends[m, i] = wire.send(
                place_i, held.at[m, :, :, :, i * 768 : (i + 1) * 768], sibling
            )

    def own_half(m, make):
        for i in range(2):
            sends[m, i].wait_recv()
            lanes = slice(i * 768, (i + 1) * 768)
            held[m, :, :, :, lanes] = (
                make(c * 1536 + i * 768, i) + held[m, :, :, :, lanes].astype(single)
            ).astype(bfloat)

    wire.drain()
    wire.count = 0

    def add(base, parts):
        return base.astype(single) + sum(part.astype(single) for part in parts)

    def first_sums(m):
        return [
            [wire.send(held.at[m, :, plus(z, k), :, low], from_z[m][k - 1], peers_z(k)) for k in turns],
            [wire.send(held.at[m, plus(x, k), :, :, high], from_x[m][k - 1], peers_x(k)) for k in turns],
        ]

    def second_sums(m, sent):
        await_all(sent[0])
        for i in range(4):
            total_z[m][i] = add(held[m, i, z, :, low], [from_z[m][k][i] for k in range(3)]).astype(bfloat)
        over_x = [
            wire.send(total_z[m].at[plus(x, k)], late_x.at[m, k - 1], peers_x(k)) for k in turns
        ]
        await_all(sent[1])
        for i in range(4):
            total_x[m][i] = add(held[m, x, i, :, high], [from_x[m][k][i] for k in range(3)]).astype(bfloat)
        over_z = [
            wire.send(total_x[m].at[plus(z, k)], late_z.at[m, k - 1], peers_z(k)) for k in turns
        ]
        return (over_x, over_z)

    def whole_sums(m, sent):
        await_all(sent[0])
        whole[m, :, low] = add(total_z[m][x], [late_x[m, k] for k in range(3)])
        await_all(sent[1])
        whole[m, :, high] = add(total_x[m][z], [late_z[m, k] for k in range(3)])
        for j in range(12):
            flat[m, pl.ds(j, 48, stride=12), :] = whole[m, :, j * 128 : (j + 1) * 128]

    branch_two = triple_grad.at[:, 2304:3072]
    branch_two[...] = flow[...].astype(bfloat)
    vec_c[c] = jnp.zeros((16, 768), single)
    vec_c[c, 7:8] = column_sums(branch_two[...])
    make_two = lambda first, i: block_grad(branch_two[...], active[:, aligned(first, 768)])
    other_half(2, make_two)
    for f in range(4):
        lanes = slice(f * 768, (f + 1) * 768)
        active_grad = matmul(branch_two[...], weight[2, :, :, :, lanes].reshape(768, 768))
        hidden_grad = (active_grad * slope[:, lanes].astype(single)).astype(bfloat)
        slope[:, lanes] = hidden_grad
        vec_c[c, 8 + f : 9 + f] = column_sums(hidden_grad)
    make_one = lambda first, i: block_grad(normed_two[...], slope[:, aligned(first, 768)])
    other_half(1, make_one)
    for f in range(4):
        lanes = slice(f * 768, (f + 1) * 768)
        piece = matmul_nt(slope[:, lanes], weight[1, :, :, :, lanes].reshape(768, 768))
        part_sum[...] = piece if f == 0 else part_sum[...] + piece
    own_half(2, make_two)
    send_y = [
        wire.send(held.at[2, :, :, :, aligned(plus(y, k) * 384, 384)], from_y[k - 1], peers_y(k))
        for k in turns
    ]
    unit_two, inverse_two = normalized(residual[...])
    vec_c[c, 2:3] = jnp.sum(part_sum[...] * unit_two, 0, keepdims=True)
    vec_c[c, 3:4] = jnp.sum(part_sum[...], 0, keepdims=True)
    flow[...] = flow[...] + normalized_back(part_sum[...], unit_two, inverse_two, vec[2:3])
    triple_grad[:, 2304:3072] = flow[...].astype(bfloat)
    vec_c[c, 6:7] = column_sums(triple_grad[:, 2304:3072])
    own_half(1, make_one)
    send_one = first_sums(1)
    active[:, 0:768] = matmul_nt(triple_grad[:, 2304:3072], attn(2304, 768)).astype(bfloat)
    attend_text_back(qkv, probs, active, triple_grad)
    vec_c[c, 4:5] = column_sums(triple_grad[:, 0:768])
    vec_c[c, 5:6] = column_sums(triple_grad[:, 1536:2304])

    def make_zero(first, i):
        left = normed[...]
        if i == 1:
            left = jnp.where(first >= 2304, attended[...], left)
        return block_grad(left, triple_grad[:, aligned(first, 768)])

    wire.clear([sends[2, i] for i in range(2)])
    other_half(0, make_zero)
    for n in range(3):
        piece = matmul_nt(triple_grad[:, n * 768 : (n + 1) * 768], attn(n * 768, 768))
        part_sum[...] = piece if n == 0 else part_sum[...] + piece
    own_half(0, make_zero)
    send_zero = first_sums(0)
    unit_one, inverse_one = normalized(tokens[...].astype(single))
    vec_c[c, 0:1] = jnp.sum(part_sum[...] * unit_one, 0, keepdims=True)
    vec_c[c, 1:2] = jnp.sum(part_sum[...], 0, keepdims=True)
    vec_swap = wire.send(vec_c.at[c], vec_c.at[c], sibling)
    part_sum[...] = flow[...] + normalized_back(part_sum[...], unit_one, inverse_one, vec[0:1])
    leave = pltpu.make_async_copy(part_sum, input_grad, load_sems.at[6])
    leave.start()
    second_one = second_sums(1, send_one)
    vec_swap.wait_recv()
    vec_z[z] = vec_c[0] + vec_c[1]
    sent_vec_z = [wire.send(vec_z.at[z], vec_z.at[z], peers_z(k)) for k in turns]

    await_all(send_y)
    quarter = aligned(y * 384, 384)
    for i in range(4):
        for j in range(4):
            total_y[i, j] = add(
                held[2, i, j, :, quarter], [from_y[k][i, j] for k in range(3)]
            ).astype(bfloat)
    down_send_x = [wire.send(total_y.at[plus(x, k)], down_x.at[k - 1], peers_x(k)) for k in turns]
    await_all(sent_vec_z)
    vec_x[x] = vec_z[0] + vec_z[1] + vec_z[2] + vec_z[3]
    sent_vec_x = [wire.send(vec_x.at[x], vec_x.at[x], peers_x(k)) for k in turns]
    whole_sums(1, second_one)
    await_all(down_send_x)
    for j in range(4):
        last[j] = add(total_y[x, j], [down_x[k, j] for k in range(3)]).astype(bfloat)
    down_send_z = [wire.send(last.at[plus(z, k)], down_z.at[k - 1], peers_z(k)) for k in turns]
    await_all(sent_vec_x)
    vec_y[y] = vec_x[0] + vec_x[1] + vec_x[2] + vec_x[3]
    sent_vec_y = [wire.send(vec_y.at[y], vec_y.at[y], peers_y(k)) for k in turns]
    second_zero = second_sums(0, send_zero)
    await_all(down_send_z)
    ended = add(last[z], [down_z[k] for k in range(3)])
    for j in range(3):
        third[pl.ds(j, 48, stride=3), :] = ended[:, j * 128 : (j + 1) * 128]
    whole_sums(0, second_zero)
    packed[160:176] = jnp.zeros((16, 128), single)
    for s in range(8):
        packed[0:72] = flat[0, s * 72 : (s + 1) * 72]
        packed[72:144] = flat[1, s * 72 : (s + 1) * 72]
        packed[144:162] = third[s * 18 : (s + 1) * 18]
        pieces[s // 2, s % 2] = packed[...].astype(bfloat)
    landed[y, c] = pieces[y, c]
    piece_sent = [
        wire.send(pieces.at[plus(y, k), lax.rem(c + d, 2)], landed.at[y, c], group_peer(k, d))
        for k, d in group
    ]
    await_all(sent_vec_y)
    vec_total = vec_y[0] + vec_y[1] + vec_y[2] + vec_y[3]
    vector_out[...] = vec_total
    await_all(piece_sent)
    for h in range(2):
        for k in range(4):
            piece = landed[k, h].astype(single)
            packed[...] = piece if k == 0 else packed[...] + piece
            sums[...] = piece[144:168]
            for j in range(3):
                at = ((h * 4 + k) * 3 + j) * 128
                mlp_out[:, 1, at : at + 128] = sums[pl.ds(j, 6, stride=3), :]
        for j in range(12):
            at = (h * 12 + j) * 128
            attn_out[:, at : at + 128] = packed[pl.ds(j, 6, stride=12), :]
            mlp_out[:, 0, at : at + 128] = packed[pl.ds(72 + j, 6, stride=12), :]
    lanes = lax.broadcasted_iota(jnp.int32, (16, 768), 1)
    start = lax.axis_index("dp") * 6
    owned = jnp.where((lanes >= start) & (lanes < start + 6), vec_total, 0.0)
    squares = sum_squares((attn_out[...], mlp_out[...], owned))
    square[...] = jnp.broadcast_to(squares, (8, 128))
    near[y, c] = square[...]
    sent = [wire.send(square, near.at[y, c], group_peer(*g)) for g in group]
    await_all(sent)
    far[x, z] = sum(near[k, d] for k in range(4) for d in range(2))
    sent = [wire.send(far.at[x, z], far.at[x, z], plane_peer(*p)) for p in plane]
    await_all(sent)
    square_out[...] = sum(far[i, j] for i in range(4) for j in range(4))
    leave.wait()
    wire.drain()


def train_step(
    lengths, text, images, image_attn, image_mlp, image_vectors, attn_master, mlp_master, vector_master
):
    copies = 160
    vmem = pl.BlockSpec(memory_space=pltpu.VMEM)
    anywhere = pl.BlockSpec(memory_space=pl.ANY)
    return pl.pallas_call(
        step_kernel,
        out_shape=(
            jax.ShapeDtypeStruct((384, 768), single),
            jax.ShapeDtypeStruct((6, 3072), single),
            jax.ShapeDtypeStruct((6, 2, 3072), single),
            jax.ShapeDtypeStruct((16, 768), single),
            jax.ShapeDtypeStruct((8, 128), single),
        ),
        in_specs=[pl.BlockSpec(memory_space=pltpu.SMEM)] + [anywhere] * 4 + [vmem] * 4,
        out_specs=[anywhere] + [vmem] * 4,
        scratch_shapes=[
            pltpu.VMEM((3, 4, 4, 48, 3072), bfloat),
            pltpu.VMEM((3, 4, 4, 48, 3072), bfloat),
            pltpu.VMEM((384, 768), bfloat),
            pltpu.VMEM((3, 128, 128), single),
            pltpu.VMEM((4, 112, 112), single),
            pltpu.VMEM((24, 768), single),
            pltpu.VMEM((4608, 128), single),
            pltpu.VMEM((400, 768), bfloat),
            pltpu.VMEM((400, 2304), bfloat),
            pltpu.VMEM((400, 768), bfloat),
            pltpu.VMEM((400, 768), single),
            pltpu.VMEM((384, 768), bfloat),
            pltpu.VMEM((384, 3072), bfloat),
            pltpu.VMEM((400, 3072), bfloat),
            pltpu.VMEM((384, 3072), bfloat),
            pltpu.VMEM((384, 768), single),
            pltpu.VMEM((384, 768), single),
            pltpu.VMEM((4, 4, 4, 48, 768), bfloat),
            pltpu.VMEM((2, 24, 768), single),
            pltpu.VMEM((2, 4, SHARD, 128), bfloat),
            pltpu.VMEM((48, 128), single),
            pltpu.VMEM((4, 4, 48, 128), bfloat),
            pltpu.VMEM((16, 768), single),
            pltpu.VMEM((8, 384), single),
            pltpu.VMEM((4, 2, 8, 384), single),
            pltpu.VMEM((4, 4, 8, 384), single),
            pltpu.VMEM((2, 3, 48, 768), bfloat),
            pltpu.VMEM((2, 3, 48, 768), bfloat),
            pltpu.VMEM((3, 4, 48, 384), bfloat),
            pltpu.VMEM((3, 48, 384), bfloat),
            pltpu.VMEM((2, 48, 1536), single),
            pltpu.VMEM((4, 48, 384), bfloat),
            pltpu.VMEM((2, 576, 128), single),
            pltpu.VMEM((144, 128), single),
            pltpu.VMEM((176, 128), single),
            pltpu.VMEM((4, 2, 176, 128), bfloat),
            pltpu.VMEM((4, 2, 176, 128), bfloat),
            pltpu.VMEM((24, 128), single),
            pltpu.VMEM((2, 16, 768), single),
            pltpu.VMEM((4, 16, 768), single),
            pltpu.VMEM((4, 16, 768), single),
            pltpu.VMEM((4, 16, 768), single),
            pltpu.VMEM((8, 128), single),
            pltpu.VMEM((4, 2, 8, 128), single),
            pltpu.VMEM((4, 4, 8, 128), single),
            pltpu.SemaphoreType.DMA((7,)),
            pltpu.SemaphoreType.DMA((copies,)),
            pltpu.SemaphoreType.DMA((copies,)),
        ],
        compiler_params=pltpu.CompilerParams(
            collective_id=1, has_side_effects=True, vmem_limit_bytes=63 * 2**20
        ),
        name="train_step",
    )(
        lengths,
        text,
        images,
        image_attn.reshape(4, 4, 48, 3072),
        image_mlp.reshape(2, 4, 4, 48, 3072),
        image_vectors,
        attn_master,
        mlp_master,
        vector_master,
    )


def close_kernel(*refs):
    given, out = (refs[:14], refs[14:])
    attn_sum, mlp_sum, vector_all, square, input_grad = given[:5]
    states = given[5:]
    out[0][...] = input_grad[...]
    grad_norm = jnp.sqrt(square[0:1, 0:1])
    out[1][...] = grad_norm
    factor = jnp.minimum(1.0, clip_norm / (grad_norm + 1e-06))
    start = lax.axis_index("dp") * 6
    vector_sum = pltpu.roll(vector_all[...], lax.rem(768 - start, 768), 1)[:, :128].T[:6, :12]
    sums = (attn_sum[...], mlp_sum[...], vector_sum)
    rates = ((learn_rate, weight_decay), (learn_rate, weight_decay), (vector_rate, 0.0))
    for n in range(3):
        out[2 + n][...] = sums[n]
        clip = factor.reshape(1, 1, 1) if n == 1 else factor
        new = adam_update(
            states[n][...], sums[n], states[3 + n][...], states[6 + n][...], clip, *rates[n]
        )
        for k in range(3):
            out[5 + 3 * k + n][...] = new[k]


def close(*given):
    vmem = pl.BlockSpec(memory_space=pltpu.VMEM)
    kinds = [(6, 3072), (6, 2, 3072), (6, 12)]
    shapes = [(384, 768), (1, 1)] + kinds * 4
    return pl.pallas_call(
        close_kernel,
        out_shape=[jax.ShapeDtypeStruct(shape, single) for shape in shapes],
        in_specs=[vmem] * 14,
        out_specs=[vmem] * 14,
        compiler_params=pltpu.CompilerParams(vmem_limit_bytes=63 * 2**20),
        name="close_step",
    )(*given)


def shards(
    text_input,
    caption_lengths,
    image_tokens,
    image_attn,
    image_mlp,
    image_vectors,
    attn_master,
    mlp_master,
    vector_master,
    attn_first,
    mlp_first,
    vector_first,
    attn_second,
    mlp_second,
    vector_second,
):
    mlp_master, mlp_first, mlp_second = (
        jnp.swapaxes(values, 0, 1) for values in (mlp_master, mlp_first, mlp_second)
    )
    vector_master, vector_first, vector_second = (
        values.T for values in (vector_master, vector_first, vector_second)
    )
    input_grad, attn_sum, mlp_sum, vector_all, square_total = train_step(
        caption_lengths.T,
        text_input,
        image_tokens,
        image_attn,
        image_mlp,
        image_vectors,
        attn_master,
        mlp_master,
        vector_master,
    )
    out = close(
        attn_sum,
        mlp_sum,
        vector_all,
        square_total,
        input_grad,
        attn_master,
        mlp_master,
        vector_master,
        attn_first,
        mlp_first,
        vector_first,
        attn_second,
        mlp_second,
        vector_second,
    )
    turned = [jnp.swapaxes(value, 0, 1) if n % 3 else value for n, value in enumerate(out[2:])]
    return (out[0], out[1].reshape(()), *turned)


def solution(mesh):
    in_specs = (
        P("dp", None),
        P("dp", None),
        P("dp", None),
        P(),
        P(),
        P(),
        P("dp", None),
        P(None, "dp", None),
        P(None, "dp"),
        P("dp", None),
        P(None, "dp", None),
        P(None, "dp"),
        P("dp", None),
        P(None, "dp", None),
        P(None, "dp"),
    )
    out_specs = (
        P("dp", None),
        P(),
        P("dp", None),
        P(None, "dp", None),
        P(None, "dp"),
        P("dp", None),
        P(None, "dp", None),
        P(None, "dp"),
        P("dp", None),
        P(None, "dp", None),
        P(None, "dp"),
        P("dp", None),
        P(None, "dp", None),
        P(None, "dp"),
    )
    return jax.shard_map(shards, mesh=mesh, in_specs=in_specs, out_specs=out_specs, check_vma=False)
```

```python
import jax
import jax.numpy as jnp
from jax import lax
from jax.experimental import pallas as pl
from jax.experimental.pallas import tpu as pltpu
from jax.sharding import PartitionSpec as P

STEP = 10


logit_scale = 60.0
clip_norm = 0.01
learn_rate = 0.05
vector_rate = 0.3
beta_first = 0.9
beta_second = 0.999
adam_epsilon = 1e-08
weight_decay = 0.1
bfloat = jnp.bfloat16
single = jnp.float32


def unit_rows(values):
    return values * lax.rsqrt(jnp.sum(values * values, -1, keepdims=True) + 1e-06)


def sum_squares(arrays):
    return sum((jnp.sum(member * member) for member in arrays))


def adam_update(weight, gradient, first_moment, second_moment, factor, rate, decay_rate):
    clipped = gradient * factor
    first_new = beta_first * first_moment + (1.0 - beta_first) * clipped
    second_new = beta_second * second_moment + (1.0 - beta_second) * clipped * clipped
    ratio = (
        first_new
        / (1.0 - beta_first**STEP)
        / (jnp.sqrt(second_new / (1.0 - beta_second**STEP)) + adam_epsilon)
    )
    return (first_new, second_new, weight - rate * (ratio + decay_rate * weight))


MESH = pl.DeviceIdType.MESH
LINES = 144
SHARD = 448
SUM_COPIES = 80
ORDERS = ("yzx", "zxy", "xyz")
TURNS = (1, 3, 2)


def place():
    me = lax.axis_index("dp")
    return (me // 32, lax.rem(me // 8, 4), lax.rem(me // 2, 4), lax.rem(me, 2))


def device(x, z, y, c):
    return ((x * 4 + z) * 4 + y) * 2 + c


def plus(index, step):
    return lax.rem(index + step, 4)


def made(item):
    return item() if callable(item) else item


class Copy:
    def __init__(self, wire, slot, source, target, to):
        self.wire, self.slot, self.parts = (wire, slot, (source, target, to))

    def make(self):
        source, target, to = (made(part) for part in self.parts)
        return pltpu.make_async_remote_copy(
            src_ref=source,
            dst_ref=target,
            send_sem=self.wire.send_sems.at[self.slot],
            recv_sem=self.wire.recv_sems.at[self.slot],
            device_id=(to,),
            device_id_type=MESH,
        )

    def wait_recv(self):
        self.make().wait_recv()

    def wait_send(self):
        self.make().wait_send()


class Wire:
    def __init__(self, send_sems, recv_sems):
        self.send_sems, self.recv_sems, self.count, self.open = (send_sems, recv_sems, 0, [])

    def send(self, source, target, to):
        copy = Copy(self, self.count, source, target, to)
        copy.make().start()
        self.count += 1
        self.open.append(copy)
        return copy

    def clear(self, copies):
        for copy in copies:
            copy.wait_send()
        self.open = [copy for copy in self.open if not any(copy is other for other in copies)]

    def drain(self):
        self.clear(self.open)


def await_all(copies):
    for copy in copies:
        copy.wait_recv()


def greet(peers):
    for peer in peers:
        pl.semaphore_signal(
            pltpu.get_barrier_semaphore(), inc=1, device_id=(peer,), device_id_type=MESH
        )


def greeted(peers):
    pl.semaphore_wait(pltpu.get_barrier_semaphore(), len(peers))


class Ring:
    def __init__(self, wire, peer, view):
        self.wire, self.peer, self.view = (wire, peer, view)
        self.ahead = self.pass_on(0, None, 1)
        self.behind = self.pass_on(0, None, 3)

    def pass_on(self, k, part, step):
        block = lambda: self.view(k, part)
        return self.wire.send(block, block, lambda: self.peer(step))

    def forward(self):
        self.ahead.wait_recv()
        self.low = self.pass_on(3, 0, 1)
        self.behind.wait_recv()
        self.high = self.pass_on(1, 1, 3)

    def finish(self):
        self.low.wait_recv()
        self.high.wait_recv()


def aligned(start, size):
    return pl.ds(pl.multiple_of(start, 128), size)


def halves(start, size, part):
    if part is None:
        return aligned(start, size)
    low = size // 256 * 128
    return aligned(start, low) if part == 0 else aligned(start + low, size - low)


class Gather:
    def __init__(self, wire, peers, here, weight, turned, lines, natural, small):
        self.wire, self.here, self.weight, self.turned = (wire, here, weight, turned)
        self.lines, self.natural, self.small = (lines, natural, small)
        self.peers_x, self.peers_z, self.peers_y, self.sibling = peers
        x, z, y, c = here
        self.half, self.quarter = (c * 1536, (c * 4 + y) * 384)
        self.across = ([], [], [])

    def span(self, m):
        return (pl.ds(0, 160), pl.ds(160, 144), pl.ds(304, 144))[m]

    def begin(self):
        x, z, y, c = self.here
        self.first = {}
        for m in (2, 0, 1):
            view = lambda m=m: self.lines.at[c, y, self.span(m)]
            self.first[m] = [self.wire.send(view, view, lambda k=k: self.peers_y(k)) for k in TURNS]

    def swap(self):
        x, z, y, c = self.here
        self.swaps = {}
        for m in (2, 0, 1):
            await_all(self.first[m])
            view = lambda m=m: self.lines.at[c, :, self.span(m)]
            self.swaps[m] = self.wire.send(view, view, self.sibling)

    def spread(self, m):
        x, z, y, c = self.here
        self.swaps[m].wait_recv()
        for s in range(8):
            self.natural[s * LINES : (s + 1) * LINES] = self.lines[
                s % 2, s // 2, 16 + m * LINES : 16 + (m + 1) * LINES
            ].astype(single)
        start, count = (c * 12, 12) if m < 2 else ((c * 4 + y) * 3, 3)
        for j in range(count):
            self.weight[m, x, z, :, aligned((start + j) * 128, 128)] = self.natural[
                pl.ds(start + j, 48, stride=24), :
            ].astype(bfloat)

    def ring(self, peer, view):
        return Ring(self.wire, peer, view)

    def attn_x(self):
        x, z, y, c = self.here
        return self.ring(
            self.peers_x,
            lambda k, part: self.weight.at[0, plus(x, k), z, :, halves(self.half, 1536, part)],
        )

    def attn_z(self, b):
        x, z, y, c = self.here
        return self.ring(
            self.peers_z,
            lambda k, part: self.weight.at[
                0, plus(x, b), plus(z, k), :, halves(self.half, 1536, part)
            ],
        )

    def up_z(self):
        x, z, y, c = self.here
        return self.ring(
            self.peers_z,
            lambda k, part: self.weight.at[1, x, plus(z, k), :, halves(self.half, 1536, part)],
        )

    def up_x(self, b):
        x, z, y, c = self.here
        return self.ring(
            self.peers_x,
            lambda k, part: self.weight.at[
                1, plus(x, k), plus(z, b), :, halves(self.half, 1536, part)
            ],
        )

    def down_x(self):
        x, z, y, c = self.here
        return self.ring(
            self.peers_x,
            lambda k, part: self.weight.at[2, plus(x, k), z, :, halves(self.quarter, 384, part)],
        )

    def down_z(self, b):
        x, z, y, c = self.here
        return self.ring(
            self.peers_z,
            lambda k, part: self.weight.at[
                2, plus(x, b), plus(z, k), :, halves(self.quarter, 384, part)
            ],
        )

    def down_y(self, b):
        x, z, y, c = self.here
        return self.ring(
            self.peers_y,
            lambda k, part: self.weight.at[
                2, plus(x, b), :, :, halves((c * 4 + plus(y, k)) * 384, 384, part)
            ],
        )

    def spread_all(self):
        x, z, y, c = self.here
        self.spread(2)
        self.c1 = self.down_x()
        self.c2 = {0: self.down_z(0)}
        self.spread(0)
        self.a1 = self.attn_x()
        self.spread(1)
        self.b1 = self.up_z()
        for s in range(8):
            self.small[s * 6 : (s + 1) * 6] = self.lines[s % 2, s // 2, 0:16].astype(single)[0:6]
        self.turned[x, z] = self.small[...].astype(bfloat)
        view = lambda: self.turned.at[x, z]
        self.turn_x = [self.wire.send(view, view, lambda k=k: self.peers_x(k)) for k in TURNS]

    def near_down(self):
        self.c1.forward()
        for b in (3, 1):
            self.c2[b] = self.down_z(b)
        self.a2 = {0: self.attn_z(0)}
        self.b2 = {0: self.up_x(0)}

    def near_others(self):
        self.a1.forward()
        self.b1.forward()
        self.c2[0].forward()

    def far_down(self):
        self.c1.finish()
        self.c2[2] = self.down_z(2)
        self.c2[0].finish()
        self.c3 = {0: self.down_y(0)}

    def second_start(self):
        for b in (3, 1):
            self.c2[b].forward()
        for b in (3, 1):
            self.a2[b] = self.attn_z(b)
            self.b2[b] = self.up_x(b)
        x, z, y, c = self.here
        await_all(self.turn_x)
        view = lambda: self.turned.at[:, z]
        self.turn_z = [self.wire.send(view, view, lambda k=k: self.peers_z(k)) for k in TURNS]

    def far_others(self):
        self.a1.finish()
        self.a2[2] = self.attn_z(2)
        self.b1.finish()
        self.b2[2] = self.up_x(2)
        self.a2[0].forward()
        self.b2[0].forward()

    def down_near(self):
        for b in (3, 1):
            self.c2[b].finish()
            self.c3[b] = self.down_y(b)
        self.c2[2].forward()

    def down_far(self):
        self.c3[0].forward()
        self.c2[2].finish()
        self.c3[2] = self.down_y(2)

    def second_near(self):
        for b in (3, 1):
            self.a2[b].forward()
            self.b2[b].forward()

    def own_end(self):
        self.finish_attn(0)
        self.finish_up(0)

    def third_near(self):
        for b in (3, 1):
            self.c3[b].forward()
        self.finish_down(0)

    def second_far(self):
        self.a2[2].forward()
        self.b2[2].forward()

    def near_end(self):
        for b in (3, 1):
            self.finish_attn(b)
            self.finish_up(b)

    def third_far(self):
        self.c3[2].forward()

    def down_end(self):
        for b in (3, 1):
            self.finish_down(b)

    def finish_attn(self, b):
        x, z, y, c = self.here
        self.a2[b].finish()
        self.cross(0, lambda: self.weight.at[0, plus(x, b), :, :, aligned(self.half, 1536)])

    def finish_up(self, b):
        x, z, y, c = self.here
        self.b2[b].finish()
        self.cross(1, lambda: self.weight.at[1, :, plus(z, b), :, aligned(self.half, 1536)])

    def finish_down(self, b):
        x, z, y, c = self.here
        self.c3[b].finish()
        self.cross(2, lambda: self.weight.at[2, plus(x, b), :, :, aligned(self.half, 1536)])

    def cross(self, m, view):
        self.across[m].append(self.wire.send(view, view, self.sibling))

    def end(self, m):
        await_all(self.across[m])


def matmul(left, right):
    return jnp.dot(left, right, preferred_element_type=single)


def matmul_nt(left, right):
    return lax.dot_general(left, right, (((1,), (1,)), ((), ())), preferred_element_type=single)


def matmul_tn(left, right):
    return lax.dot_general(left, right, (((0,), (0,)), ((), ())), preferred_element_type=single)


def normalized(values):
    center = jnp.mean(values, -1, keepdims=True)
    shifted = values - center
    spread = jnp.mean(shifted * shifted, -1, keepdims=True)
    inverse = lax.rsqrt(spread + 1e-06)
    return (shifted * inverse, inverse)


def normalized_back(cotangent, unit, inverse, gain):
    scaled = cotangent * gain
    center = jnp.mean(scaled, -1, keepdims=True)
    along = jnp.mean(scaled * unit, -1, keepdims=True)
    return inverse * (scaled - center - unit * along)


def gelu_parts(hidden):
    squared = hidden * hidden
    angle = jnp.tanh(hidden * (0.7978845608028654 + 0.035677408136300125 * squared))
    return (squared, angle)


def even_lanes(rows):
    return lax.broadcasted_iota(jnp.int32, (rows, 128), 1) < 64


def split_heads(values):
    even = even_lanes(values.shape[0])
    zero = jnp.zeros_like(values)
    return jnp.concatenate([jnp.where(even, values, zero), jnp.where(even, zero, values)], 0)


def join_heads(values):
    rows = values.shape[0] // 2
    return jnp.where(even_lanes(rows), values[:rows], values[rows:])


def pair_weights(queries, key_rows, bias):
    scores = matmul_nt(split_heads(queries * 0.125), key_rows)
    scores = scores + jnp.concatenate([bias, bias], 0)
    weights = jnp.exp(scores - jnp.max(scores, -1, keepdims=True))
    return (weights, 1.0 / jnp.sum(weights, -1, keepdims=True))


def attend_images(qkv, attended, bias):
    starts = (0, 96, 192, 288)
    rows = lax.broadcasted_iota(jnp.int32, (16, 128), 0)

    @pl.loop(0, 6, unroll=3)
    def _(p):
        out = []
        for w, start in enumerate(starts):
            window = slice(start, start + 112)
            weights, scale = pair_weights(
                qkv[window, aligned(p * 128, 128)], qkv[window, aligned((6 + p) * 128, 128)], bias[w]
            )
            values = qkv[window, aligned((12 + p) * 128, 128)]
            out.append(join_heads(matmul(weights.astype(bfloat), values) * scale))
        lanes = aligned(p * 128, 128)
        attended[0:96, lanes] = out[0][0:96].astype(bfloat)
        for w in range(1, 4):
            edge = jnp.where(rows < 4 * w, out[w - 1][96:112], out[w][0:16])
            attended[starts[w] : starts[w] + 16, lanes] = edge.astype(bfloat)
            stop = 112 if w == 3 else 96
            attended[starts[w] + 16 : starts[w] + stop, lanes] = out[w][16:stop].astype(bfloat)


class UnitGather:
    def __init__(self, wire, peers, here, units, own, images, first, count):
        self.wire, self.here, self.units, self.own, self.images = (wire, here, units, own, images)
        self.peers_x, self.peers_z, self.peers_y, self.sibling = peers
        self.first, self.count, self.step = (first, count, 0)

    def swap(self):
        c = self.here[3]
        rows = pl.ds(self.first, self.count)
        self.own[c, rows] = self.units[rows, :]
        self.swapped = self.wire.send(self.own.at[c, rows], self.own.at[c, rows], self.sibling)

    def begin(self):
        x, z, y, c = self.here
        self.swapped.wait_recv()
        lanes = aligned(c * 384, 384)
        for first in range(self.first, self.first + self.count, 8):
            both = [self.own[core, first : first + 8, lanes] for core in range(2)]
            self.images[x, z, y, 2 * first : 2 * first + 16, lanes] = jnp.concatenate(both, 0).astype(
                bfloat
            )
        self.start()

    def block(self, o, k):
        x, z, y, c = self.here
        here = {"x": x, "z": z, "y": y}
        order = ORDERS[o]
        index = [
            slice(None)
            if n in order[: self.step]
            else plus(here[n], k)
            if n == order[self.step]
            else here[n]
            for n in "xzy"
        ]
        rows = pl.ds(2 * self.first, 2 * self.count)
        return self.images.at[(*index, rows, aligned((c * 3 + o) * 128, 128))]

    def start(self):
        peer = {"x": self.peers_x, "z": self.peers_z, "y": self.peers_y}
        self.sent = []
        for k in TURNS:
            for o in range(3):
                view = self.block(o, 0)
                to = peer[ORDERS[o][self.step]](k)
                self.sent.append((o, k, self.wire.send(view, view, to)))

    def next(self):
        for _, _, copy in self.sent:
            copy.wait_recv()
        self.step += 1
        self.start()
        if self.step == 2:
            self.crossed = [self.cross(o, 0) for o in range(3)]

    def cross(self, o, k):
        view = self.block(o, k)
        return self.wire.send(view, view, self.sibling)

    def finish(self):
        for o, k, copy in self.sent:
            copy.wait_recv()
            self.crossed.append(self.cross(o, 4 - k))

    def end(self):
        await_all(self.crossed)


def image_bias(bias):
    for w in range(4):
        first = 96 * w
        query = (lax.broadcasted_iota(jnp.int32, (112, 112), 0) + first) // 50
        key = (lax.broadcasted_iota(jnp.int32, (112, 112), 1) + first) // 50
        bias[w] = jnp.where(query == key, 0.0, -1e30)


def image_chunk(t, tokens, weight, vec, normed, qkv, attended, residual, bias, units, hook):
    lanes_t = slice(t * 768, (t + 1) * 768)
    unit, _ = normalized(tokens[:, lanes_t].astype(single))
    normed[...] = (unit * vec[0:1] + vec[1:2]).astype(bfloat)
    hook()
    for n, shift in enumerate((4, None, 5)):
        triple = matmul(normed[...], weight(0, n * 768, 768))
        if shift is not None:
            triple = triple + vec[shift : shift + 1]
        qkv[:, n * 768 : (n + 1) * 768] = triple.astype(bfloat)
    hook()
    attend_images(qkv, attended, bias)
    hook()
    residual[...] = (
        tokens[:, lanes_t].astype(single) + matmul(attended[...], weight(0, 2304, 768)) + vec[6:7]
    )
    unit, _ = normalized(residual[...])
    normed[...] = (unit * vec[2:3] + vec[3:4]).astype(bfloat)
    residual[...] = residual[...] + vec[7:8]
    hook()
    for f in range(4):
        hidden = matmul(normed[...], weight(1, f * 768, 768)) + vec[8 + f : 9 + f]
        _, angle = gelu_parts(hidden)
        active = (0.5 * hidden * (1.0 + angle)).astype(bfloat)
        residual[...] = residual[...] + matmul_nt(active, weight(2, f * 768, 768))
        hook()
    image = lax.broadcasted_iota(jnp.int32, (8, 400), 0)
    token = lax.broadcasted_iota(jnp.int32, (8, 400), 1)
    member = (token // 50 == image).astype(bfloat)
    high = residual[...].astype(bfloat)
    low = (residual[...] - high.astype(single)).astype(bfloat)
    pooled = (matmul(member, high) + matmul(member, low)) * (1.0 / 50.0)
    units[t * 8 : (t + 1) * 8, :] = unit_rows(pooled)


PLAN = {
    (0, 2): "swap",
    (0, 4): "spread_all",
    (0, 7): "near_down",
    (1, 0): "near_others",
    (1, 2): "far_down",
    (1, 3): "second_start",
    (1, 4): "far_others",
    (1, 6): "down_near",
    (1, 7): "down_far",
    (2, 1): "second_near",
    (2, 2): "own_end third_near",
    (2, 5): "second_far",
    (2, 6): "near_end",
    (2, 7): "third_far down_end",
}


def slot_codes(index, ends, window):
    later = index >= 64
    position = jnp.where(later, index - 64, index)
    slots = [
        sum((position >= ends[2 * window + r][k]).astype(jnp.int32) for k in range(4)) for r in (0, 1)
    ]
    return jnp.where(later, slots[1] + 8, slots[0])


def text_masks(lengths, bias):
    ends = []
    for r in range(6):
        row, end = ([], 0)
        for k in range(4):
            end = end + lengths[k, r]
            row.append(end)
        ends.append(row)
    codes = []
    for w in range(3):
        query = slot_codes(lax.broadcasted_iota(jnp.int32, (128, 128), 0), ends, w)
        key = slot_codes(lax.broadcasted_iota(jnp.int32, (128, 128), 1), ends, w)
        bias[w] = jnp.where(query == key, 0.0, -1e30)
        code = slot_codes(lax.broadcasted_iota(jnp.int32, (24, 128), 1), ends, w)
        slot = jnp.where(code >= 8, code - 8, code)
        caption = 8 * w + jnp.where(code >= 8, 4, 0) + slot
        codes.append(jnp.where(slot < 4, caption, -1))
    caption = jnp.concatenate(codes, 1)
    return (caption == lax.broadcasted_iota(jnp.int32, (24, 384), 0)).astype(single)


def attend_text(qkv, attended, probs, bias):
    @pl.loop(0, 6, unroll=3)
    def _(p):
        for w in range(3):
            window = slice(w * 128, (w + 1) * 128)
            weights, scale = pair_weights(
                qkv[window, aligned(p * 128, 128)], qkv[window, aligned((6 + p) * 128, 128)], bias[w]
            )
            pair = weights * scale
            probs[pl.ds(pl.multiple_of((p * 3 + w) * 256, 256), 256)] = pair
            out = matmul(pair.astype(bfloat), qkv[window, aligned((12 + p) * 128, 128)])
            attended[window, aligned(p * 128, 128)] = join_heads(out).astype(bfloat)


def attend_text_back(qkv, probs, attended_grad, triple_grad):
    @pl.loop(0, 6, unroll=3)
    def _(p):
        for w in range(3):
            window = slice(w * 128, (w + 1) * 128)
            at = [aligned((6 * n + p) * 128, 128) for n in range(3)]
            queries, key_rows, value_rows = (qkv[window, lanes] for lanes in at)
            grads = split_heads(attended_grad[window, at[0]])
            pair = probs[pl.ds(pl.multiple_of((p * 3 + w) * 256, 256), 256)]
            value_grad = matmul_tn(pair.astype(bfloat), grads)
            prob_grad = matmul_nt(grads, value_rows)
            along = jnp.sum(pair * prob_grad, -1, keepdims=True)
            score_grad = (pair * (prob_grad - along) * 0.125).astype(bfloat)
            query_grad = join_heads(matmul(score_grad, key_rows))
            key_grad = matmul_tn(score_grad, split_heads(queries))
            triple_grad[window, at[0]] = query_grad.astype(bfloat)
            triple_grad[window, at[1]] = key_grad.astype(bfloat)
            triple_grad[window, at[2]] = value_grad.astype(bfloat)


def column_sums(values):
    return jnp.sum(values.astype(single), 0, keepdims=True)


def step_kernel(
    lengths,
    tokens_ref,
    image_ref,
    image_attn_ref,
    image_mlp_ref,
    image_vec,
    attn_ref,
    mlp_ref,
    vector_ref,
    input_grad,
    attn_out,
    mlp_out,
    vector_out,
    square_out,
    weight,
    store,
    tokens,
    bias,
    image_masks,
    units,
    probs,
    normed,
    qkv,
    attended,
    residual,
    normed_two,
    active,
    slope,
    triple_grad,
    flow,
    part_sum,
    images,
    own,
    lines,
    small,
    turned,
    vec,
    row_part,
    row_near,
    row_far,
    late_x,
    late_z,
    down_x,
    down_z,
    whole,
    last,
    flat,
    third,
    packed,
    pieces,
    landed,
    sums,
    vec_c,
    vec_z,
    vec_x,
    vec_y,
    square,
    near,
    far,
    load_sems,
    send_sems,
    recv_sems,
):
    x, z, y, c = place()
    peers_x = lambda k: device(plus(x, k), z, y, c)
    peers_z = lambda k: device(x, plus(z, k), y, c)
    peers_y = lambda k: device(x, z, plus(y, k), c)
    sibling = device(x, z, y, 1 - c)
    group = [(k, d) for k in range(4) for d in range(2) if (k, d) != (0, 0)]
    plane = [(i, j) for i in range(4) for j in range(4) if (i, j) != (0, 0)]
    group_peer = lambda k, d: device(x, z, plus(y, k), lax.rem(c + d, 2))
    plane_peer = lambda i, j: device(plus(x, i), plus(z, j), y, c)
    wire = Wire(send_sems, recv_sems)
    turns = TURNS

    held = store.at[:, :, :, :, 0:1536]
    low, high = (slice(0, 768), slice(768, 1536))
    from_z = [[store.at[m, k, :, :, 1536:2304] for k in range(3)] for m in range(2)]
    from_x = [[store.at[m, k, :, :, 2304:3072] for k in range(3)] for m in range(2)]
    from_y = [store.at[2, :, :, :, 1536 + 384 * k : 1920 + 384 * k] for k in range(3)]
    total_z = [store.at[m, 3, :, :, 1536:2304] for m in range(2)]
    total_x = [store.at[m, 3, :, :, 2304:3072] for m in range(2)]
    total_y = store.at[2, :, :, :, 2688:3072]

    loads = [
        pltpu.make_async_copy(source, target, load_sems.at[n])
        for n, (source, target) in enumerate(
            [
                (image_ref.at[0:400], slope.at[:, 0:768]),
                (image_attn_ref, store.at[0]),
                (image_mlp_ref, store.at[1:3]),
                (image_ref.at[400:800], slope.at[:, 768:1536]),
                (image_ref.at[800:1200], slope.at[:, 1536:2304]),
                (tokens_ref, tokens),
            ]
        )
    ]
    for load in loads:
        load.start()
    others = [group_peer(*g) for g in group] + [plane_peer(*p) for p in plane]
    greet(others)
    natural, line = (probs.at[0:1152], [probs.at[1152 + 144 * m : 1296 + 144 * m] for m in range(3)])
    small[0:16] = jnp.zeros((16, 128), single)
    small[0:6, 0:12] = vector_ref[...]
    lines[c, y, 0:16] = small[0:16].astype(bfloat)
    for m in range(3):
        for j in range(24):
            columns = slice(j * 128, (j + 1) * 128)
            rows = attn_ref[:, columns] if m == 0 else mlp_ref[:, m - 1, columns]
            line[m][pl.ds(j, 6, stride=24), :] = rows
        lines[c, y, 16 + m * LINES : 16 + (m + 1) * LINES] = line[m][...].astype(bfloat)
    greeted(others)
    peers = (peers_x, peers_z, peers_y, sibling)
    unit_gather = UnitGather(wire, peers, (x, z, y, c), units, own, images, 0, 24)
    gather = Gather(
        wire, peers, (x, z, y, c), weight, turned, lines, natural, small
    )
    gather.begin()
    image_bias(image_masks)
    for load in loads:
        load.wait()
    plan = PLAN
    image_weight = lambda m, first, size: store[m, :, :, :, first : first + size].reshape(768, size)

    for t in range(3):
        points = iter(range(99))

        def hook():
            for name in plan.get((t, next(points)), "").split():
                getattr(gather, name)()

        image_chunk(
            t, slope, image_weight, image_vec, normed, qkv, attended, residual, image_masks, units, hook
        )

    unit_gather.swap()
    member = text_masks(lengths, bias)
    unit_gather.begin()
    gather.finish_attn(2)
    await_all(gather.turn_z)
    vec[...] = turned[...].reshape(768, 128).astype(single).T[0:16]
    unit_gather.next()
    gather.finish_up(2)

    normed, qkv, attended, residual, slope = (
        ref.at[0:384] for ref in (normed, qkv, attended, residual, slope)
    )
    unit_one, _ = normalized(tokens[...].astype(single))
    normed[...] = (unit_one * vec[0:1] + vec[1:2]).astype(bfloat)
    gather.end(0)
    attn = lambda first, size: weight[0, :, :, :, first : first + size].reshape(768, size)
    for n, shift in enumerate((4, None, 5)):
        triple = matmul(normed[...], attn(n * 768, 768))
        if shift is not None:
            triple = triple + vec[shift : shift + 1]
        qkv[:, n * 768 : (n + 1) * 768] = triple.astype(bfloat)
    unit_gather.next()
    gather.finish_down(2)
    attend_text(qkv, attended, probs, bias)
    residual[...] = tokens[...].astype(single) + matmul(attended[...], attn(2304, 768)) + vec[6:7]
    unit_two, _ = normalized(residual[...])
    normed_two[...] = (unit_two * vec[2:3] + vec[3:4]).astype(bfloat)
    gather.end(1)
    for f in range(4):
        lanes = slice(f * 768, (f + 1) * 768)
        hidden = matmul(normed_two[...], weight[1, :, :, :, lanes].reshape(768, 768)) + vec[8 + f : 9 + f]
        squared, angle = gelu_parts(hidden)
        active[:, lanes] = (0.5 * hidden * (1.0 + angle)).astype(bfloat)
        curve = 0.7978845608028654 + 0.10703222440890037 * squared
        slope[:, lanes] = (
            0.5 * (1.0 + angle) + 0.5 * hidden * (1.0 - angle * angle) * curve
        ).astype(bfloat)
    gather.end(2)
    flow[...] = residual[...] + vec[7:8]
    for f in range(4):
        lanes = slice(f * 768, (f + 1) * 768)
        flow[...] = flow[...] + matmul_nt(
            active[:, lanes], weight[2, :, :, :, lanes].reshape(768, 768)
        )
    unit_gather.finish()
    highest = lax.Precision.HIGHEST
    per_length = 1.0 / jnp.sum(member, -1, keepdims=True)
    pooled = per_length * jnp.dot(member, flow[...], precision=highest, preferred_element_type=single)

    scale = lax.rsqrt(jnp.sum(pooled * pooled, -1, keepdims=True) + 1e-06)
    unit = pooled * scale
    unit_gather.end()
    every = images[...].reshape(3072, 768)
    logits = logit_scale * matmul_nt(unit.astype(bfloat), every)
    powers = jnp.exp(logits)
    column = jnp.sum(powers, 1, keepdims=True)
    rows = jnp.sum(powers, 0, keepdims=True)
    for k in range(8):
        row_part[k : k + 1, :] = rows[:, k * 384 : (k + 1) * 384]
    row_near[y, c] = row_part[...]
    wire.count = max(wire.count, SUM_COPIES)
    sent = [wire.send(row_part, row_near.at[y, c], group_peer(*g)) for g in group]
    caption = lax.broadcasted_iota(jnp.int32, (24, 3072), 0) + lax.axis_index("dp") * 24
    at = lax.broadcasted_iota(jnp.int32, (24, 3072), 1)
    inside = at % 48
    image = at - inside + inside // 8 % 2 * 24 + inside // 16 * 8 + inside % 8
    same = (caption == image).astype(single)
    of_column = powers / column - 2.0 * same
    await_all(sent)
    row_far[x, z] = sum(row_near[k, d] for k in range(4) for d in range(2))
    sent = [wire.send(row_far.at[x, z], row_far.at[x, z], plane_peer(*p)) for p in plane]
    await_all(sent)
    total = sum(row_far[i, j] for i in range(4) for j in range(4))
    every_row = jnp.concatenate([total[k : k + 1] for k in range(8)], 1)
    logit_grad = (logit_scale / (2.0 * 3072) * (powers / every_row + of_column)).astype(bfloat)
    unit_grad = matmul(logit_grad, every)
    pooled_grad = scale * (unit_grad - unit * jnp.sum(unit * unit_grad, -1, keepdims=True))
    flow[...] = lax.dot_general(
        member,
        pooled_grad * per_length,
        (((0,), (0,)), ((), ())),
        precision=highest,
        preferred_element_type=single,
    )

    sends = {}

    def block_grad(left, right):
        return matmul_tn(left, right).reshape(4, 4, 48, right.shape[1])

    def other_half(m, make):
        for i in range(2):
            place_i = images.at[:, :, 2 * (m % 2) + i]
            place_i[...] = make((1 - c) * 1536 + i * 768, i).astype(bfloat)
            sends[m, i] = wire.send(
                place_i, held.at[m, :, :, :, i * 768 : (i + 1) * 768], sibling
            )

    def own_half(m, make):
        for i in range(2):
            sends[m, i].wait_recv()
            lanes = slice(i * 768, (i + 1) * 768)
            held[m, :, :, :, lanes] = (
                make(c * 1536 + i * 768, i) + held[m, :, :, :, lanes].astype(single)
            ).astype(bfloat)

    wire.drain()
    wire.count = 0

    def add(base, parts):
        return base.astype(single) + sum(part.astype(single) for part in parts)

    def first_sums(m):
        return [
            [wire.send(held.at[m, :, plus(z, k), :, low], from_z[m][k - 1], peers_z(k)) for k in turns],
            [wire.send(held.at[m, plus(x, k), :, :, high], from_x[m][k - 1], peers_x(k)) for k in turns],
        ]

    def second_sums(m, sent):
        await_all(sent[0])
        for i in range(4):
            total_z[m][i] = add(held[m, i, z, :, low], [from_z[m][k][i] for k in range(3)]).astype(bfloat)
        over_x = [
            wire.send(total_z[m].at[plus(x, k)], late_x.at[m, k - 1], peers_x(k)) for k in turns
        ]
        await_all(sent[1])
        for i in range(4):
            total_x[m][i] = add(held[m, x, i, :, high], [from_x[m][k][i] for k in range(3)]).astype(bfloat)
        over_z = [
            wire.send(total_x[m].at[plus(z, k)], late_z.at[m, k - 1], peers_z(k)) for k in turns
        ]
        return (over_x, over_z)

    def whole_sums(m, sent):
        await_all(sent[0])
        whole[m, :, low] = add(total_z[m][x], [late_x[m, k] for k in range(3)])
        await_all(sent[1])
        whole[m, :, high] = add(total_x[m][z], [late_z[m, k] for k in range(3)])
        for j in range(12):
            flat[m, pl.ds(j, 48, stride=12), :] = whole[m, :, j * 128 : (j + 1) * 128]

    branch_two = triple_grad.at[:, 2304:3072]
    branch_two[...] = flow[...].astype(bfloat)
    vec_c[c] = jnp.zeros((16, 768), single)
    vec_c[c, 7:8] = column_sums(branch_two[...])
    make_two = lambda first, i: block_grad(branch_two[...], active[:, aligned(first, 768)])
    other_half(2, make_two)
    for f in range(4):
        lanes = slice(f * 768, (f + 1) * 768)
        active_grad = matmul(branch_two[...], weight[2, :, :, :, lanes].reshape(768, 768))
        hidden_grad = (active_grad * slope[:, lanes].astype(single)).astype(bfloat)
        slope[:, lanes] = hidden_grad
        vec_c[c, 8 + f : 9 + f] = column_sums(hidden_grad)
    make_one = lambda first, i: block_grad(normed_two[...], slope[:, aligned(first, 768)])
    other_half(1, make_one)
    for f in range(4):
        lanes = slice(f * 768, (f + 1) * 768)
        piece = matmul_nt(slope[:, lanes], weight[1, :, :, :, lanes].reshape(768, 768))
        part_sum[...] = piece if f == 0 else part_sum[...] + piece
    own_half(2, make_two)
    send_y = [
        wire.send(held.at[2, :, :, :, aligned(plus(y, k) * 384, 384)], from_y[k - 1], peers_y(k))
        for k in turns
    ]
    unit_two, inverse_two = normalized(residual[...])
    vec_c[c, 2:3] = jnp.sum(part_sum[...] * unit_two, 0, keepdims=True)
    vec_c[c, 3:4] = jnp.sum(part_sum[...], 0, keepdims=True)
    flow[...] = flow[...] + normalized_back(part_sum[...], unit_two, inverse_two, vec[2:3])
    triple_grad[:, 2304:3072] = flow[...].astype(bfloat)
    vec_c[c, 6:7] = column_sums(triple_grad[:, 2304:3072])
    own_half(1, make_one)
    send_one = first_sums(1)
    active[:, 0:768] = matmul_nt(triple_grad[:, 2304:3072], attn(2304, 768)).astype(bfloat)
    attend_text_back(qkv, probs, active, triple_grad)
    vec_c[c, 4:5] = column_sums(triple_grad[:, 0:768])
    vec_c[c, 5:6] = column_sums(triple_grad[:, 1536:2304])

    def make_zero(first, i):
        left = normed[...]
        if i == 1:
            left = jnp.where(first >= 2304, attended[...], left)
        return block_grad(left, triple_grad[:, aligned(first, 768)])

    wire.clear([sends[2, i] for i in range(2)])
    other_half(0, make_zero)
    for n in range(3):
        piece = matmul_nt(triple_grad[:, n * 768 : (n + 1) * 768], attn(n * 768, 768))
        part_sum[...] = piece if n == 0 else part_sum[...] + piece
    own_half(0, make_zero)
    send_zero = first_sums(0)
    unit_one, inverse_one = normalized(tokens[...].astype(single))
    vec_c[c, 0:1] = jnp.sum(part_sum[...] * unit_one, 0, keepdims=True)
    vec_c[c, 1:2] = jnp.sum(part_sum[...], 0, keepdims=True)
    vec_swap = wire.send(vec_c.at[c], vec_c.at[c], sibling)
    part_sum[...] = flow[...] + normalized_back(part_sum[...], unit_one, inverse_one, vec[0:1])
    leave = pltpu.make_async_copy(part_sum, input_grad, load_sems.at[6])
    leave.start()
    second_one = second_sums(1, send_one)
    vec_swap.wait_recv()
    vec_z[z] = vec_c[0] + vec_c[1]
    sent_vec_z = [wire.send(vec_z.at[z], vec_z.at[z], peers_z(k)) for k in turns]

    await_all(send_y)
    quarter = aligned(y * 384, 384)
    for i in range(4):
        for j in range(4):
            total_y[i, j] = add(
                held[2, i, j, :, quarter], [from_y[k][i, j] for k in range(3)]
            ).astype(bfloat)
    down_send_x = [wire.send(total_y.at[plus(x, k)], down_x.at[k - 1], peers_x(k)) for k in turns]
    await_all(sent_vec_z)
    vec_x[x] = vec_z[0] + vec_z[1] + vec_z[2] + vec_z[3]
    sent_vec_x = [wire.send(vec_x.at[x], vec_x.at[x], peers_x(k)) for k in turns]
    whole_sums(1, second_one)
    await_all(down_send_x)
    for j in range(4):
        last[j] = add(total_y[x, j], [down_x[k, j] for k in range(3)]).astype(bfloat)
    down_send_z = [wire.send(last.at[plus(z, k)], down_z.at[k - 1], peers_z(k)) for k in turns]
    await_all(sent_vec_x)
    vec_y[y] = vec_x[0] + vec_x[1] + vec_x[2] + vec_x[3]
    sent_vec_y = [wire.send(vec_y.at[y], vec_y.at[y], peers_y(k)) for k in turns]
    second_zero = second_sums(0, send_zero)
    await_all(down_send_z)
    ended = add(last[z], [down_z[k] for k in range(3)])
    for j in range(3):
        third[pl.ds(j, 48, stride=3), :] = ended[:, j * 128 : (j + 1) * 128]
    whole_sums(0, second_zero)
    packed[160:176] = jnp.zeros((16, 128), single)
    for s in range(8):
        packed[0:72] = flat[0, s * 72 : (s + 1) * 72]
        packed[72:144] = flat[1, s * 72 : (s + 1) * 72]
        packed[144:162] = third[s * 18 : (s + 1) * 18]
        pieces[s // 2, s % 2] = packed[...].astype(bfloat)
    landed[y, c] = pieces[y, c]
    piece_sent = [
        wire.send(pieces.at[plus(y, k), lax.rem(c + d, 2)], landed.at[y, c], group_peer(k, d))
        for k, d in group
    ]
    await_all(sent_vec_y)
    vec_total = vec_y[0] + vec_y[1] + vec_y[2] + vec_y[3]
    vector_out[...] = vec_total
    await_all(piece_sent)
    for h in range(2):
        for k in range(4):
            piece = landed[k, h].astype(single)
            packed[...] = piece if k == 0 else packed[...] + piece
            sums[...] = piece[144:168]
            for j in range(3):
                at = ((h * 4 + k) * 3 + j) * 128
                mlp_out[:, 1, at : at + 128] = sums[pl.ds(j, 6, stride=3), :]
        for j in range(12):
            at = (h * 12 + j) * 128
            attn_out[:, at : at + 128] = packed[pl.ds(j, 6, stride=12), :]
            mlp_out[:, 0, at : at + 128] = packed[pl.ds(72 + j, 6, stride=12), :]
    lanes = lax.broadcasted_iota(jnp.int32, (16, 768), 1)
    start = lax.axis_index("dp") * 6
    owned = jnp.where((lanes >= start) & (lanes < start + 6), vec_total, 0.0)
    squares = sum_squares((attn_out[...], mlp_out[...], owned))
    square[...] = jnp.broadcast_to(squares, (8, 128))
    near[y, c] = square[...]
    sent = [wire.send(square, near.at[y, c], group_peer(*g)) for g in group]
    await_all(sent)
    far[x, z] = sum(near[k, d] for k in range(4) for d in range(2))
    sent = [wire.send(far.at[x, z], far.at[x, z], plane_peer(*p)) for p in plane]
    await_all(sent)
    square_out[...] = sum(far[i, j] for i in range(4) for j in range(4))
    leave.wait()
    wire.drain()


def train_step(
    lengths, text, images, image_attn, image_mlp, image_vectors, attn_master, mlp_master, vector_master
):
    copies = 172
    vmem = pl.BlockSpec(memory_space=pltpu.VMEM)
    anywhere = pl.BlockSpec(memory_space=pl.ANY)
    return pl.pallas_call(
        step_kernel,
        out_shape=(
            jax.ShapeDtypeStruct((384, 768), single),
            jax.ShapeDtypeStruct((6, 3072), single),
            jax.ShapeDtypeStruct((6, 2, 3072), single),
            jax.ShapeDtypeStruct((16, 768), single),
            jax.ShapeDtypeStruct((8, 128), single),
        ),
        in_specs=[pl.BlockSpec(memory_space=pltpu.SMEM)] + [anywhere] * 4 + [vmem] * 4,
        out_specs=[anywhere] + [vmem] * 4,
        scratch_shapes=[
            pltpu.VMEM((3, 4, 4, 48, 3072), bfloat),
            pltpu.VMEM((3, 4, 4, 48, 3072), bfloat),
            pltpu.VMEM((384, 768), bfloat),
            pltpu.VMEM((3, 128, 128), single),
            pltpu.VMEM((4, 112, 112), single),
            pltpu.VMEM((24, 768), single),
            pltpu.VMEM((4608, 128), single),
            pltpu.VMEM((400, 768), bfloat),
            pltpu.VMEM((400, 2304), bfloat),
            pltpu.VMEM((400, 768), bfloat),
            pltpu.VMEM((400, 768), single),
            pltpu.VMEM((384, 768), bfloat),
            pltpu.VMEM((384, 3072), bfloat),
            pltpu.VMEM((400, 3072), bfloat),
            pltpu.VMEM((384, 3072), bfloat),
            pltpu.VMEM((384, 768), single),
            pltpu.VMEM((384, 768), single),
            pltpu.VMEM((4, 4, 4, 48, 768), bfloat),
            pltpu.VMEM((2, 24, 768), single),
            pltpu.VMEM((2, 4, SHARD, 128), bfloat),
            pltpu.VMEM((48, 128), single),
            pltpu.VMEM((4, 4, 48, 128), bfloat),
            pltpu.VMEM((16, 768), single),
            pltpu.VMEM((8, 384), single),
            pltpu.VMEM((4, 2, 8, 384), single),
            pltpu.VMEM((4, 4, 8, 384), single),
            pltpu.VMEM((2, 3, 48, 768), bfloat),
            pltpu.VMEM((2, 3, 48, 768), bfloat),
            pltpu.VMEM((3, 4, 48, 384), bfloat),
            pltpu.VMEM((3, 48, 384), bfloat),
            pltpu.VMEM((2, 48, 1536), single),
            pltpu.VMEM((4, 48, 384), bfloat),
            pltpu.VMEM((2, 576, 128), single),
            pltpu.VMEM((144, 128), single),
            pltpu.VMEM((176, 128), single),
            pltpu.VMEM((4, 2, 176, 128), bfloat),
            pltpu.VMEM((4, 2, 176, 128), bfloat),
            pltpu.VMEM((24, 128), single),
            pltpu.VMEM((2, 16, 768), single),
            pltpu.VMEM((4, 16, 768), single),
            pltpu.VMEM((4, 16, 768), single),
            pltpu.VMEM((4, 16, 768), single),
            pltpu.VMEM((8, 128), single),
            pltpu.VMEM((4, 2, 8, 128), single),
            pltpu.VMEM((4, 4, 8, 128), single),
            pltpu.SemaphoreType.DMA((7,)),
            pltpu.SemaphoreType.DMA((copies,)),
            pltpu.SemaphoreType.DMA((copies,)),
        ],
        compiler_params=pltpu.CompilerParams(
            collective_id=1, has_side_effects=True, vmem_limit_bytes=63 * 2**20
        ),
        name="train_step",
    )(
        lengths,
        text,
        images,
        image_attn.reshape(4, 4, 48, 3072),
        image_mlp.reshape(2, 4, 4, 48, 3072),
        image_vectors,
        attn_master,
        mlp_master,
        vector_master,
    )


def close_kernel(*refs):
    given, out = (refs[:14], refs[14:])
    attn_sum, mlp_sum, vector_all, square, input_grad = given[:5]
    states = given[5:]
    out[0][...] = input_grad[...]
    grad_norm = jnp.sqrt(square[0:1, 0:1])
    out[1][...] = grad_norm
    factor = jnp.minimum(1.0, clip_norm / (grad_norm + 1e-06))
    start = lax.axis_index("dp") * 6
    vector_sum = pltpu.roll(vector_all[...], lax.rem(768 - start, 768), 1)[:, :128].T[:6, :12]
    sums = (attn_sum[...], mlp_sum[...], vector_sum)
    rates = ((learn_rate, weight_decay), (learn_rate, weight_decay), (vector_rate, 0.0))
    for n in range(3):
        out[2 + n][...] = sums[n]
        clip = factor.reshape(1, 1, 1) if n == 1 else factor
        new = adam_update(
            states[n][...], sums[n], states[3 + n][...], states[6 + n][...], clip, *rates[n]
        )
        for k in range(3):
            out[5 + 3 * k + n][...] = new[k]


def close(*given):
    vmem = pl.BlockSpec(memory_space=pltpu.VMEM)
    kinds = [(6, 3072), (6, 2, 3072), (6, 12)]
    shapes = [(384, 768), (1, 1)] + kinds * 4
    return pl.pallas_call(
        close_kernel,
        out_shape=[jax.ShapeDtypeStruct(shape, single) for shape in shapes],
        in_specs=[vmem] * 14,
        out_specs=[vmem] * 14,
        compiler_params=pltpu.CompilerParams(vmem_limit_bytes=63 * 2**20),
        name="close_step",
    )(*given)


def shards(
    text_input,
    caption_lengths,
    image_tokens,
    image_attn,
    image_mlp,
    image_vectors,
    attn_master,
    mlp_master,
    vector_master,
    attn_first,
    mlp_first,
    vector_first,
    attn_second,
    mlp_second,
    vector_second,
):
    mlp_master, mlp_first, mlp_second = (
        jnp.swapaxes(values, 0, 1) for values in (mlp_master, mlp_first, mlp_second)
    )
    vector_master, vector_first, vector_second = (
        values.T for values in (vector_master, vector_first, vector_second)
    )
    input_grad, attn_sum, mlp_sum, vector_all, square_total = train_step(
        caption_lengths.T,
        text_input,
        image_tokens,
        image_attn,
        image_mlp,
        image_vectors,
        attn_master,
        mlp_master,
        vector_master,
    )
    out = close(
        attn_sum,
        mlp_sum,
        vector_all,
        square_total,
        input_grad,
        attn_master,
        mlp_master,
        vector_master,
        attn_first,
        mlp_first,
        vector_first,
        attn_second,
        mlp_second,
        vector_second,
    )
    turned = [jnp.swapaxes(value, 0, 1) if n % 3 else value for n, value in enumerate(out[2:])]
    return (out[0], out[1].reshape(()), *turned)


def solution(mesh):
    in_specs = (
        P("dp", None),
        P("dp", None),
        P("dp", None),
        P(),
        P(),
        P(),
        P("dp", None),
        P(None, "dp", None),
        P(None, "dp"),
        P("dp", None),
        P(None, "dp", None),
        P(None, "dp"),
        P("dp", None),
        P(None, "dp", None),
        P(None, "dp"),
    )
    out_specs = (
        P("dp", None),
        P(),
        P("dp", None),
        P(None, "dp", None),
        P(None, "dp"),
        P("dp", None),
        P(None, "dp", None),
        P(None, "dp"),
        P("dp", None),
        P(None, "dp", None),
        P(None, "dp"),
        P("dp", None),
        P(None, "dp", None),
        P(None, "dp"),
    )
    return jax.shard_map(shards, mesh=mesh, in_specs=in_specs, out_specs=out_specs, check_vma=False)
```

```python
import jax
import jax.numpy as jnp
from jax import lax
from jax.experimental import pallas as pl
from jax.experimental.pallas import tpu as pltpu
from jax.sharding import PartitionSpec as P

STEP = 10


logit_scale = 60.0
clip_norm = 0.01
learn_rate = 0.05
vector_rate = 0.3
beta_first = 0.9
beta_second = 0.999
adam_epsilon = 1e-08
weight_decay = 0.1
bfloat = jnp.bfloat16
single = jnp.float32


def unit_rows(values):
    return values * lax.rsqrt(jnp.sum(values * values, -1, keepdims=True) + 1e-06)


def sum_squares(arrays):
    return sum((jnp.sum(member * member) for member in arrays))


def adam_update(weight, gradient, first_moment, second_moment, factor, rate, decay_rate):
    clipped = gradient * factor
    first_new = beta_first * first_moment + (1.0 - beta_first) * clipped
    second_new = beta_second * second_moment + (1.0 - beta_second) * clipped * clipped
    ratio = (
        first_new
        / (1.0 - beta_first**STEP)
        / (jnp.sqrt(second_new / (1.0 - beta_second**STEP)) + adam_epsilon)
    )
    return (first_new, second_new, weight - rate * (ratio + decay_rate * weight))


MESH = pl.DeviceIdType.MESH
LINES = 144
SHARD = 448
SUM_COPIES = 80
ORDERS = ("yzx", "zxy", "xyz")
TURNS = (1, 3, 2)


def place():
    me = lax.axis_index("dp")
    return (me // 32, lax.rem(me // 8, 4), lax.rem(me // 2, 4), lax.rem(me, 2))


def device(x, z, y, c):
    return ((x * 4 + z) * 4 + y) * 2 + c


def plus(index, step):
    return lax.rem(index + step, 4)


def made(item):
    return item() if callable(item) else item


class Copy:
    def __init__(self, wire, slot, source, target, to):
        self.wire, self.slot, self.parts = (wire, slot, (source, target, to))

    def make(self):
        source, target, to = (made(part) for part in self.parts)
        return pltpu.make_async_remote_copy(
            src_ref=source,
            dst_ref=target,
            send_sem=self.wire.send_sems.at[self.slot],
            recv_sem=self.wire.recv_sems.at[self.slot],
            device_id=(to,),
            device_id_type=MESH,
        )

    def wait_recv(self):
        self.make().wait_recv()

    def wait_send(self):
        self.make().wait_send()


class Wire:
    def __init__(self, send_sems, recv_sems):
        self.send_sems, self.recv_sems, self.count, self.open = (send_sems, recv_sems, 0, [])

    def send(self, source, target, to):
        copy = Copy(self, self.count, source, target, to)
        copy.make().start()
        self.count += 1
        self.open.append(copy)
        return copy

    def clear(self, copies):
        for copy in copies:
            copy.wait_send()
        self.open = [copy for copy in self.open if not any(copy is other for other in copies)]

    def drain(self):
        self.clear(self.open)


def await_all(copies):
    for copy in copies:
        copy.wait_recv()


def greet(peers):
    for peer in peers:
        pl.semaphore_signal(
            pltpu.get_barrier_semaphore(), inc=1, device_id=(peer,), device_id_type=MESH
        )


def greeted(peers):
    pl.semaphore_wait(pltpu.get_barrier_semaphore(), len(peers))


class Ring:
    def __init__(self, wire, peer, view):
        self.wire, self.peer, self.view = (wire, peer, view)
        self.ahead = self.pass_on(0, None, 1)
        self.behind = self.pass_on(0, None, 3)

    def pass_on(self, k, part, step):
        block = lambda: self.view(k, part)
        return self.wire.send(block, block, lambda: self.peer(step))

    def forward(self):
        self.ahead.wait_recv()
        self.low = self.pass_on(3, 0, 1)
        self.behind.wait_recv()
        self.high = self.pass_on(1, 1, 3)

    def finish(self):
        self.low.wait_recv()
        self.high.wait_recv()


def aligned(start, size):
    return pl.ds(pl.multiple_of(start, 128), size)


def halves(start, size, part):
    if part is None:
        return aligned(start, size)
    low = size // 256 * 128
    return aligned(start, low) if part == 0 else aligned(start + low, size - low)


class Gather:
    def __init__(self, wire, peers, here, weight, turned, lines, natural, small):
        self.wire, self.here, self.weight, self.turned = (wire, here, weight, turned)
        self.lines, self.natural, self.small = (lines, natural, small)
        self.peers_x, self.peers_z, self.peers_y, self.sibling = peers
        x, z, y, c = here
        self.half, self.quarter = (c * 1536, (c * 4 + y) * 384)
        self.across = ([], [], [])

    def span(self, m):
        return (pl.ds(0, 160), pl.ds(160, 144), pl.ds(304, 144))[m]

    def begin(self):
        x, z, y, c = self.here
        self.first = {}
        for m in (2, 0, 1):
            view = lambda m=m: self.lines.at[c, y, self.span(m)]
            self.first[m] = [self.wire.send(view, view, lambda k=k: self.peers_y(k)) for k in TURNS]

    def swap(self):
        x, z, y, c = self.here
        self.swaps = {}
        for m in (2, 0, 1):
            await_all(self.first[m])
            view = lambda m=m: self.lines.at[c, :, self.span(m)]
            self.swaps[m] = self.wire.send(view, view, self.sibling)

    def spread(self, m):
        x, z, y, c = self.here
        self.swaps[m].wait_recv()
        for s in range(8):
            self.natural[s * LINES : (s + 1) * LINES] = self.lines[
                s % 2, s // 2, 16 + m * LINES : 16 + (m + 1) * LINES
            ].astype(single)
        start, count = (c * 12, 12) if m < 2 else ((c * 4 + y) * 3, 3)
        for j in range(count):
            self.weight[m, x, z, :, aligned((start + j) * 128, 128)] = self.natural[
                pl.ds(start + j, 48, stride=24), :
            ].astype(bfloat)

    def ring(self, peer, view):
        return Ring(self.wire, peer, view)

    def attn_x(self):
        x, z, y, c = self.here
        return self.ring(
            self.peers_x,
            lambda k, part: self.weight.at[0, plus(x, k), z, :, halves(self.half, 1536, part)],
        )

    def attn_z(self, b):
        x, z, y, c = self.here
        return self.ring(
            self.peers_z,
            lambda k, part: self.weight.at[
                0, plus(x, b), plus(z, k), :, halves(self.half, 1536, part)
            ],
        )

    def up_z(self):
        x, z, y, c = self.here
        return self.ring(
            self.peers_z,
            lambda k, part: self.weight.at[1, x, plus(z, k), :, halves(self.half, 1536, part)],
        )

    def up_x(self, b):
        x, z, y, c = self.here
        return self.ring(
            self.peers_x,
            lambda k, part: self.weight.at[
                1, plus(x, k), plus(z, b), :, halves(self.half, 1536, part)
            ],
        )

    def down_x(self):
        x, z, y, c = self.here
        return self.ring(
            self.peers_x,
            lambda k, part: self.weight.at[2, plus(x, k), z, :, halves(self.quarter, 384, part)],
        )

    def down_z(self, b):
        x, z, y, c = self.here
        return self.ring(
            self.peers_z,
            lambda k, part: self.weight.at[
                2, plus(x, b), plus(z, k), :, halves(self.quarter, 384, part)
            ],
        )

    def down_y(self, b):
        x, z, y, c = self.here
        return self.ring(
            self.peers_y,
            lambda k, part: self.weight.at[
                2, plus(x, b), :, :, halves((c * 4 + plus(y, k)) * 384, 384, part)
            ],
        )

    def spread_all(self):
        x, z, y, c = self.here
        self.spread(2)
        self.c1 = self.down_x()
        self.c2 = {0: self.down_z(0)}
        self.spread(0)
        self.a1 = self.attn_x()
        self.spread(1)
        self.b1 = self.up_z()
        for s in range(8):
            self.small[s * 6 : (s + 1) * 6] = self.lines[s % 2, s // 2, 0:16].astype(single)[0:6]
        self.turned[x, z] = self.small[...].astype(bfloat)
        view = lambda: self.turned.at[x, z]
        self.turn_x = [self.wire.send(view, view, lambda k=k: self.peers_x(k)) for k in TURNS]

    def near_down(self):
        self.c1.forward()
        for b in (3, 1):
            self.c2[b] = self.down_z(b)
        self.a2 = {0: self.attn_z(0)}
        self.b2 = {0: self.up_x(0)}

    def near_others(self):
        self.a1.forward()
        self.b1.forward()
        self.c2[0].forward()

    def far_down(self):
        self.c1.finish()
        self.c2[2] = self.down_z(2)
        self.c2[0].finish()
        self.c3 = {0: self.down_y(0)}

    def second_start(self):
        for b in (3, 1):
            self.c2[b].forward()
        for b in (3, 1):
            self.a2[b] = self.attn_z(b)
            self.b2[b] = self.up_x(b)
        x, z, y, c = self.here
        await_all(self.turn_x)
        view = lambda: self.turned.at[:, z]
        self.turn_z = [self.wire.send(view, view, lambda k=k: self.peers_z(k)) for k in TURNS]

    def far_others(self):
        self.a1.finish()
        self.a2[2] = self.attn_z(2)
        self.b1.finish()
        self.b2[2] = self.up_x(2)
        self.a2[0].forward()
        self.b2[0].forward()

    def down_near(self):
        for b in (3, 1):
            self.c2[b].finish()
            self.c3[b] = self.down_y(b)
        self.c2[2].forward()

    def down_far(self):
        self.c3[0].forward()
        self.c2[2].finish()
        self.c3[2] = self.down_y(2)

    def second_near(self):
        for b in (3, 1):
            self.a2[b].forward()
            self.b2[b].forward()

    def own_end(self):
        self.finish_attn(0)
        self.finish_up(0)

    def third_near(self):
        for b in (3, 1):
            self.c3[b].forward()
        self.finish_down(0)

    def second_far(self):
        self.a2[2].forward()
        self.b2[2].forward()

    def near_end(self):
        for b in (3, 1):
            self.finish_attn(b)
            self.finish_up(b)

    def third_far(self):
        self.c3[2].forward()

    def down_end(self):
        for b in (3, 1):
            self.finish_down(b)

    def finish_attn(self, b):
        x, z, y, c = self.here
        self.a2[b].finish()
        self.cross(0, lambda: self.weight.at[0, plus(x, b), :, :, aligned(self.half, 1536)])

    def finish_up(self, b):
        x, z, y, c = self.here
        self.b2[b].finish()
        self.cross(1, lambda: self.weight.at[1, :, plus(z, b), :, aligned(self.half, 1536)])

    def finish_down(self, b):
        x, z, y, c = self.here
        self.c3[b].finish()
        self.cross(2, lambda: self.weight.at[2, plus(x, b), :, :, aligned(self.half, 1536)])

    def cross(self, m, view):
        self.across[m].append(self.wire.send(view, view, self.sibling))

    def end(self, m):
        await_all(self.across[m])


def matmul(left, right):
    return jnp.dot(left, right, preferred_element_type=single)


def matmul_nt(left, right):
    return lax.dot_general(left, right, (((1,), (1,)), ((), ())), preferred_element_type=single)


def matmul_tn(left, right):
    return lax.dot_general(left, right, (((0,), (0,)), ((), ())), preferred_element_type=single)


def normalized(values):
    center = jnp.mean(values, -1, keepdims=True)
    shifted = values - center
    spread = jnp.mean(shifted * shifted, -1, keepdims=True)
    inverse = lax.rsqrt(spread + 1e-06)
    return (shifted * inverse, inverse)


def normalized_back(cotangent, unit, inverse, gain):
    scaled = cotangent * gain
    center = jnp.mean(scaled, -1, keepdims=True)
    along = jnp.mean(scaled * unit, -1, keepdims=True)
    return inverse * (scaled - center - unit * along)


def gelu_parts(hidden):
    squared = hidden * hidden
    angle = jnp.tanh(hidden * (0.7978845608028654 + 0.035677408136300125 * squared))
    return (squared, angle)


def even_lanes(rows):
    return lax.broadcasted_iota(jnp.int32, (rows, 128), 1) < 64


def split_heads(values):
    even = even_lanes(values.shape[0])
    zero = jnp.zeros_like(values)
    return jnp.concatenate([jnp.where(even, values, zero), jnp.where(even, zero, values)], 0)


def join_heads(values):
    rows = values.shape[0] // 2
    return jnp.where(even_lanes(rows), values[:rows], values[rows:])


def pair_weights(queries, key_rows, bias):
    scores = matmul_nt(split_heads(queries * 0.125), key_rows)
    scores = scores + jnp.concatenate([bias, bias], 0)
    weights = jnp.exp(scores - jnp.max(scores, -1, keepdims=True))
    return (weights, 1.0 / jnp.sum(weights, -1, keepdims=True))


def attend_images(qkv, attended, bias):
    starts = (0, 96, 192, 288)
    rows = lax.broadcasted_iota(jnp.int32, (16, 128), 0)

    @pl.loop(0, 6, unroll=3)
    def _(p):
        out = []
        for w, start in enumerate(starts):
            window = slice(start, start + 112)
            weights, scale = pair_weights(
                qkv[window, aligned(p * 128, 128)], qkv[window, aligned((6 + p) * 128, 128)], bias[w]
            )
            values = qkv[window, aligned((12 + p) * 128, 128)]
            out.append(join_heads(matmul(weights.astype(bfloat), values) * scale))
        lanes = aligned(p * 128, 128)
        attended[0:96, lanes] = out[0][0:96].astype(bfloat)
        for w in range(1, 4):
            edge = jnp.where(rows < 4 * w, out[w - 1][96:112], out[w][0:16])
            attended[starts[w] : starts[w] + 16, lanes] = edge.astype(bfloat)
            stop = 112 if w == 3 else 96
            attended[starts[w] + 16 : starts[w] + stop, lanes] = out[w][16:stop].astype(bfloat)


class UnitGather:
    def __init__(self, wire, peers, here, units, own, images, first, count):
        self.wire, self.here, self.units, self.own, self.images = (wire, here, units, own, images)
        self.peers_x, self.peers_z, self.peers_y, self.sibling = peers
        self.first, self.count, self.step = (first, count, 0)

    def swap(self):
        c = self.here[3]
        rows = pl.ds(self.first, self.count)
        self.own[c, rows] = self.units[rows, :]
        self.swapped = self.wire.send(self.own.at[c, rows], self.own.at[c, rows], self.sibling)

    def begin(self):
        x, z, y, c = self.here
        self.swapped.wait_recv()
        lanes = aligned(c * 384, 384)
        for first in range(self.first, self.first + self.count, 8):
            both = [self.own[core, first : first + 8, lanes] for core in range(2)]
            self.images[x, z, y, 2 * first : 2 * first + 16, lanes] = jnp.concatenate(both, 0).astype(
                bfloat
            )
        self.start()

    def block(self, o, k):
        x, z, y, c = self.here
        here = {"x": x, "z": z, "y": y}
        order = ORDERS[o]
        index = [
            slice(None)
            if n in order[: self.step]
            else plus(here[n], k)
            if n == order[self.step]
            else here[n]
            for n in "xzy"
        ]
        rows = pl.ds(2 * self.first, 2 * self.count)
        return self.images.at[(*index, rows, aligned((c * 3 + o) * 128, 128))]

    def start(self):
        peer = {"x": self.peers_x, "z": self.peers_z, "y": self.peers_y}
        self.sent = []
        for k in TURNS:
            for o in range(3):
                view = self.block(o, 0)
                to = peer[ORDERS[o][self.step]](k)
                self.sent.append((o, k, self.wire.send(view, view, to)))

    def next(self):
        for _, _, copy in self.sent:
            copy.wait_recv()
        self.step += 1
        self.start()
        if self.step == 2:
            self.crossed = [self.cross(o, 0) for o in range(3)]

    def cross(self, o, k):
        view = self.block(o, k)
        return self.wire.send(view, view, self.sibling)

    def finish(self):
        for o, k, copy in self.sent:
            copy.wait_recv()
            self.crossed.append(self.cross(o, 4 - k))

    def end(self):
        await_all(self.crossed)


def image_bias(bias):
    for w in range(4):
        first = 96 * w
        query = (lax.broadcasted_iota(jnp.int32, (112, 112), 0) + first) // 50
        key = (lax.broadcasted_iota(jnp.int32, (112, 112), 1) + first) // 50
        bias[w] = jnp.where(query == key, 0.0, -1e30)


def image_chunk(t, tokens, weight, vec, normed, qkv, attended, residual, bias, units, hook):
    lanes_t = slice(t * 768, (t + 1) * 768)
    unit, _ = normalized(tokens[:, lanes_t].astype(single))
    normed[...] = (unit * vec[0:1] + vec[1:2]).astype(bfloat)
    hook()
    for n, shift in enumerate((4, None, 5)):
        triple = matmul(normed[...], weight(0, n * 768, 768))
        if shift is not None:
            triple = triple + vec[shift : shift + 1]
        qkv[:, n * 768 : (n + 1) * 768] = triple.astype(bfloat)
    hook()
    attend_images(qkv, attended, bias)
    hook()
    residual[...] = (
        tokens[:, lanes_t].astype(single) + matmul(attended[...], weight(0, 2304, 768)) + vec[6:7]
    )
    unit, _ = normalized(residual[...])
    normed[...] = (unit * vec[2:3] + vec[3:4]).astype(bfloat)
    residual[...] = residual[...] + vec[7:8]
    hook()
    for f in range(4):
        hidden = matmul(normed[...], weight(1, f * 768, 768)) + vec[8 + f : 9 + f]
        _, angle = gelu_parts(hidden)
        active = (0.5 * hidden * (1.0 + angle)).astype(bfloat)
        residual[...] = residual[...] + matmul_nt(active, weight(2, f * 768, 768))
        hook()
    image = lax.broadcasted_iota(jnp.int32, (8, 400), 0)
    token = lax.broadcasted_iota(jnp.int32, (8, 400), 1)
    member = (token // 50 == image).astype(bfloat)
    high = residual[...].astype(bfloat)
    low = (residual[...] - high.astype(single)).astype(bfloat)
    pooled = (matmul(member, high) + matmul(member, low)) * (1.0 / 50.0)
    units[t * 8 : (t + 1) * 8, :] = unit_rows(pooled)


PLAN = {
    (0, 2): "swap",
    (0, 4): "spread_all",
    (0, 7): "near_down",
    (1, 0): "near_others",
    (1, 2): "far_down",
    (1, 3): "second_start",
    (1, 4): "far_others",
    (1, 6): "down_near",
    (1, 7): "down_far",
    (2, 1): "second_near",
    (2, 2): "own_end third_near",
    (2, 5): "second_far",
    (2, 6): "near_end",
    (2, 7): "third_far down_end",
}


def slot_codes(index, ends, window):
    later = index >= 64
    position = jnp.where(later, index - 64, index)
    slots = [
        sum((position >= ends[2 * window + r][k]).astype(jnp.int32) for k in range(4)) for r in (0, 1)
    ]
    return jnp.where(later, slots[1] + 8, slots[0])


def text_masks(lengths, bias):
    ends = []
    for r in range(6):
        row, end = ([], 0)
        for k in range(4):
            end = end + lengths[k, r]
            row.append(end)
        ends.append(row)
    codes = []
    for w in range(3):
        query = slot_codes(lax.broadcasted_iota(jnp.int32, (128, 128), 0), ends, w)
        key = slot_codes(lax.broadcasted_iota(jnp.int32, (128, 128), 1), ends, w)
        bias[w] = jnp.where(query == key, 0.0, -1e30)
        code = slot_codes(lax.broadcasted_iota(jnp.int32, (24, 128), 1), ends, w)
        slot = jnp.where(code >= 8, code - 8, code)
        caption = 8 * w + jnp.where(code >= 8, 4, 0) + slot
        codes.append(jnp.where(slot < 4, caption, -1))
    caption = jnp.concatenate(codes, 1)
    return (caption == lax.broadcasted_iota(jnp.int32, (24, 384), 0)).astype(single)


def attend_text(qkv, attended, probs, bias):
    @pl.loop(0, 6, unroll=3)
    def _(p):
        for w in range(3):
            window = slice(w * 128, (w + 1) * 128)
            weights, scale = pair_weights(
                qkv[window, aligned(p * 128, 128)], qkv[window, aligned((6 + p) * 128, 128)], bias[w]
            )
            pair = weights * scale
            probs[pl.ds(pl.multiple_of((p * 3 + w) * 256, 256), 256)] = pair
            out = matmul(pair.astype(bfloat), qkv[window, aligned((12 + p) * 128, 128)])
            attended[window, aligned(p * 128, 128)] = join_heads(out).astype(bfloat)


def attend_text_back(qkv, probs, attended_grad, triple_grad):
    @pl.loop(0, 6, unroll=3)
    def _(p):
        for w in range(3):
            window = slice(w * 128, (w + 1) * 128)
            at = [aligned((6 * n + p) * 128, 128) for n in range(3)]
            queries, key_rows, value_rows = (qkv[window, lanes] for lanes in at)
            grads = split_heads(attended_grad[window, at[0]])
            pair = probs[pl.ds(pl.multiple_of((p * 3 + w) * 256, 256), 256)]
            value_grad = matmul_tn(pair.astype(bfloat), grads)
            prob_grad = matmul_nt(grads, value_rows)
            along = jnp.sum(pair * prob_grad, -1, keepdims=True)
            score_grad = (pair * (prob_grad - along) * 0.125).astype(bfloat)
            query_grad = join_heads(matmul(score_grad, key_rows))
            key_grad = matmul_tn(score_grad, split_heads(queries))
            triple_grad[window, at[0]] = query_grad.astype(bfloat)
            triple_grad[window, at[1]] = key_grad.astype(bfloat)
            triple_grad[window, at[2]] = value_grad.astype(bfloat)


def column_sums(values):
    return jnp.sum(values.astype(single), 0, keepdims=True)


def step_kernel(
    lengths,
    tokens_ref,
    image_ref,
    image_attn_ref,
    image_mlp_ref,
    image_vec,
    attn_ref,
    mlp_ref,
    vector_ref,
    input_grad,
    attn_out,
    mlp_out,
    vector_out,
    square_out,
    weight,
    store,
    tokens,
    bias,
    image_masks,
    units,
    probs,
    normed,
    qkv,
    attended,
    residual,
    normed_two,
    active,
    slope,
    triple_grad,
    flow,
    part_sum,
    images,
    own,
    lines,
    small,
    turned,
    vec,
    row_part,
    row_near,
    row_far,
    late_x,
    late_z,
    down_x,
    down_z,
    whole,
    last,
    flat,
    third,
    packed,
    pieces,
    landed,
    sums,
    vec_c,
    vec_z,
    vec_x,
    vec_y,
    square,
    near,
    far,
    load_sems,
    send_sems,
    recv_sems,
):
    x, z, y, c = place()
    peers_x = lambda k: device(plus(x, k), z, y, c)
    peers_z = lambda k: device(x, plus(z, k), y, c)
    peers_y = lambda k: device(x, z, plus(y, k), c)
    sibling = device(x, z, y, 1 - c)
    group = [(k, d) for k in (2, 1, 3, 0) for d in (1, 0) if (k, d) != (0, 0)]
    far_first = (2, 1, 3, 0)
    plane = [(i, j) for i in far_first for j in far_first if (i, j) != (0, 0)]
    group_peer = lambda k, d: device(x, z, plus(y, k), lax.rem(c + d, 2))
    plane_peer = lambda i, j: device(plus(x, i), plus(z, j), y, c)
    wire = Wire(send_sems, recv_sems)
    turns = TURNS

    held = store.at[:, :, :, :, 0:1536]
    low, high = (slice(0, 768), slice(768, 1536))
    from_z = [[store.at[m, k, :, :, 1536:2304] for k in range(3)] for m in range(2)]
    from_x = [[store.at[m, k, :, :, 2304:3072] for k in range(3)] for m in range(2)]
    from_y = [store.at[2, :, :, :, 1536 + 384 * k : 1920 + 384 * k] for k in range(3)]
    total_z = [store.at[m, 3, :, :, 1536:2304] for m in range(2)]
    total_x = [store.at[m, 3, :, :, 2304:3072] for m in range(2)]
    total_y = store.at[2, :, :, :, 2688:3072]

    loads = [
        pltpu.make_async_copy(source, target, load_sems.at[n])
        for n, (source, target) in enumerate(
            [
                (image_ref.at[0:400], slope.at[:, 0:768]),
                (image_attn_ref, store.at[0]),
                (image_mlp_ref, store.at[1:3]),
                (image_ref.at[400:800], slope.at[:, 768:1536]),
                (image_ref.at[800:1200], slope.at[:, 1536:2304]),
                (tokens_ref, tokens),
            ]
        )
    ]
    for load in loads:
        load.start()
    others = [group_peer(*g) for g in group] + [plane_peer(*p) for p in plane]
    greet(others)
    natural, line = (probs.at[0:1152], [probs.at[1152 + 144 * m : 1296 + 144 * m] for m in range(3)])
    small[0:16] = jnp.zeros((16, 128), single)
    small[0:6, 0:12] = vector_ref[...]
    lines[c, y, 0:16] = small[0:16].astype(bfloat)
    for m in range(3):
        for j in range(24):
            columns = slice(j * 128, (j + 1) * 128)
            rows = attn_ref[:, columns] if m == 0 else mlp_ref[:, m - 1, columns]
            line[m][pl.ds(j, 6, stride=24), :] = rows
        lines[c, y, 16 + m * LINES : 16 + (m + 1) * LINES] = line[m][...].astype(bfloat)
    greeted(others)
    peers = (peers_x, peers_z, peers_y, sibling)
    unit_gather = UnitGather(wire, peers, (x, z, y, c), units, own, images, 0, 24)
    gather = Gather(
        wire, peers, (x, z, y, c), weight, turned, lines, natural, small
    )
    gather.begin()
    image_bias(image_masks)
    for load in loads:
        load.wait()
    plan = PLAN
    image_weight = lambda m, first, size: store[m, :, :, :, first : first + size].reshape(768, size)

    for t in range(3):
        points = iter(range(99))

        def hook():
            for name in plan.get((t, next(points)), "").split():
                getattr(gather, name)()

        image_chunk(
            t, slope, image_weight, image_vec, normed, qkv, attended, residual, image_masks, units, hook
        )

    unit_gather.swap()
    member = text_masks(lengths, bias)
    unit_gather.begin()
    gather.finish_attn(2)
    await_all(gather.turn_z)
    vec[...] = turned[...].reshape(768, 128).astype(single).T[0:16]
    unit_gather.next()
    gather.finish_up(2)

    normed, qkv, attended, residual, slope = (
        ref.at[0:384] for ref in (normed, qkv, attended, residual, slope)
    )
    unit_one, _ = normalized(tokens[...].astype(single))
    normed[...] = (unit_one * vec[0:1] + vec[1:2]).astype(bfloat)
    gather.end(0)
    attn = lambda first, size: weight[0, :, :, :, first : first + size].reshape(768, size)
    for n, shift in enumerate((4, None, 5)):
        triple = matmul(normed[...], attn(n * 768, 768))
        if shift is not None:
            triple = triple + vec[shift : shift + 1]
        qkv[:, n * 768 : (n + 1) * 768] = triple.astype(bfloat)
    unit_gather.next()
    gather.finish_down(2)
    attend_text(qkv, attended, probs, bias)
    residual[...] = tokens[...].astype(single) + matmul(attended[...], attn(2304, 768)) + vec[6:7]
    unit_two, _ = normalized(residual[...])
    normed_two[...] = (unit_two * vec[2:3] + vec[3:4]).astype(bfloat)
    gather.end(1)
    for f in range(4):
        lanes = slice(f * 768, (f + 1) * 768)
        hidden = matmul(normed_two[...], weight[1, :, :, :, lanes].reshape(768, 768)) + vec[8 + f : 9 + f]
        squared, angle = gelu_parts(hidden)
        active[:, lanes] = (0.5 * hidden * (1.0 + angle)).astype(bfloat)
        curve = 0.7978845608028654 + 0.10703222440890037 * squared
        slope[:, lanes] = (
            0.5 * (1.0 + angle) + 0.5 * hidden * (1.0 - angle * angle) * curve
        ).astype(bfloat)
    gather.end(2)
    flow[...] = residual[...] + vec[7:8]
    for f in range(4):
        lanes = slice(f * 768, (f + 1) * 768)
        flow[...] = flow[...] + matmul_nt(
            active[:, lanes], weight[2, :, :, :, lanes].reshape(768, 768)
        )
    unit_gather.finish()
    highest = lax.Precision.HIGHEST
    per_length = 1.0 / jnp.sum(member, -1, keepdims=True)
    pooled = per_length * jnp.dot(member, flow[...], precision=highest, preferred_element_type=single)

    scale = lax.rsqrt(jnp.sum(pooled * pooled, -1, keepdims=True) + 1e-06)
    unit = pooled * scale
    unit_gather.end()
    every = images[...].reshape(3072, 768)
    logits = logit_scale * matmul_nt(unit.astype(bfloat), every)
    powers = jnp.exp(logits)
    column = jnp.sum(powers, 1, keepdims=True)
    rows = jnp.sum(powers, 0, keepdims=True)
    for k in range(8):
        row_part[k : k + 1, :] = rows[:, k * 384 : (k + 1) * 384]
    row_near[y, c] = row_part[...]
    wire.count = max(wire.count, SUM_COPIES)
    sent = [wire.send(row_part, row_near.at[y, c], group_peer(*g)) for g in group]
    caption = lax.broadcasted_iota(jnp.int32, (24, 3072), 0) + lax.axis_index("dp") * 24
    at = lax.broadcasted_iota(jnp.int32, (24, 3072), 1)
    inside = at % 48
    image = at - inside + inside // 8 % 2 * 24 + inside // 16 * 8 + inside % 8
    same = (caption == image).astype(single)
    of_column = powers / column - 2.0 * same
    await_all(sent)
    row_far[x, z] = sum(row_near[k, d] for k in range(4) for d in range(2))
    sent = [wire.send(row_far.at[x, z], row_far.at[x, z], plane_peer(*p)) for p in plane]
    await_all(sent)
    total = sum(row_far[i, j] for i in range(4) for j in range(4))
    every_row = jnp.concatenate([total[k : k + 1] for k in range(8)], 1)
    logit_grad = (logit_scale / (2.0 * 3072) * (powers / every_row + of_column)).astype(bfloat)
    unit_grad = matmul(logit_grad, every)
    pooled_grad = scale * (unit_grad - unit * jnp.sum(unit * unit_grad, -1, keepdims=True))
    flow[...] = lax.dot_general(
        member,
        pooled_grad * per_length,
        (((0,), (0,)), ((), ())),
        precision=highest,
        preferred_element_type=single,
    )

    sends = {}

    def block_grad(left, right):
        return matmul_tn(left, right).reshape(4, 4, 48, right.shape[1])

    def other_half(m, make):
        for i in range(2):
            place_i = images.at[:, :, 2 * (m % 2) + i]
            place_i[...] = make((1 - c) * 1536 + i * 768, i).astype(bfloat)
            sends[m, i] = wire.send(
                place_i, held.at[m, :, :, :, i * 768 : (i + 1) * 768], sibling
            )

    def own_half(m, make, then=lambda m, i: None):
        sent = []
        for i in range(2):
            sends[m, i].wait_recv()
            lanes = slice(i * 768, (i + 1) * 768)
            held[m, :, :, :, lanes] = (
                make(c * 1536 + i * 768, i) + held[m, :, :, :, lanes].astype(single)
            ).astype(bfloat)
            sent.append(then(m, i))
        return sent

    wire.drain()
    wire.count = 0

    def add(base, parts):
        return base.astype(single) + sum(part.astype(single) for part in parts)

    def first_sums(m, i):
        if i == 0:
            return [
                wire.send(held.at[m, :, plus(z, k), :, low], from_z[m][k - 1], peers_z(k)) for k in turns
            ]
        return [
            wire.send(held.at[m, plus(x, k), :, :, high], from_x[m][k - 1], peers_x(k)) for k in turns
        ]

    def second_sums(m, sent):
        await_all(sent[0])
        for i in range(4):
            total_z[m][i] = add(held[m, i, z, :, low], [from_z[m][k][i] for k in range(3)]).astype(bfloat)
        over_x = [
            wire.send(total_z[m].at[plus(x, k)], late_x.at[m, k - 1], peers_x(k)) for k in turns
        ]
        await_all(sent[1])
        for i in range(4):
            total_x[m][i] = add(held[m, x, i, :, high], [from_x[m][k][i] for k in range(3)]).astype(bfloat)
        over_z = [
            wire.send(total_x[m].at[plus(z, k)], late_z.at[m, k - 1], peers_z(k)) for k in turns
        ]
        return (over_x, over_z)

    def whole_sums(m, sent):
        await_all(sent[0])
        whole[m, :, low] = add(total_z[m][x], [late_x[m, k] for k in range(3)])
        await_all(sent[1])
        whole[m, :, high] = add(total_x[m][z], [late_z[m, k] for k in range(3)])
        for j in range(12):
            flat[m, pl.ds(j, 48, stride=12), :] = whole[m, :, j * 128 : (j + 1) * 128]

    branch_two = triple_grad.at[:, 2304:3072]
    branch_two[...] = flow[...].astype(bfloat)
    vec_c[c] = jnp.zeros((16, 768), single)
    vec_c[c, 7:8] = column_sums(branch_two[...])
    make_two = lambda first, i: block_grad(branch_two[...], active[:, aligned(first, 768)])
    other_half(2, make_two)
    for f in range(4):
        lanes = slice(f * 768, (f + 1) * 768)
        active_grad = matmul(branch_two[...], weight[2, :, :, :, lanes].reshape(768, 768))
        hidden_grad = (active_grad * slope[:, lanes].astype(single)).astype(bfloat)
        slope[:, lanes] = hidden_grad
        vec_c[c, 8 + f : 9 + f] = column_sums(hidden_grad)
    make_one = lambda first, i: block_grad(normed_two[...], slope[:, aligned(first, 768)])
    other_half(1, make_one)
    for f in range(4):
        lanes = slice(f * 768, (f + 1) * 768)
        piece = matmul_nt(slope[:, lanes], weight[1, :, :, :, lanes].reshape(768, 768))
        part_sum[...] = piece if f == 0 else part_sum[...] + piece
    own_half(2, make_two)
    send_y = [
        wire.send(held.at[2, :, :, :, aligned(plus(y, k) * 384, 384)], from_y[k - 1], peers_y(k))
        for k in turns
    ]
    unit_two, inverse_two = normalized(residual[...])
    vec_c[c, 2:3] = jnp.sum(part_sum[...] * unit_two, 0, keepdims=True)
    vec_c[c, 3:4] = jnp.sum(part_sum[...], 0, keepdims=True)
    flow[...] = flow[...] + normalized_back(part_sum[...], unit_two, inverse_two, vec[2:3])
    triple_grad[:, 2304:3072] = flow[...].astype(bfloat)
    vec_c[c, 6:7] = column_sums(triple_grad[:, 2304:3072])
    send_one = own_half(1, make_one, first_sums)
    active[:, 0:768] = matmul_nt(triple_grad[:, 2304:3072], attn(2304, 768)).astype(bfloat)
    attend_text_back(qkv, probs, active, triple_grad)
    vec_c[c, 4:5] = column_sums(triple_grad[:, 0:768])
    vec_c[c, 5:6] = column_sums(triple_grad[:, 1536:2304])

    def make_zero(first, i):
        left = normed[...]
        if i == 1:
            left = jnp.where(first >= 2304, attended[...], left)
        return block_grad(left, triple_grad[:, aligned(first, 768)])

    wire.clear([sends[2, i] for i in range(2)])
    other_half(0, make_zero)
    for n in range(3):
        piece = matmul_nt(triple_grad[:, n * 768 : (n + 1) * 768], attn(n * 768, 768))
        part_sum[...] = piece if n == 0 else part_sum[...] + piece
    send_zero = own_half(0, make_zero, first_sums)
    unit_one, inverse_one = normalized(tokens[...].astype(single))
    vec_c[c, 0:1] = jnp.sum(part_sum[...] * unit_one, 0, keepdims=True)
    vec_c[c, 1:2] = jnp.sum(part_sum[...], 0, keepdims=True)
    vec_swap = wire.send(vec_c.at[c], vec_c.at[c], sibling)
    part_sum[...] = flow[...] + normalized_back(part_sum[...], unit_one, inverse_one, vec[0:1])
    leave = pltpu.make_async_copy(part_sum, input_grad, load_sems.at[6])
    leave.start()
    second_one = second_sums(1, send_one)
    vec_swap.wait_recv()
    vec_z[z] = vec_c[0] + vec_c[1]
    sent_vec_z = [wire.send(vec_z.at[z], vec_z.at[z], peers_z(k)) for k in turns]

    await_all(send_y)
    quarter = aligned(y * 384, 384)
    for i in range(4):
        for j in range(4):
            total_y[i, j] = add(
                held[2, i, j, :, quarter], [from_y[k][i, j] for k in range(3)]
            ).astype(bfloat)
    down_send_x = [wire.send(total_y.at[plus(x, k)], down_x.at[k - 1], peers_x(k)) for k in turns]
    await_all(sent_vec_z)
    vec_x[x] = vec_z[0] + vec_z[1] + vec_z[2] + vec_z[3]
    sent_vec_x = [wire.send(vec_x.at[x], vec_x.at[x], peers_x(k)) for k in turns]
    whole_sums(1, second_one)
    await_all(down_send_x)
    for j in range(4):
        last[j] = add(total_y[x, j], [down_x[k, j] for k in range(3)]).astype(bfloat)
    down_send_z = [wire.send(last.at[plus(z, k)], down_z.at[k - 1], peers_z(k)) for k in turns]
    await_all(sent_vec_x)
    vec_y[y] = vec_x[0] + vec_x[1] + vec_x[2] + vec_x[3]
    sent_vec_y = [wire.send(vec_y.at[y], vec_y.at[y], peers_y(k)) for k in turns]
    second_zero = second_sums(0, send_zero)
    await_all(down_send_z)
    ended = add(last[z], [down_z[k] for k in range(3)])
    for j in range(3):
        third[pl.ds(j, 48, stride=3), :] = ended[:, j * 128 : (j + 1) * 128]
    whole_sums(0, second_zero)
    packed[160:176] = jnp.zeros((16, 128), single)
    for s in range(8):
        packed[0:72] = flat[0, s * 72 : (s + 1) * 72]
        packed[72:144] = flat[1, s * 72 : (s + 1) * 72]
        packed[144:162] = third[s * 18 : (s + 1) * 18]
        pieces[s // 2, s % 2] = packed[...].astype(bfloat)
    landed[y, c] = pieces[y, c]
    piece_sent = [
        wire.send(pieces.at[plus(y, k), lax.rem(c + d, 2)], landed.at[y, c], group_peer(k, d))
        for k, d in group
    ]
    await_all(sent_vec_y)
    vec_total = vec_y[0] + vec_y[1] + vec_y[2] + vec_y[3]
    vector_out[...] = vec_total
    await_all(piece_sent)
    for h in range(2):
        for k in range(4):
            piece = landed[k, h].astype(single)
            packed[...] = piece if k == 0 else packed[...] + piece
            sums[...] = piece[144:168]
            for j in range(3):
                at = ((h * 4 + k) * 3 + j) * 128
                mlp_out[:, 1, at : at + 128] = sums[pl.ds(j, 6, stride=3), :]
        for j in range(12):
            at = (h * 12 + j) * 128
            attn_out[:, at : at + 128] = packed[pl.ds(j, 6, stride=12), :]
            mlp_out[:, 0, at : at + 128] = packed[pl.ds(72 + j, 6, stride=12), :]
    lanes = lax.broadcasted_iota(jnp.int32, (16, 768), 1)
    start = lax.axis_index("dp") * 6
    owned = jnp.where((lanes >= start) & (lanes < start + 6), vec_total, 0.0)
    squares = sum_squares((attn_out[...], mlp_out[...], owned))
    square[...] = jnp.broadcast_to(squares, (8, 128))
    near[y, c] = square[...]
    sent = [wire.send(square, near.at[y, c], group_peer(*g)) for g in group]
    await_all(sent)
    far[x, z] = sum(near[k, d] for k in range(4) for d in range(2))
    sent = [wire.send(far.at[x, z], far.at[x, z], plane_peer(*p)) for p in plane]
    await_all(sent)
    square_out[...] = sum(far[i, j] for i in range(4) for j in range(4))
    leave.wait()
    wire.drain()


def train_step(
    lengths, text, images, image_attn, image_mlp, image_vectors, attn_master, mlp_master, vector_master
):
    copies = 172
    vmem = pl.BlockSpec(memory_space=pltpu.VMEM)
    anywhere = pl.BlockSpec(memory_space=pl.ANY)
    return pl.pallas_call(
        step_kernel,
        out_shape=(
            jax.ShapeDtypeStruct((384, 768), single),
            jax.ShapeDtypeStruct((6, 3072), single),
            jax.ShapeDtypeStruct((6, 2, 3072), single),
            jax.ShapeDtypeStruct((16, 768), single),
            jax.ShapeDtypeStruct((8, 128), single),
        ),
        in_specs=[pl.BlockSpec(memory_space=pltpu.SMEM)] + [anywhere] * 4 + [vmem] * 4,
        out_specs=[anywhere] + [vmem] * 4,
        scratch_shapes=[
            pltpu.VMEM((3, 4, 4, 48, 3072), bfloat),
            pltpu.VMEM((3, 4, 4, 48, 3072), bfloat),
            pltpu.VMEM((384, 768), bfloat),
            pltpu.VMEM((3, 128, 128), single),
            pltpu.VMEM((4, 112, 112), single),
            pltpu.VMEM((24, 768), single),
            pltpu.VMEM((4608, 128), single),
            pltpu.VMEM((400, 768), bfloat),
            pltpu.VMEM((400, 2304), bfloat),
            pltpu.VMEM((400, 768), bfloat),
            pltpu.VMEM((400, 768), single),
            pltpu.VMEM((384, 768), bfloat),
            pltpu.VMEM((384, 3072), bfloat),
            pltpu.VMEM((400, 3072), bfloat),
            pltpu.VMEM((384, 3072), bfloat),
            pltpu.VMEM((384, 768), single),
            pltpu.VMEM((384, 768), single),
            pltpu.VMEM((4, 4, 4, 48, 768), bfloat),
            pltpu.VMEM((2, 24, 768), single),
            pltpu.VMEM((2, 4, SHARD, 128), bfloat),
            pltpu.VMEM((48, 128), single),
            pltpu.VMEM((4, 4, 48, 128), bfloat),
            pltpu.VMEM((16, 768), single),
            pltpu.VMEM((8, 384), single),
            pltpu.VMEM((4, 2, 8, 384), single),
            pltpu.VMEM((4, 4, 8, 384), single),
            pltpu.VMEM((2, 3, 48, 768), bfloat),
            pltpu.VMEM((2, 3, 48, 768), bfloat),
            pltpu.VMEM((3, 4, 48, 384), bfloat),
            pltpu.VMEM((3, 48, 384), bfloat),
            pltpu.VMEM((2, 48, 1536), single),
            pltpu.VMEM((4, 48, 384), bfloat),
            pltpu.VMEM((2, 576, 128), single),
            pltpu.VMEM((144, 128), single),
            pltpu.VMEM((176, 128), single),
            pltpu.VMEM((4, 2, 176, 128), bfloat),
            pltpu.VMEM((4, 2, 176, 128), bfloat),
            pltpu.VMEM((24, 128), single),
            pltpu.VMEM((2, 16, 768), single),
            pltpu.VMEM((4, 16, 768), single),
            pltpu.VMEM((4, 16, 768), single),
            pltpu.VMEM((4, 16, 768), single),
            pltpu.VMEM((8, 128), single),
            pltpu.VMEM((4, 2, 8, 128), single),
            pltpu.VMEM((4, 4, 8, 128), single),
            pltpu.SemaphoreType.DMA((7,)),
            pltpu.SemaphoreType.DMA((copies,)),
            pltpu.SemaphoreType.DMA((copies,)),
        ],
        compiler_params=pltpu.CompilerParams(
            collective_id=1, has_side_effects=True, vmem_limit_bytes=63 * 2**20
        ),
        name="train_step",
    )(
        lengths,
        text,
        images,
        image_attn.reshape(4, 4, 48, 3072),
        image_mlp.reshape(2, 4, 4, 48, 3072),
        image_vectors,
        attn_master,
        mlp_master,
        vector_master,
    )


def close_kernel(*refs):
    given, out = (refs[:14], refs[14:])
    attn_sum, mlp_sum, vector_all, square, input_grad = given[:5]
    states = given[5:]
    out[0][...] = input_grad[...]
    grad_norm = jnp.sqrt(square[0:1, 0:1])
    out[1][...] = grad_norm
    factor = jnp.minimum(1.0, clip_norm / (grad_norm + 1e-06))
    start = lax.axis_index("dp") * 6
    vector_sum = pltpu.roll(vector_all[...], lax.rem(768 - start, 768), 1)[:, :128].T[:6, :12]
    sums = (attn_sum[...], mlp_sum[...], vector_sum)
    rates = ((learn_rate, weight_decay), (learn_rate, weight_decay), (vector_rate, 0.0))
    for n in range(3):
        out[2 + n][...] = sums[n]
        clip = factor.reshape(1, 1, 1) if n == 1 else factor
        new = adam_update(
            states[n][...], sums[n], states[3 + n][...], states[6 + n][...], clip, *rates[n]
        )
        for k in range(3):
            out[5 + 3 * k + n][...] = new[k]


def close(*given):
    vmem = pl.BlockSpec(memory_space=pltpu.VMEM)
    kinds = [(6, 3072), (6, 2, 3072), (6, 12)]
    shapes = [(384, 768), (1, 1)] + kinds * 4
    return pl.pallas_call(
        close_kernel,
        out_shape=[jax.ShapeDtypeStruct(shape, single) for shape in shapes],
        in_specs=[vmem] * 14,
        out_specs=[vmem] * 14,
        compiler_params=pltpu.CompilerParams(vmem_limit_bytes=63 * 2**20),
        name="close_step",
    )(*given)


def shards(
    text_input,
    caption_lengths,
    image_tokens,
    image_attn,
    image_mlp,
    image_vectors,
    attn_master,
    mlp_master,
    vector_master,
    attn_first,
    mlp_first,
    vector_first,
    attn_second,
    mlp_second,
    vector_second,
):
    mlp_master, mlp_first, mlp_second = (
        jnp.swapaxes(values, 0, 1) for values in (mlp_master, mlp_first, mlp_second)
    )
    vector_master, vector_first, vector_second = (
        values.T for values in (vector_master, vector_first, vector_second)
    )
    input_grad, attn_sum, mlp_sum, vector_all, square_total = train_step(
        caption_lengths.T,
        text_input,
        image_tokens,
        image_attn,
        image_mlp,
        image_vectors,
        attn_master,
        mlp_master,
        vector_master,
    )
    out = close(
        attn_sum,
        mlp_sum,
        vector_all,
        square_total,
        input_grad,
        attn_master,
        mlp_master,
        vector_master,
        attn_first,
        mlp_first,
        vector_first,
        attn_second,
        mlp_second,
        vector_second,
    )
    turned = [jnp.swapaxes(value, 0, 1) if n % 3 else value for n, value in enumerate(out[2:])]
    return (out[0], out[1].reshape(()), *turned)


def solution(mesh):
    in_specs = (
        P("dp", None),
        P("dp", None),
        P("dp", None),
        P(),
        P(),
        P(),
        P("dp", None),
        P(None, "dp", None),
        P(None, "dp"),
        P("dp", None),
        P(None, "dp", None),
        P(None, "dp"),
        P("dp", None),
        P(None, "dp", None),
        P(None, "dp"),
    )
    out_specs = (
        P("dp", None),
        P(),
        P("dp", None),
        P(None, "dp", None),
        P(None, "dp"),
        P("dp", None),
        P(None, "dp", None),
        P(None, "dp"),
        P("dp", None),
        P(None, "dp", None),
        P(None, "dp"),
        P("dp", None),
        P(None, "dp", None),
        P(None, "dp"),
    )
    return jax.shard_map(shards, mesh=mesh, in_specs=in_specs, out_specs=out_specs, check_vma=False)
```
